256 devices in a mesh: gx: 8 (over x, core), gy: 32 (over y, z).
Axes of the slice: x: 4, y: 4, z: 8, core: 2. Of those that a mesh axis runs over, the one named last changes fastest.
Arguments:
- u_electric: float32 [3, 128, 512, 128], P(None, 'gx', 'gy'), may hold values from -18 to 18
- u_magnetic: float32 [3, 128, 512, 128], P(None, 'gx', 'gy'), may hold values from -18 to 18
- eps_inv: float32 [128, 512, 128], P('gx', 'gy'), may hold values from 0.25 to 1
- metal_map: int32 [16, 64], replicated, may hold values from 0 to 1, as said below
- pole_omega: float32 [6], replicated, may hold values from 0.5 to 2
- pole_gamma: float32 [6], replicated, may hold values from 0.05 to 0.8
- pole_strength: float32 [6], replicated, may hold values from 0.3 to 1.5
Outputs:
- out_electric: float32 [3, 128, 512, 128], P(None, 'gx', 'gy')
- out_magnetic: float32 [3, 128, 512, 128], P(None, 'gx', 'gy')
- out_poles: float32 [512, 2, 6, 3, 8, 8, 128], P(('gx', 'gy'))
- coefficients: float32 [4, 3], replicated
The draws below stay inside these ranges and needn't reach their ends.
Inputs may be any that keep to these rules, and one draw needn't show every extreme that they name: `metal_map`: each block of 2 x 2 tiles (rows 2a, 2a+1 and columns 2b, 2b+1) holds at most 2 metal tiles, and some block holds exactly 2.
All inputs are finite; a program needn't handle non-finite values.
Results may differ from the reference program's by a relative error of at most 0.0001.
Values sent between devices are 32-bit elements; how exact they have to be, the bound alone decides.
A program may use at most 192 MiB of HBM per device.

```python
import math
import jax
import jax.numpy as jnp
from jax import lax

POLES = 6
STEPS = 4
MS = 2
NX = 128
NY = 512
NZ = 128
TX = 8
TY = 8
TGX = 16
TGY = 64
SLOTS = 512


def draw_u_electric(key, part):
    key = jax.random.fold_in(key, 5)
    full_shape = (3, NX, NY, NZ)
    ramp_x = jnp.arange(NX, dtype=jnp.float32) / max(NX - 1, 1)
    random_part = jnp.clip(jax.random.normal(key, full_shape, jnp.float32), -6.0, 6.0)
    factor = (1.0 + 2.0 * ramp_x)[:, None, None] * jnp.ones((1, NY, 1), jnp.float32)
    return random_part * factor[None]


def draw_u_magnetic(key, part):
    key = jax.random.fold_in(key, 7)
    full_shape = (3, NX, NY, NZ)
    ramp_x = jnp.arange(NX, dtype=jnp.float32) / max(NX - 1, 1)
    random_part = jnp.clip(jax.random.normal(key, full_shape, jnp.float32), -6.0, 6.0)
    factor = (1.0 + 2.0 * ramp_x)[:, None, None] * jnp.ones((1, NY, 1), jnp.float32)
    return random_part * factor[None]


def draw_metal_map(key, part):
    key = jax.random.fold_in(key, 11)
    key_kinds, key_force, key_order = jax.random.split(key, 3)
    blocks_x = TGX // 2
    pairs_y = TGY // 4
    pair_total = blocks_x * pairs_y
    pair_kinds = jax.random.randint(key_kinds, (pair_total,), 0, 5)
    forced = jax.random.randint(key_force, (), 0, pair_total)
    pair_kinds = jnp.where(jnp.arange(pair_total) == forced, 0, pair_kinds)
    first_count = jnp.array([MS, 0, 1, 1, 0], jnp.int32)[pair_kinds]
    second = jnp.array([0, MS, 1, 0, 0], jnp.int32)[pair_kinds]
    counts = jnp.stack([first_count, second], axis=-1).reshape(blocks_x, 2 * pairs_y)
    scores = jax.random.randint(key_order, (blocks_x, 2 * pairs_y, 4), 0, 1 << 20) * 4 + jnp.arange(4, dtype=jnp.int32)
    tile_ranks = jnp.argsort(jnp.argsort(scores, axis=-1), axis=-1)
    metal_flags = (tile_ranks < counts[:, :, None]).astype(jnp.int32)
    return metal_flags.reshape(blocks_x, 2 * pairs_y, 2, 2).transpose(0, 2, 1, 3).reshape(TGX, TGY)


def level_of(key, shape, pieces, smallest, largest):
    def one(axis_at, parts):
        draws = jax.random.uniform(jax.random.fold_in(jax.random.fold_in(key, 6), axis_at), (parts,), jnp.float32, smallest / len(pieces), largest / len(pieces))
        return jnp.repeat(jnp.exp(draws), shape[axis_at] // parts).reshape((-1,) + (1,) * (len(shape) - axis_at - 1))

    level = one(*pieces[0])
    for cut in pieces[1:]:
        level = level * one(*cut)
    return level


def setup_inputs(seed: int = 0) -> dict:
    arg_keys = jax.random.split(jax.random.key(seed), 8)
    return {
        "u_electric": draw_u_electric(jax.random.fold_in(arg_keys[7], 71), 0),
        "u_magnetic": draw_u_magnetic(jax.random.fold_in(arg_keys[7], 71), 0),
        "eps_inv": jnp.clip(jnp.exp(math.log(1.0) - 1.3862944 * jax.random.uniform(arg_keys[2], (NX, NY, NZ), jnp.float32) ** level_of(arg_keys[2], (NX, NY, NZ), ((0, 8), (1, 32)), -0.2, 0.2)), 0.25, 1.0),
        "metal_map": draw_metal_map(jax.random.fold_in(arg_keys[7], 71), 0),
        "pole_omega": jnp.clip(jnp.exp(jax.random.uniform(arg_keys[4], (POLES,), jnp.float32, math.log(0.5), math.log(2.0))), 0.5, 2.0),
        "pole_gamma": jnp.clip(jnp.exp(jax.random.uniform(arg_keys[5], (POLES,), jnp.float32, math.log(0.05), math.log(0.8))), 0.05, 0.8),
        "pole_strength": jnp.clip(jnp.exp(jax.random.uniform(arg_keys[6], (POLES,), jnp.float32, math.log(0.3), math.log(1.5))), 0.3, 1.5),
    }


EPSILON = 1e-06

def forward_diff(values, direction):
    return jnp.roll(values, -1, direction) - values

def backward_diff(values, direction):
    return values - jnp.roll(values, 1, direction)

def curls(electric, magnetic):
    curl_e = jnp.stack([forward_diff(electric[2], 1) - forward_diff(electric[1], 2), forward_diff(electric[0], 2) - forward_diff(electric[2], 0), forward_diff(electric[1], 0) - forward_diff(electric[0], 1)])
    curl_h = jnp.stack([backward_diff(magnetic[2], 1) - backward_diff(magnetic[1], 2), backward_diff(magnetic[0], 2) - backward_diff(magnetic[2], 0), backward_diff(magnetic[1], 0) - backward_diff(magnetic[0], 1)])
    return (curl_e, curl_h)

def to_tiles(field):
    return field.reshape(3, TGX, TX, TGY, TY, NZ).transpose(1, 3, 0, 2, 4, 5)

def from_tiles(tiled):
    return tiled.transpose(2, 0, 3, 1, 4, 5).reshape(3, NX, NY, NZ)

def pole_update(pole_state, field_tiles, pole_omega, pole_gamma, pole_strength):
    polarization = pole_state[:, 0]
    current = pole_state[:, 1]
    summed = lax.optimization_barrier(jnp.sum(current, axis=1))
    spring_rate = (pole_omega * pole_omega)[None, :, None, None, None, None]
    damping = pole_gamma[None, :, None, None, None, None]
    coupling = pole_strength[None, :, None, None, None, None]
    renewed = -spring_rate * polarization - damping * current + coupling * field_tiles[:, None]
    return (summed, jnp.stack([current, renewed], axis=1))

def field_dot(first_e, first_h, second_e, second_h, cell_count):
    return (jnp.sum(first_e * second_e) + jnp.sum(first_h * second_h)) / cell_count

def reference(u_electric, u_magnetic, eps_inv, metal_map, pole_omega, pole_gamma, pole_strength):
    cell_count = 6.0 * NX * NY * NZ
    blocks_x = TGX // 2
    blocks_y = TGY // 2
    metal_flags = metal_map.reshape(blocks_x, 2, blocks_y, 2).transpose(0, 2, 1, 3).reshape(blocks_x, blocks_y, 4)
    before = (jnp.cumsum(metal_flags, axis=-1) - metal_flags).astype(jnp.int32)
    tile_order = jnp.arange(4, dtype=jnp.int32)
    picked = jnp.stack([jnp.logical_and(metal_flags == 1, before == slot_id).astype(jnp.int32) for slot_id in range(MS)], axis=2)
    tile_number = lax.optimization_barrier(jnp.sum(picked * tile_order, axis=-1)).astype(jnp.int32)
    valid_mask = lax.optimization_barrier(jnp.sum(picked, axis=-1)).astype(jnp.int32)
    block_rows = jnp.arange(blocks_x, dtype=jnp.int32)[:, None, None]
    block_cols = jnp.arange(blocks_y, dtype=jnp.int32)[None, :, None]
    tile_x = (2 * block_rows + tile_number // 2).reshape(-1).astype(jnp.int32)
    tile_y = (2 * block_cols + tile_number % 2).reshape(-1).astype(jnp.int32)
    slot_weight = valid_mask.reshape(-1).astype(jnp.float32)[:, None, None, None, None]

    def apply(electric, magnetic, pole_state):
        curl_e, curl_h = curls(electric, magnetic)
        field_tiles = to_tiles(electric)[tile_x, tile_y] * slot_weight
        summed, renewed = pole_update(pole_state, field_tiles, pole_omega, pole_gamma, pole_strength)
        empty_tiles = jnp.zeros((TGX, TGY, 3, TX, TY, NZ), jnp.float32)
        pole_term = from_tiles(empty_tiles.at[tile_x, tile_y].add(summed))
        return (eps_inv[None] * (curl_h - pole_term), -curl_e, renewed)
    scale_u = field_dot(u_electric, u_magnetic, u_electric, u_magnetic, cell_count)
    root_value = jnp.sqrt(scale_u + EPSILON)
    q_e = u_electric / root_value
    q_h = u_magnetic / root_value
    v_e, v_h = (q_e, q_h)
    v_poles = jnp.zeros((SLOTS, 2, POLES, 3, TX, TY, NZ), jnp.float32)
    coeff_rows = []
    for step_id in range(STEPS):
        w_e, w_h, w_poles = apply(v_e, v_h, v_poles)
        along_q = field_dot(q_e, q_h, w_e, w_h, cell_count)
        if step_id == 0:
            along_v = jnp.zeros((), jnp.float32)
        else:
            along_v = field_dot(v_e, v_h, w_e, w_h, cell_count)
        z_e = w_e - along_q * q_e - along_v * v_e
        z_h = w_h - along_q * q_h - along_v * v_h
        z_poles = w_poles - along_v * v_poles
        norm_value = jnp.sqrt(field_dot(z_e, z_h, z_e, z_h, cell_count) + EPSILON)
        v_e = z_e / norm_value
        v_h = z_h / norm_value
        v_poles = z_poles / norm_value
        coeff_rows.append(jnp.stack([along_q, along_v, norm_value]))
    return (v_e, v_h, v_poles, jnp.stack(coeff_rows))
```

```python
import functools

import jax
import jax.numpy as jnp
from jax import lax
from jax.experimental import pallas as pl
from jax.experimental.pallas import tpu as pltpu
from jax.sharding import PartitionSpec as P

POLES = 6
STEPS = 4
MS = 2
EPSILON = 1e-06
MESH = pl.DeviceIdType.MESH

EDGE = 2
OWN = 16
PADX = OWN + 2 * EDGE
PADY = 24
HIGH = 16
LOW = 22
FIELDS = 7
TO_PREVIOUS = [(f, 0) for f in range(FIELDS)] + [(f, 1) for f in (0, 2, 3, 4, 5, 6)]
TO_NEXT = [(f, 1) for f in range(FIELDS)] + [(f, 0) for f in (0, 1, 2, 3, 5)]
ROW = PADX * PADY
CORNER_ROWS = 32
PAIRS = [(i, j) for i in range(STEPS + 1) for j in range(i, STEPS + 1)]
VMEM_LIMIT = 40 * 1024 * 1024


def layout(gx_size, gy_size):
    cores = 2
    z_size = min(8, gy_size // 2)
    return gx_size // cores, cores, gy_size // z_size, z_size


def rings(sizes):
    result = []
    for axis, size in (("x", sizes[0]), ("y", sizes[2]), ("z", sizes[3])):
        near = sorted({1 % size, size - 1} - {0})
        far = sorted({2 % size, (size - 2) % size} - {0}) if size > 3 else []
        result.append((axis, size, near, far))
    return result


def farthest_first(first, second):
    def hops(step, size):
        return min(step, size - step)

    steps = [(a, b) for a in range(first) for b in range(second) if a or b]
    return sorted(steps, key=lambda step: -hops(step[0], first) - hops(step[1], second))


def next_y(value):
    return pltpu.roll(value, PADY - 1, 0)


def prev_y(value):
    return pltpu.roll(value, 1, 0)


def next_z(value):
    return pltpu.roll(value, value.shape[1] - 1, 1)


def prev_z(value):
    return pltpu.roll(value, 1, 1)


def settle(buffer, semaphore):
    pltpu.make_async_copy(buffer, buffer, semaphore).wait()


def exchange_kernel(
    sizes,
    tiles,
    u_e,
    u_h,
    eps_in,
    metal_in,
    omega_in,
    gamma_in,
    strength_in,
    k1,
    k2,
    k3,
    k4,
    gram_out,
    tiles_out,
    kicks_out,
    raw,
    face_in,
    u,
    previous_out,
    previous_in,
    next_out,
    next_in,
    corner_out,
    corner_in,
    mask,
    acc_rows,
    sum_a,
    sum_b,
    metal,
    omega,
    gamma,
    strength,
    heard,
    load_sem,
    face_send,
    face_recv,
    stage_send,
    stage_recv,
):
    x_size, cores, y_size, z_size = sizes
    gx_size, gy_size = x_size * cores, y_size * z_size
    gx = lax.axis_index("gx")
    gy = lax.axis_index("gy")

    loads = [
        pltpu.make_async_copy(u_e, raw.at[pl.ds(0, 3)], load_sem.at[0]),
        pltpu.make_async_copy(u_h, raw.at[pl.ds(3, 3)], load_sem.at[1]),
        pltpu.make_async_copy(eps_in, raw.at[6], load_sem.at[2]),
        pltpu.make_async_copy(metal_in, metal, load_sem.at[3]),
        pltpu.make_async_copy(omega_in, omega, load_sem.at[4]),
        pltpu.make_async_copy(gamma_in, gamma, load_sem.at[5]),
        pltpu.make_async_copy(strength_in, strength, load_sem.at[6]),
    ]
    for load in loads:
        load.start()

    def ring(position, size):
        return [position] + [lax.rem(position + step, size) for step in range(1, size)]

    def device(x, core, y, z):
        return (x * cores + core, y * z_size + z)

    around_x = {0: gx, -1: lax.rem(gx + gx_size - 1, gx_size), 1: lax.rem(gx + 1, gx_size)}
    around_y = {0: gy, -1: lax.rem(gy + gy_size - 1, gy_size), 1: lax.rem(gy + 1, gy_size)}

    def neighbour(dx, dy):
        return (around_x[dx], around_y[dy])

    my_x, my_core = lax.div(gx, cores), lax.rem(gx, cores)
    my_y, my_z = lax.div(gy, z_size), lax.rem(gy, z_size)
    ring_x, ring_core = ring(my_x, x_size), ring(my_core, cores)
    ring_y, ring_z = ring(my_y, y_size), ring(my_z, z_size)

    def along(axis, step, core=0):
        return device(
            ring_x[step if axis == "x" else 0],
            ring_core[core],
            ring_y[step if axis == "y" else 0],
            ring_z[step if axis == "z" else 0],
        )

    def signal(semaphore, target):
        pl.semaphore_signal(semaphore, inc=1, device_id=target, device_id_type=MESH)

    beside = [(0, -1), (0, 1), (-1, 0), (1, 0)]
    near = [(axis, step, 0) for axis, _, steps, _ in rings(sizes) for step in steps]
    near += [(axis, step, 1) for axis, step, _ in near if axis == "z"]
    far = [(axis, step) for axis, _, _, steps in rings(sizes) for step in steps]
    barrier = pltpu.get_barrier_semaphore()
    for dx, dy in beside:
        signal(barrier, neighbour(dx, dy))
    for place in near:
        signal(barrier, along(*place))

    for load in loads:
        load.wait()

    for number, (f, layer) in enumerate(TO_PREVIOUS):
        previous_out[number] = raw[f, pl.ds(layer, OWN, stride=OWN), :]
    for number, (f, layer) in enumerate(TO_NEXT):
        next_out[number] = raw[f, pl.ds(OWN - 2 + layer, OWN, stride=OWN), :]
    corners = [(0, 0), (0, 1), (1, 0), (1, 1)]
    for number, (side_x, side_y) in enumerate(corners):
        for f in range(FIELDS):
            for layer in range(2):
                if side_x != side_y:
                    x = (0 if side_x == 0 else OWN - 2) + layer
                    y = 0 if side_y == 0 else OWN - 2
                    cells = raw[f, pl.ds(x * OWN + y, 2), :]
                    corner_out[number, pl.ds(f * 4 + layer * 2, 2), :] = cells
                elif layer == 0:
                    cell = 0 if side_x == 0 else OWN * OWN - 1
                    corner_out[number, pl.ds(f, 1), :] = raw[f, pl.ds(cell, 1), :]

    pl.semaphore_wait(barrier, len(beside) + len(near))

    copies = []

    def send(src, dst, device):
        number = len(copies)
        copy = pltpu.make_async_remote_copy(
            src_ref=src,
            dst_ref=dst,
            send_sem=face_send.at[number],
            recv_sem=face_recv.at[number],
            device_id=device,
            device_id_type=MESH,
        )
        copy.start()
        copies.append(copy)

    send(previous_out, previous_in, neighbour(0, -1))
    send(next_out, next_in, neighbour(0, 1))
    everything = pl.ds(0, FIELDS)
    layers = EDGE * OWN
    send(raw.at[everything, pl.ds(0, layers)], face_in.at[0], neighbour(-1, 0))
    send(raw.at[everything, pl.ds(OWN * OWN - layers, layers)], face_in.at[1], neighbour(1, 0))
    for dx, dy in beside[2:]:
        signal(heard.at[0], neighbour(dx, dy))
    for place in near:
        signal(heard.at[0], along(*place))

    tile_rows = [lax.rem(2 * gx + s - 1 + tiles[0], tiles[0]) for s in range(4)]
    tile_cols = [lax.rem(2 * gy + t - 1 + tiles[1], tiles[1]) for t in range(4)]
    upper = lax.broadcasted_iota(jnp.int32, (8, 128), 0) < 4
    for s in range(4):
        flag = [
            jnp.full((8, 128), metal[tile_rows[s], tile_cols[t]].astype(jnp.float32)) for t in range(4)
        ]
        mask[s, 0:8] = flag[1]
        mask[s, 8:16] = flag[2]
        mask[s, 16:24] = jnp.where(upper, flag[3], flag[0])

    response = [jnp.float32(0.0)] * 3
    for p in range(POLES):
        g0 = strength[p]
        g1 = -gamma[p] * g0
        g2 = -(omega[p] * omega[p]) * g0 - gamma[p] * g1
        response = [response[0] + g0, response[1] + g1, response[2] + g2]

    def copy_own(x, carry):
        for f in range(FIELDS):
            source = raw[f, pl.ds(pl.multiple_of(x * OWN, 8), OWN), :]
            u[f, pl.ds(pl.multiple_of((x + EDGE) * PADY, 8), OWN), :] = source
        return carry

    lax.fori_loop(0, OWN, copy_own, 0)

    pl.semaphore_wait(heard.at[0], len(beside[2:]) + len(near))
    for axis, step in far:
        signal(heard.at[1], along(axis, step))
    for number, (side_x, side_y) in enumerate(corners):
        rows = pl.ds(0, 8 if side_x == side_y else CORNER_ROWS)
        send(
            corner_out.at[number, rows],
            corner_in.at[number, rows],
            neighbour(2 * side_x - 1, 2 * side_y - 1),
        )

    class Padded:
        def __getitem__(self, at):
            f, x = at
            return u[f, pl.ds(pl.multiple_of(x * PADY, 8), PADY), :]

    start = Padded()
    states = [start, k1, k2, k3, k4]

    def electric(step, x):
        old = states[step - 1]
        hx, hy, hz = old[3, x], old[4, x], old[5, x]
        hy_back, hz_back = old[4, x - 1], old[5, x - 1]
        curl = [
            (hz - prev_y(hz)) - (hy - prev_z(hy)),
            (hx - prev_z(hx)) - (hz - hz_back),
            (hy - hy_back) - (hx - prev_y(hx)),
        ]
        eps = start[6, x]
        if step > 1:
            metal_here = mask[(x + 6) // 8]
            for c in range(3):
                current = response[step - 2] * start[c, x]
                for j in range(1, step - 1):
                    current = current + response[step - 2 - j] * states[j][c, x]
                curl[c] = curl[c] - metal_here * current
        return [eps * part for part in curl]

    def magnetic(step, x):
        old = states[step - 1]
        ex, ey, ez = old[0, x], old[1, x], old[2, x]
        ey_next, ez_next = old[1, x + 1], old[2, x + 1]
        return [
            (next_z(ey) - ey) - (next_y(ez) - ez),
            (ez_next - ez) - (next_z(ex) - ex),
            (next_y(ex) - ex) - (ey_next - ey),
        ]

    def write_rows(step, starts, shift):
        new = states[step]
        parts = [(x, electric(step, x), magnetic(step, x - shift)) for x in starts]
        for x, of_e, of_h in parts:
            for c in range(3):
                new[c, x] = of_e[c]
                new[3 + c, x - shift] = of_h[c]

    def interior(step, low, high, shift):
        def rows(x, carry):
            write_rows(step, [x], shift)
            return carry

        lax.fori_loop(low, high, rows, 0)

    def edges(step, low, high, shift):
        def rows(x, carry):
            write_rows(step, [low + x, high + x], shift)
            return carry

        lax.fori_loop(0, EDGE, rows, 0)

    def products(x, sums):
        sums = list(sums)
        for c in range(6):
            for t in range(2):
                cells = pl.ds(8 * t, 8)
                first = u[c, pl.ds(pl.multiple_of(x * PADY + 8 * t, 8), 8), :]
                values = [first] + [state[c, x, cells, :] for state in states[1:]]
                for number, (i, j) in enumerate(PAIRS):
                    sums[number] = sums[number] + values[i] * values[j]
        return tuple(sums)

    zero = jnp.zeros((8, 128), jnp.float32)

    for copy in copies[:2]:
        copy.wait_recv()
    for number, (f, layer) in enumerate(TO_PREVIOUS):
        u[f, pl.ds(EDGE * PADY + HIGH + layer, OWN, stride=PADY), :] = previous_in[number]
    for number, (f, layer) in enumerate(TO_NEXT):
        u[f, pl.ds(EDGE * PADY + LOW + layer, OWN, stride=PADY), :] = next_in[number]
    interior(1, EDGE + 1, EDGE + OWN, 1)
    interior(2, EDGE + 1, EDGE + OWN - 1, 0)
    interior(3, EDGE + 2, EDGE + OWN - 1, 1)
    interior(4, EDGE + 2, EDGE + OWN - 2, 0)
    sums = lax.fori_loop(EDGE + 2, EDGE + OWN - 2, products, (zero,) * len(PAIRS))

    for copy in copies[2:]:
        copy.wait_recv()
    for f in range(FIELDS):
        for side, first in ((0, EDGE + OWN), (1, 0)):
            for layer in range(2):
                source = face_in[side, f, pl.ds(layer * OWN, OWN), :]
                u[f, pl.ds((first + layer) * PADY, OWN), :] = source
    for number, (side_x, side_y) in enumerate(corners):
        for f in range(FIELDS):
            for layer in range(2):
                x = (EDGE + OWN if side_x == 0 else 0) + layer
                y = HIGH if side_y == 0 else LOW
                if side_x != side_y:
                    source = corner_in[number, pl.ds(f * 4 + layer * 2, 2), :]
                    u[f, pl.ds(x * PADY + y, 2), :] = source
                elif layer == side_x:
                    u[f, pl.ds(x * PADY + y + layer, 1), :] = corner_in[number, pl.ds(f, 1), :]
    edges(1, 1, EDGE + OWN, 1)
    edges(2, 1, EDGE + OWN - 1, 0)
    edges(3, EDGE, EDGE + OWN - 1, 1)
    edges(4, EDGE, EDGE + OWN - 2, 0)
    sums = lax.fori_loop(0, EDGE, lambda i, sums: products(EDGE + i, sums), sums)
    sums = lax.fori_loop(0, EDGE, lambda i, sums: products(OWN + i, sums), sums)
    for number, part in enumerate(sums):
        acc_rows[pl.ds(8 * number, 8), :] = part
    acc_rows[pl.ds(8 * len(PAIRS), 8), :] = zero
    total = acc_rows[pl.ds(0, 16, stride=8), :]
    for s in range(1, 8):
        total = total + acc_rows[pl.ds(s, 16, stride=8), :]
    diagonal = lax.broadcasted_iota(jnp.int32, (16, 128), 0) == lax.broadcasted_iota(jnp.int32, (16, 128), 1)

    def to_row(column):
        return jnp.sum(jnp.where(diagonal, column, 0.0), axis=0, keepdims=True)

    def gather_metal():
        flags = [metal[tile_rows[1 + t // 2], tile_cols[1 + t % 2]] for t in range(4)]
        present = [flag.astype(jnp.float32) for flag in flags]
        before = jnp.float32(0.0)
        chosen = [[None] * 4 for _ in range(MS)]
        for t in range(4):
            taken = [present[t] * (1.0 - before), present[t] * before]
            before = before + present[t]
            for slot in range(MS):
                chosen[slot][t] = taken[slot]

        def rows(x, carry):
            for c in range(3):
                for j, state in enumerate(states[:STEPS]):
                    parts = []
                    for t in range(4):
                        at = EDGE + 8 * (t // 2) + x
                        y = 8 * (t % 2)
                        if j == 0:
                            start_row = pl.multiple_of(at * PADY + y, 8)
                            parts.append(u[c, pl.ds(start_row, 8), :])
                        else:
                            parts.append(state[c, at, pl.ds(y, 8), :])
                    for slot in range(MS):
                        value = chosen[slot][0] * parts[0]
                        for t in range(1, 4):
                            value = value + chosen[slot][t] * parts[t]
                        tiles_out[slot, j, c, x] = value
            return carry

        lax.fori_loop(0, 8, rows, 0)
        for p in range(POLES):
            kicks = [strength[p]]
            kicks.append(-gamma[p] * kicks[0])
            for k in range(2, STEPS):
                kicks.append(-(omega[p] * omega[p]) * kicks[k - 2] - gamma[p] * kicks[k - 1])
            for k in range(STEPS):
                kicks_out[pl.ds(p * STEPS + k, 1), :] = jnp.full((1, 128), kicks[k])

    row = to_row(jnp.sum(total, axis=1, keepdims=True))
    if far:
        pl.semaphore_wait(heard.at[1], len(far))
    me_a = my_core * z_size + my_z
    me_b = my_x * y_size + my_y
    targets_a = [
        device(my_x, ring_core[c], my_y, ring_z[z]) for c, z in farthest_first(cores, z_size)
    ]
    targets_b = [
        device(ring_x[x], my_core, ring_y[y], my_z) for x, y in farthest_first(x_size, y_size)
    ]
    for stage, (slots, me, targets) in enumerate(((sum_a, me_a, targets_a), (sum_b, me_b, targets_b))):
        slots[me] = row
        for target in targets:
            pltpu.make_async_remote_copy(
                src_ref=slots.at[me],
                dst_ref=slots.at[me],
                send_sem=stage_send.at[stage],
                recv_sem=stage_recv.at[stage],
                device_id=target,
                device_id_type=MESH,
            ).start()
        if stage == 0:
            gather_metal()
        settle(slots.at[pl.ds(0, len(targets))], stage_recv.at[stage])
        row = slots[0]
        for member in range(1, len(targets) + 1):
            row = row + slots[member]
    gram_out[...] = jnp.broadcast_to(
        jnp.sum(jnp.where(diagonal, row, 0.0), axis=1, keepdims=True), (16, 128)
    )

    for copy in copies:
        copy.wait_send()
    for stage, (slots, targets) in enumerate(((sum_a, targets_a), (sum_b, targets_b))):
        settle(slots.at[pl.ds(0, len(targets))], stage_send.at[stage])


def finish_kernel(
    cell_count,
    k0,
    k1,
    k2,
    k3,
    k4,
    gram,
    tiles,
    kicks,
    out_e,
    out_h,
    out_poles,
    out_coefficients,
    coefficients,
    table,
    fields,
    poles,
    store_sem,
):
    stores = []

    def store(src, dst):
        copy = pltpu.make_async_copy(src, dst, store_sem.at[len(stores)])
        copy.start()
        stores.append(copy)

    inner = {}
    for number, (i, j) in enumerate(PAIRS):
        inner[i, j] = inner[j, i] = gram[pl.ds(number, 1), :] * (1.0 / cell_count)
    unit = 1.0 / jnp.sqrt(inner[0, 0] + EPSILON)
    weights = [unit]
    lane = lax.broadcasted_iota(jnp.int32, (1, 128), 1)
    for step in range(1, STEPS + 1):
        image = [None] + weights

        def total(terms):
            return functools.reduce(jnp.add, terms)

        along_q = unit * total([image[j] * inner[0, j] for j in range(1, step + 1)])
        rest = [-along_q * unit] + image[1:]
        along_v = jnp.zeros_like(unit)
        if step > 1:
            along_v = total(
                [
                    image[j] * total([weights[i] * inner[i, j] for i in range(step)])
                    for j in range(1, step + 1)
                ]
            )
            for i in range(step):
                rest[i] = rest[i] - along_v * weights[i]
        squared = total(
            [rest[i] * total([rest[j] * inner[i, j] for j in range(step + 1)]) for i in range(step + 1)]
        )
        norm = jnp.sqrt(jnp.maximum(squared, 0.0) + EPSILON)
        scale = 1.0 / norm
        weights = [part * scale for part in rest]
        line = jnp.where(lane == 0, along_q, jnp.where(lane == 1, along_v, norm))
        coefficients[pl.ds(step - 1, 1), :] = line[:, :3]

    store(coefficients, out_coefficients)

    for p in range(POLES):
        kick = [kicks[pl.ds(p * STEPS + k, 1), :] for k in range(STEPS)]
        for j in range(STEPS):
            parts = [weights[k] * kick[k - 1 - j] for k in range(j + 1, STEPS + 1)]
            table[pl.ds(p * 8 + j, 1), :] = functools.reduce(jnp.add, parts)
        for j in range(STEPS - 1):
            parts = [weights[k] * kick[k - 2 - j] for k in range(j + 2, STEPS + 1)]
            table[pl.ds(p * 8 + 4 + j, 1), :] = functools.reduce(jnp.add, parts)
    for j in range(STEPS + 1):
        table[pl.ds(48 + j, 1), :] = weights[j]

    def entry(number):
        return jnp.broadcast_to(table[pl.ds(number, 1), :], (8, 128))

    for slot in range(MS):
        for c in range(3):

            def pole_cells(x, carry):
                field = [tiles[slot, j, c, x] for j in range(STEPS)]
                for p in range(POLES):
                    poles[slot, 1, p, c, x] = functools.reduce(
                        jnp.add, [entry(p * 8 + j) * field[j] for j in range(STEPS)]
                    )
                    poles[slot, 0, p, c, x] = functools.reduce(
                        jnp.add, [entry(p * 8 + 4 + j) * field[j] for j in range(STEPS - 1)]
                    )
                return carry

            lax.fori_loop(0, 8, pole_cells, 0)
            part = (slot, pl.ds(0, 2), pl.ds(0, POLES), c)
            store(poles.at[part], out_poles.at[part])

    for half, out in enumerate((out_e, out_h)):

        def field_cells(x, carry):
            for c in range(3 * half, 3 * half + 3):
                own = pl.ds(pl.multiple_of(x * OWN, 8), OWN)
                value = table[pl.ds(48, 1), :] * k0[c, own, :]
                for j, state in enumerate((k1, k2, k3, k4)):
                    value = value + table[pl.ds(49 + j, 1), :] * state[c, EDGE + x, pl.ds(0, OWN), :]
                fields[c, x] = value
            return carry

        lax.fori_loop(0, OWN, field_cells, 0)
        store(fields.at[pl.ds(3 * half, 3)], out)
    for copy in stores:
        copy.wait()


def body(sizes, u_electric, u_magnetic, eps_inv, metal_map, pole_omega, pole_gamma, pole_strength):
    depth = u_electric.shape[3]
    cell_count = 6.0 * OWN * OWN * depth * sizes[0] * sizes[1] * sizes[2] * sizes[3]
    f32 = jnp.float32
    any_spec = pl.BlockSpec(memory_space=pl.ANY)
    hbm = pl.BlockSpec(memory_space=pltpu.HBM)
    vmem = pl.BlockSpec(memory_space=pltpu.VMEM)
    state = jax.ShapeDtypeStruct((6, PADX, PADY, depth), f32)
    a_size = sizes[1] * sizes[3]
    b_size = sizes[0] * sizes[2]

    def stay(value):
        return pltpu.with_memory_space_constraint(value, pltpu.HBM)

    start = [u_electric.reshape(3, OWN * OWN, depth), u_magnetic.reshape(3, OWN * OWN, depth)]
    model = [stay(part) for part in (metal_map, pole_omega, pole_gamma, pole_strength)]
    dma = pltpu.SemaphoreType.DMA
    results = pl.pallas_call(
        functools.partial(exchange_kernel, sizes, metal_map.shape),
        out_shape=[state] * 4
        + [
            jax.ShapeDtypeStruct((16, depth), f32),
            jax.ShapeDtypeStruct((MS, STEPS, 3, 8, 8, depth), f32),
            jax.ShapeDtypeStruct((POLES * STEPS, depth), f32),
            jax.ShapeDtypeStruct((FIELDS, OWN * OWN, depth), f32),
        ],
        in_specs=[hbm] * 7,
        out_specs=[vmem] * 8,
        scratch_shapes=[
            pltpu.VMEM((2, FIELDS, EDGE * OWN, depth), f32),
            pltpu.VMEM((FIELDS, ROW, depth), f32),
            pltpu.VMEM((len(TO_PREVIOUS), OWN, depth), f32),
            pltpu.VMEM((len(TO_PREVIOUS), OWN, depth), f32),
            pltpu.VMEM((len(TO_NEXT), OWN, depth), f32),
            pltpu.VMEM((len(TO_NEXT), OWN, depth), f32),
            pltpu.VMEM((4, CORNER_ROWS, depth), f32),
            pltpu.VMEM((4, CORNER_ROWS, depth), f32),
            pltpu.VMEM((4, PADY, depth), f32),
            pltpu.VMEM((128, depth), f32),
            pltpu.VMEM((a_size, 1, depth), f32),
            pltpu.VMEM((b_size, 1, depth), f32),
            pltpu.SMEM(metal_map.shape, jnp.int32),
            pltpu.SMEM((POLES,), f32),
            pltpu.SMEM((POLES,), f32),
            pltpu.SMEM((POLES,), f32),
            pltpu.SemaphoreType.REGULAR((2,)),
            dma((7,)),
            dma((8,)),
            dma((8,)),
            dma((2,)),
            dma((2,)),
        ],
        compiler_params=pltpu.CompilerParams(
            collective_id=0, has_side_effects=True, vmem_limit_bytes=VMEM_LIMIT
        ),
    )(*[stay(part) for part in start], stay(eps_inv.reshape(OWN * OWN, depth)), *model)

    k1, k2, k3, k4, gram, tiles, kicks, raw = results

    return pl.pallas_call(
        functools.partial(finish_kernel, cell_count),
        out_shape=[
            jax.ShapeDtypeStruct(u_electric.shape, f32),
            jax.ShapeDtypeStruct(u_magnetic.shape, f32),
            jax.ShapeDtypeStruct((MS, 2, POLES, 3, 8, 8, depth), f32),
            jax.ShapeDtypeStruct((STEPS, 3), f32),
        ],
        in_specs=[vmem] * 8,
        out_specs=[any_spec] * 4,
        scratch_shapes=[
            pltpu.VMEM((STEPS, 3), f32),
            pltpu.VMEM((56, depth), f32),
            pltpu.VMEM((6, OWN, OWN, depth), f32),
            pltpu.VMEM((MS, 2, POLES, 3, 8, 8, depth), f32),
            dma((9,)),
        ],
        compiler_params=pltpu.CompilerParams(vmem_limit_bytes=VMEM_LIMIT),
    )(raw, k1, k2, k3, k4, gram, tiles, kicks)


def solution(mesh):
    sizes = layout(mesh.shape["gx"], mesh.shape["gy"])
    placed = (
        P(None, "gx", "gy", None),
        P(None, "gx", "gy", None),
        P("gx", "gy", None),
        P(),
        P(),
        P(),
        P(),
    )
    return jax.shard_map(
        functools.partial(body, sizes),
        mesh=mesh,
        in_specs=placed,
        out_specs=(
            P(None, "gx", "gy", None),
            P(None, "gx", "gy", None),
            P(("gx", "gy"), None, None, None, None, None, None),
            P(),
        ),
        check_vma=False,
    )
```

```python
import functools

import jax
import jax.numpy as jnp
from jax import lax
from jax.experimental import pallas as pl
from jax.experimental.pallas import tpu as pltpu
from jax.sharding import PartitionSpec as P

POLES = 6
STEPS = 4
MS = 2
EPSILON = 1e-06
MESH = pl.DeviceIdType.MESH

EDGE = 2
OWN = 16
PADX = OWN + 2 * EDGE
PADY = 24
HIGH = 18
LOW = 20
STRIP = 16
FIELDS = 7
TO_PREVIOUS = [(f, 0) for f in range(FIELDS)] + [(f, 1) for f in (0, 2, 3, 4, 5, 6)]
TO_NEXT = [(f, 1) for f in range(FIELDS)] + [(f, 0) for f in (0, 1, 2, 3, 5)]
ROW = PADX * PADY
CORNER_ROWS = 32
CHUNK = 5
STRIP_CHUNK = 8
PAIRS = [(i, j) for i in range(STEPS + 1) for j in range(i, STEPS + 1)]
VMEM_LIMIT = 40 * 1024 * 1024


def layout(gx_size, gy_size):
    cores = 2
    z_size = min(8, gy_size // 2)
    return gx_size // cores, cores, gy_size // z_size, z_size


def rings(sizes):
    result = []
    for axis, size in (("x", sizes[0]), ("y", sizes[2]), ("z", sizes[3])):
        near = sorted({1 % size, size - 1} - {0})
        far = sorted({2 % size, (size - 2) % size} - {0}) if size > 3 else []
        result.append((axis, size, near, far))
    return result


def farthest_first(first, second):
    def hops(step, size):
        return min(step, size - step)

    steps = [(a, b) for a in range(first) for b in range(second) if a or b]
    return sorted(steps, key=lambda step: -hops(step[0], first) - hops(step[1], second))


def next_y(value):
    return pltpu.roll(value, PADY - 1, 0)


def prev_y(value):
    return pltpu.roll(value, 1, 0)


def next_z(value):
    return pltpu.roll(value, value.shape[1] - 1, 1)


def prev_z(value):
    return pltpu.roll(value, 1, 1)


def settle(buffer, semaphore):
    pltpu.make_async_copy(buffer, buffer, semaphore).wait()


def exchange_kernel(
    sizes,
    tiles,
    u_e,
    u_h,
    eps_in,
    metal_in,
    omega_in,
    gamma_in,
    strength_in,
    own_out,
    gram_out,
    tiles_out,
    kicks_out,
    raw,
    face_in,
    k1,
    k2,
    k3,
    k4,
    u,
    previous_out,
    previous_in,
    next_out,
    next_in,
    corner_out,
    corner_in,
    mask,
    acc_rows,
    sum_a,
    sum_b,
    metal,
    omega,
    gamma,
    strength,
    heard,
    load_sem,
    face_send,
    face_recv,
    stage_send,
    stage_recv,
):
    x_size, cores, y_size, z_size = sizes
    gx_size, gy_size = x_size * cores, y_size * z_size
    gx = lax.axis_index("gx")
    gy = lax.axis_index("gy")

    loads = [
        pltpu.make_async_copy(u_e, raw.at[pl.ds(0, 3)], load_sem.at[0]),
        pltpu.make_async_copy(u_h, raw.at[pl.ds(3, 3)], load_sem.at[1]),
        pltpu.make_async_copy(eps_in, raw.at[6], load_sem.at[2]),
        pltpu.make_async_copy(metal_in, metal, load_sem.at[3]),
        pltpu.make_async_copy(omega_in, omega, load_sem.at[4]),
        pltpu.make_async_copy(gamma_in, gamma, load_sem.at[5]),
        pltpu.make_async_copy(strength_in, strength, load_sem.at[6]),
    ]
    for load in loads:
        load.start()

    def ring(position, size):
        return [position] + [lax.rem(position + step, size) for step in range(1, size)]

    def device(x, core, y, z):
        return (x * cores + core, y * z_size + z)

    around_x = {0: gx, -1: lax.rem(gx + gx_size - 1, gx_size), 1: lax.rem(gx + 1, gx_size)}
    around_y = {0: gy, -1: lax.rem(gy + gy_size - 1, gy_size), 1: lax.rem(gy + 1, gy_size)}

    def neighbour(dx, dy):
        return (around_x[dx], around_y[dy])

    my_x, my_core = lax.div(gx, cores), lax.rem(gx, cores)
    my_y, my_z = lax.div(gy, z_size), lax.rem(gy, z_size)
    ring_x, ring_core = ring(my_x, x_size), ring(my_core, cores)
    ring_y, ring_z = ring(my_y, y_size), ring(my_z, z_size)

    def along(axis, step, core=0):
        return device(
            ring_x[step if axis == "x" else 0],
            ring_core[core],
            ring_y[step if axis == "y" else 0],
            ring_z[step if axis == "z" else 0],
        )

    def signal(semaphore, target):
        pl.semaphore_signal(semaphore, inc=1, device_id=target, device_id_type=MESH)

    beside = [(0, -1), (0, 1), (-1, 0), (1, 0)]
    near = [(axis, step, 0) for axis, _, steps, _ in rings(sizes) for step in steps]
    near += [(axis, step, 1) for axis, step, _ in near if axis == "z"]
    far = [(axis, step) for axis, _, _, steps in rings(sizes) for step in steps]
    barrier = pltpu.get_barrier_semaphore()
    for dx, dy in beside:
        signal(barrier, neighbour(dx, dy))
    for place in near:
        signal(barrier, along(*place))

    for load in loads:
        load.wait()

    for number, (f, layer) in enumerate(TO_PREVIOUS):
        previous_out[number] = raw[f, pl.ds(layer, OWN, stride=OWN), :]
    for number, (f, layer) in enumerate(TO_NEXT):
        next_out[number] = raw[f, pl.ds(OWN - 2 + layer, OWN, stride=OWN), :]
    corners = [(0, 0), (0, 1), (1, 0), (1, 1)]
    for number, (side_x, side_y) in enumerate(corners):
        for f in range(FIELDS):
            for layer in range(2):
                if side_x != side_y:
                    x = (0 if side_x == 0 else OWN - 2) + layer
                    y = 0 if side_y == 0 else OWN - 2
                    cells = raw[f, pl.ds(x * OWN + y, 2), :]
                    corner_out[number, pl.ds(f * 4 + layer * 2, 2), :] = cells
                elif layer == 0:
                    cell = 0 if side_x == 0 else OWN * OWN - 1
                    corner_out[number, pl.ds(f, 1), :] = raw[f, pl.ds(cell, 1), :]

    pl.semaphore_wait(barrier, len(beside) + len(near))

    copies = []

    def send(src, dst, device):
        number = len(copies)
        copy = pltpu.make_async_remote_copy(
            src_ref=src,
            dst_ref=dst,
            send_sem=face_send.at[number],
            recv_sem=face_recv.at[number],
            device_id=device,
            device_id_type=MESH,
        )
        copy.start()
        copies.append(copy)

    send(previous_out, previous_in, neighbour(0, -1))
    send(next_out, next_in, neighbour(0, 1))
    everything = pl.ds(0, FIELDS)
    layers = EDGE * OWN
    send(raw.at[everything, pl.ds(0, layers)], face_in.at[0], neighbour(-1, 0))
    send(raw.at[everything, pl.ds(OWN * OWN - layers, layers)], face_in.at[1], neighbour(1, 0))
    for dx, dy in beside[2:]:
        signal(heard.at[0], neighbour(dx, dy))
    for place in near:
        signal(heard.at[0], along(*place))

    tile_rows = [lax.rem(2 * gx + s - 1 + tiles[0], tiles[0]) for s in range(4)]
    tile_cols = [lax.rem(2 * gy + t - 1 + tiles[1], tiles[1]) for t in range(4)]
    place = lax.broadcasted_iota(jnp.int32, (8, 128), 0)
    for s in range(4):
        flag = [
            jnp.full((8, 128), metal[tile_rows[s], tile_cols[t]].astype(jnp.float32)) for t in range(4)
        ]
        mask[s, 0:8] = jnp.where(place < 6, flag[1], flag[2])
        mask[s, 8:16] = jnp.where(place < 2, flag[1], flag[2])
        beyond = jnp.where(place < 4, flag[3], flag[0])
        mask[s, 16:24] = jnp.where(place < 2, flag[2], jnp.where(place < 6, beyond, flag[1]))

    response = [jnp.float32(0.0)] * 3
    for p in range(POLES):
        g0 = strength[p]
        g1 = -gamma[p] * g0
        g2 = -(omega[p] * omega[p]) * g0 - gamma[p] * g1
        response = [response[0] + g0, response[1] + g1, response[2] + g2]

    def put_row(f, x, low, high):
        first = pl.multiple_of(x * PADY, 8)
        low_by_6, low_by_2 = pltpu.roll(low, 6, 0), pltpu.roll(low, 2, 0)
        high_by_6, high_by_2 = pltpu.roll(high, 6, 0), pltpu.roll(high, 2, 0)
        u[f, pl.ds(first, 8), :] = jnp.where(place < 6, low_by_6, high_by_6)
        u[f, pl.ds(first + 8, 8), :] = jnp.where(place < 2, low_by_2, high_by_2)
        u[f, pl.ds(first + 16, 8), :] = jnp.where(place < 4, high_by_2, low_by_6)

    def copy_own(x, carry):
        first = pl.multiple_of(x * OWN, 8)
        for f in range(FIELDS):
            put_row(f, x + EDGE, raw[f, pl.ds(first, 8), :], raw[f, pl.ds(first + 8, 8), :])
        return carry

    lax.fori_loop(0, OWN, copy_own, 0)

    pl.semaphore_wait(heard.at[0], len(beside[2:]) + len(near))
    for axis, step in far:
        signal(heard.at[1], along(axis, step))
    for number, (side_x, side_y) in enumerate(corners):
        rows = pl.ds(0, 8 if side_x == side_y else CORNER_ROWS)
        send(
            corner_out.at[number, rows],
            corner_in.at[number, rows],
            neighbour(2 * side_x - 1, 2 * side_y - 1),
        )

    class Padded:
        def __getitem__(self, at):
            f, x = at
            return u[f, pl.ds(pl.multiple_of(x * PADY, 8), PADY), :]

    start = Padded()
    states = [start, k1, k2, k3, k4]

    def electric(step, x):
        old = states[step - 1]
        hx, hy, hz = old[3, x], old[4, x], old[5, x]
        hy_back, hz_back = old[4, x - 1], old[5, x - 1]
        curl = [
            (hz - prev_y(hz)) - (hy - prev_z(hy)),
            (hx - prev_z(hx)) - (hz - hz_back),
            (hy - hy_back) - (hx - prev_y(hx)),
        ]
        eps = start[6, x]
        if step > 1:
            metal_here = mask[(x + 6) // 8]
            for c in range(3):
                current = response[step - 2] * start[c, x]
                for j in range(1, step - 1):
                    current = current + response[step - 2 - j] * states[j][c, x]
                curl[c] = curl[c] - metal_here * current
        return [eps * part for part in curl]

    def magnetic(step, x):
        old = states[step - 1]
        ex, ey, ez = old[0, x], old[1, x], old[2, x]
        ey_next, ez_next = old[1, x + 1], old[2, x + 1]
        return [
            (next_z(ey) - ey) - (next_y(ez) - ez),
            (ez_next - ez) - (next_z(ex) - ex),
            (next_y(ex) - ex) - (ey_next - ey),
        ]

    def write_rows(step, starts, shift):
        new = states[step]
        parts = [(x, electric(step, x), magnetic(step, x - shift)) for x in starts]
        for x, of_e, of_h in parts:
            for c in range(3):
                new[c, x] = of_e[c]
                new[3 + c, x - shift] = of_h[c]

    def interior(step, low, high, shift):
        rest = high - low - CHUNK
        chunks = -(-rest // CHUNK) + 1

        def rows(i, carry):
            first = low + (i * rest) // (chunks - 1)
            write_rows(step, [first + k for k in range(CHUNK)], shift)
            return carry

        lax.fori_loop(0, chunks, rows, 0)

    def edges(step, low, high, shift):
        write_rows(step, [low, low + 1, high, high + 1], shift)

    def state_at(j, c, x, first, count):
        if j == 0:
            return u[c, pl.ds(x * PADY + first, count), :]
        return states[j][c, x, pl.ds(first, count), :]

    def strip(j, c, x):
        if j == 0:
            return u[c, pl.ds(pl.multiple_of(x * PADY + STRIP, 8), 8), :]
        return states[j][c, x, pl.ds(STRIP, 8), :]

    def strip_prev(j, c, x, value):
        return jnp.where(place == 0, state_at(j, c, x, STRIP - 1, 1), pltpu.roll(value, 1, 0))

    def strip_next(j, c, x, value):
        return jnp.where(place == 7, state_at(j, c, x, 0, 1), pltpu.roll(value, 7, 0))

    def strip_electric(step, x):
        old = step - 1
        hx, hy, hz = (strip(old, c, x) for c in (3, 4, 5))
        hy_back, hz_back = strip(old, 4, x - 1), strip(old, 5, x - 1)
        curl = [
            (hz - strip_prev(old, 5, x, hz)) - (hy - prev_z(hy)),
            (hx - prev_z(hx)) - (hz - hz_back),
            (hy - hy_back) - (hx - strip_prev(old, 3, x, hx)),
        ]
        if step > 1:
            metal_here = mask[(x + 6) // 8, pl.ds(STRIP, 8), :]
            for c in range(3):
                current = response[step - 2] * strip(0, c, x)
                for j in range(1, step - 1):
                    current = current + response[step - 2 - j] * strip(j, c, x)
                curl[c] = curl[c] - metal_here * current
        eps = strip(0, 6, x)
        return [eps * part for part in curl]

    def strip_magnetic(step, x):
        old = step - 1
        ex, ey, ez = (strip(old, c, x) for c in (0, 1, 2))
        ey_next, ez_next = strip(old, 1, x + 1), strip(old, 2, x + 1)
        return [
            (next_z(ey) - ey) - (strip_next(old, 2, x, ez) - ez),
            (ez_next - ez) - (next_z(ex) - ex),
            (strip_next(old, 0, x, ex) - ex) - (ey_next - ey),
        ]

    def write_strips(step, starts, shift):
        new = states[step]
        parts = [(x, strip_electric(step, x), strip_magnetic(step, x - shift)) for x in starts]
        for x, of_e, of_h in parts:
            for c in range(3):
                new[c, x, pl.ds(STRIP, 8), :] = of_e[c]
                new[3 + c, x - shift, pl.ds(STRIP, 8), :] = of_h[c]

    def interior_strips(step, low, high, shift):
        rest = high - low - STRIP_CHUNK

        def rows(i, carry):
            write_strips(step, [low + i * rest + k for k in range(STRIP_CHUNK)], shift)
            return carry

        lax.fori_loop(0, 2, rows, 0)

    def edge_strips(step, low, high, shift):
        write_strips(step, [low, low + 1, high, high + 1], shift)

    zero = jnp.zeros((8, 128), jnp.float32)

    def products(first, x, sums):
        sums = list(sums)
        cells = pl.ds(first, 8)
        for c in range(6):
            values = [u[c, pl.ds(pl.multiple_of(x * PADY + first, 8), 8), :]]
            values += [state[c, x, cells, :] for state in states[1:]]
            for number, (i, j) in enumerate(PAIRS):
                sums[number] = sums[number] + values[i] * values[j]
        return tuple(sums)

    def interior_products(first, sums):
        return lax.fori_loop(
            EDGE + 2, EDGE + OWN - 2, lambda x, sums: products(first, x, sums), sums
        )

    def edge_products(first, sums):
        return lax.fori_loop(
            0,
            2 * EDGE,
            lambda i, sums: products(first, EDGE + i + i // 2 * (OWN - 4), sums),
            sums,
        )

    def keep(sums, wanted, into):
        for number, part in enumerate(sums):
            at = pl.ds(8 * number, 8)
            part = jnp.where(wanted, part, 0.0)
            acc_rows[at, :] = part + acc_rows[at, :] if into else part

    none = (zero,) * len(PAIRS)
    interior(1, EDGE + 1, EDGE + OWN, 1)
    interior(2, EDGE + 1, EDGE + OWN - 1, 0)
    interior(3, EDGE + 2, EDGE + OWN - 1, 1)
    interior(4, EDGE + 2, EDGE + OWN - 2, 0)
    keep(interior_products(0, none), place < 6, False)
    keep(interior_products(8, none), place >= 2, True)
    acc_rows[pl.ds(8 * len(PAIRS), 8), :] = zero

    for copy in copies[2:4]:
        copy.wait_recv()
    for f in range(FIELDS):
        for side, first in ((0, EDGE + OWN), (1, 0)):
            for layer in range(2):
                low = face_in[side, f, pl.ds(layer * OWN, 8), :]
                high = face_in[side, f, pl.ds(layer * OWN + 8, 8), :]
                put_row(f, first + layer, low, high)
    edges(1, 1, EDGE + OWN, 1)
    edges(2, 1, EDGE + OWN - 1, 0)
    edges(3, EDGE, EDGE + OWN - 1, 1)
    edges(4, EDGE, EDGE + OWN - 2, 0)
    keep(edge_products(0, none), place < 6, True)
    keep(edge_products(8, none), place >= 2, True)

    for copy in copies[:2]:
        copy.wait_recv()
    for number, (f, layer) in enumerate(TO_PREVIOUS):
        u[f, pl.ds(EDGE * PADY + HIGH + layer, OWN, stride=PADY), :] = previous_in[number]
    for number, (f, layer) in enumerate(TO_NEXT):
        u[f, pl.ds(EDGE * PADY + LOW + layer, OWN, stride=PADY), :] = next_in[number]
    interior_strips(1, EDGE + 1, EDGE + OWN, 1)
    interior_strips(2, EDGE + 1, EDGE + OWN - 1, 0)
    interior_strips(3, EDGE + 2, EDGE + OWN - 1, 1)
    interior_strips(4, EDGE + 2, EDGE + OWN - 2, 0)
    sums = interior_products(STRIP, none)

    for copy in copies[4:]:
        copy.wait_recv()
    for number, (side_x, side_y) in enumerate(corners):
        for f in range(FIELDS):
            for layer in range(2):
                x = (EDGE + OWN if side_x == 0 else 0) + layer
                y = HIGH if side_y == 0 else LOW
                if side_x != side_y:
                    source = corner_in[number, pl.ds(f * 4 + layer * 2, 2), :]
                    u[f, pl.ds(x * PADY + y, 2), :] = source
                elif layer == side_x:
                    u[f, pl.ds(x * PADY + y + layer, 1), :] = corner_in[number, pl.ds(f, 1), :]
    edge_strips(1, 1, EDGE + OWN, 1)
    edge_strips(2, 1, EDGE + OWN - 1, 0)
    edge_strips(3, EDGE, EDGE + OWN - 1, 1)
    edge_strips(4, EDGE, EDGE + OWN - 2, 0)
    keep(edge_products(STRIP, sums), jnp.logical_or(place < 2, place >= 6), True)

    total = acc_rows[pl.ds(0, 16, stride=8), :]
    for s in range(1, 8):
        total = total + acc_rows[pl.ds(s, 16, stride=8), :]
    diagonal = lax.broadcasted_iota(jnp.int32, (16, 128), 0) == lax.broadcasted_iota(jnp.int32, (16, 128), 1)

    def to_row(column):
        return jnp.sum(jnp.where(diagonal, column, 0.0), axis=0, keepdims=True)

    def gather_metal():
        flags = [metal[tile_rows[1 + t // 2], tile_cols[1 + t % 2]] for t in range(4)]
        present = [flag.astype(jnp.float32) for flag in flags]
        before = jnp.float32(0.0)
        chosen = [[None] * 4 for _ in range(MS)]
        for t in range(4):
            taken = [present[t] * (1.0 - before), present[t] * before]
            before = before + present[t]
            for slot in range(MS):
                chosen[slot][t] = taken[slot]

        def rows(x, carry):
            for c in range(3):
                for j in range(STEPS):
                    parts = []
                    for t in range(4):
                        at = 8 * (t // 2) + x
                        y = 8 * (t % 2)
                        if j == 0:
                            parts.append(raw[c, pl.ds(pl.multiple_of(at * OWN + y, 8), 8), :])
                        else:
                            parts.append(own_out[j - 1, c, at, pl.ds(y, 8), :])
                    for slot in range(MS):
                        value = chosen[slot][0] * parts[0]
                        for t in range(1, 4):
                            value = value + chosen[slot][t] * parts[t]
                        tiles_out[slot, j, c, x] = value
            return carry

        lax.fori_loop(0, 8, rows, 0)
        for p in range(POLES):
            kicks = [strength[p]]
            kicks.append(-gamma[p] * kicks[0])
            for k in range(2, STEPS):
                kicks.append(-(omega[p] * omega[p]) * kicks[k - 2] - gamma[p] * kicks[k - 1])
            for k in range(STEPS):
                kicks_out[pl.ds(p * STEPS + k, 1), :] = jnp.full((1, 128), kicks[k])

    def order_own():
        def rows(x, carry):
            for j, state in enumerate(states[1:]):
                for c in range(6):
                    tile = [state[c, x + EDGE, pl.ds(8 * t, 8), :] for t in range(3)]
                    own_out[j, c, x, pl.ds(0, 8), :] = jnp.where(
                        place < 2, pltpu.roll(tile[2], 2, 0), pltpu.roll(tile[0], 2, 0)
                    )
                    own_out[j, c, x, pl.ds(8, 8), :] = jnp.where(
                        place < 6, pltpu.roll(tile[1], 6, 0), pltpu.roll(tile[2], 6, 0)
                    )
            return carry

        lax.fori_loop(0, OWN, rows, 0)

    row = to_row(jnp.sum(total, axis=1, keepdims=True))
    if far:
        pl.semaphore_wait(heard.at[1], len(far))
    me_a = my_core * z_size + my_z
    me_b = my_x * y_size + my_y
    targets_a = [
        device(my_x, ring_core[c], my_y, ring_z[z]) for c, z in farthest_first(cores, z_size)
    ]
    targets_b = [
        device(ring_x[x], my_core, ring_y[y], my_z) for x, y in farthest_first(x_size, y_size)
    ]
    for stage, (slots, me, targets) in enumerate(((sum_a, me_a, targets_a), (sum_b, me_b, targets_b))):
        slots[me] = row
        for target in targets:
            pltpu.make_async_remote_copy(
                src_ref=slots.at[me],
                dst_ref=slots.at[me],
                send_sem=stage_send.at[stage],
                recv_sem=stage_recv.at[stage],
                device_id=target,
                device_id_type=MESH,
            ).start()
        if stage == 0:
            order_own()
        else:
            gather_metal()
        settle(slots.at[pl.ds(0, len(targets))], stage_recv.at[stage])
        row = slots[0]
        for member in range(1, len(targets) + 1):
            row = row + slots[member]
    gram_out[...] = jnp.broadcast_to(
        jnp.sum(jnp.where(diagonal, row, 0.0), axis=1, keepdims=True), (16, 128)
    )

    for copy in copies:
        copy.wait_send()
    for stage, (slots, targets) in enumerate(((sum_a, targets_a), (sum_b, targets_b))):
        settle(slots.at[pl.ds(0, len(targets))], stage_send.at[stage])


def finish_kernel(
    cell_count,
    k0,
    own,
    gram,
    tiles,
    kicks,
    out_e,
    out_h,
    out_poles,
    out_coefficients,
    coefficients,
    table,
    fields,
    poles,
    pole_sem,
    store_sem,
):
    stores = []

    def store(src, dst):
        copy = pltpu.make_async_copy(src, dst, store_sem.at[len(stores)])
        copy.start()
        stores.append(copy)

    inner = {}
    for number, (i, j) in enumerate(PAIRS):
        inner[i, j] = inner[j, i] = gram[pl.ds(number, 1), :] * (1.0 / cell_count)
    unit = 1.0 / jnp.sqrt(inner[0, 0] + EPSILON)
    weights = [unit]
    lane = lax.broadcasted_iota(jnp.int32, (1, 128), 1)
    for step in range(1, STEPS + 1):
        image = [None] + weights

        def total(terms):
            return functools.reduce(jnp.add, terms)

        along_q = unit * total([image[j] * inner[0, j] for j in range(1, step + 1)])
        rest = [-along_q * unit] + image[1:]
        along_v = jnp.zeros_like(unit)
        if step > 1:
            along_v = total(
                [
                    image[j] * total([weights[i] * inner[i, j] for i in range(step)])
                    for j in range(1, step + 1)
                ]
            )
            for i in range(step):
                rest[i] = rest[i] - along_v * weights[i]
        squared = total(
            [rest[i] * total([rest[j] * inner[i, j] for j in range(step + 1)]) for i in range(step + 1)]
        )
        norm = jnp.sqrt(jnp.maximum(squared, 0.0) + EPSILON)
        scale = 1.0 / norm
        weights = [part * scale for part in rest]
        line = jnp.where(lane == 0, along_q, jnp.where(lane == 1, along_v, norm))
        coefficients[pl.ds(step - 1, 1), :] = line[:, :3]

    store(coefficients, out_coefficients)

    for p in range(POLES):
        kick = [kicks[pl.ds(p * STEPS + k, 1), :] for k in range(STEPS)]
        for j in range(STEPS):
            parts = [weights[k] * kick[k - 1 - j] for k in range(j + 1, STEPS + 1)]
            table[pl.ds(p * 8 + j, 1), :] = functools.reduce(jnp.add, parts)
        for j in range(STEPS - 1):
            parts = [weights[k] * kick[k - 2 - j] for k in range(j + 2, STEPS + 1)]
            table[pl.ds(p * 8 + 4 + j, 1), :] = functools.reduce(jnp.add, parts)
    for j in range(STEPS + 1):
        table[pl.ds(48 + j, 1), :] = weights[j]

    def entry(number):
        return jnp.broadcast_to(table[pl.ds(number, 1), :], (8, 128))

    def pole_part(i):
        return (i // 3, pl.ds(0, 2), pl.ds(0, POLES), i % 3)

    def pole_cells(i, carry):
        slot, c = i // 3, i % 3
        for x in range(8):
            field = [tiles[slot, j, c, x] for j in range(STEPS)]
            for p in range(POLES):
                poles[slot, 1, p, c, x] = functools.reduce(
                    jnp.add, [entry(p * 8 + j) * field[j] for j in range(STEPS)]
                )
                poles[slot, 0, p, c, x] = functools.reduce(
                    jnp.add, [entry(p * 8 + 4 + j) * field[j] for j in range(STEPS - 1)]
                )
        pltpu.make_async_copy(
            poles.at[pole_part(i)], out_poles.at[pole_part(i)], pole_sem.at[i]
        ).start()
        return carry

    lax.fori_loop(0, 3 * MS, pole_cells, 0)

    for half, out in enumerate((out_e, out_h)):

        def field_cells(i, carry):
            for x in [4 * i + k for k in range(4)]:
                for c in range(3 * half, 3 * half + 3):
                    cells = pl.ds(pl.multiple_of(x * OWN, 8), OWN)
                    value = table[pl.ds(48, 1), :] * k0[c, cells, :]
                    for j in range(STEPS):
                        value = value + table[pl.ds(49 + j, 1), :] * own[j, c, x]
                    fields[c, x] = value
            return carry

        lax.fori_loop(0, OWN // 4, field_cells, 0)
        store(fields.at[pl.ds(3 * half, 3)], out)
    for i in range(3 * MS):
        pltpu.make_async_copy(poles.at[pole_part(i)], out_poles.at[pole_part(i)], pole_sem.at[i]).wait()
    for copy in stores:
        copy.wait()


def body(sizes, u_electric, u_magnetic, eps_inv, metal_map, pole_omega, pole_gamma, pole_strength):
    depth = u_electric.shape[3]
    cell_count = 6.0 * OWN * OWN * depth * sizes[0] * sizes[1] * sizes[2] * sizes[3]
    f32 = jnp.float32
    any_spec = pl.BlockSpec(memory_space=pl.ANY)
    hbm = pl.BlockSpec(memory_space=pltpu.HBM)
    vmem = pl.BlockSpec(memory_space=pltpu.VMEM)
    a_size = sizes[1] * sizes[3]
    b_size = sizes[0] * sizes[2]

    def stay(value):
        return pltpu.with_memory_space_constraint(value, pltpu.HBM)

    start = [u_electric.reshape(3, OWN * OWN, depth), u_magnetic.reshape(3, OWN * OWN, depth)]
    model = [stay(part) for part in (metal_map, pole_omega, pole_gamma, pole_strength)]
    dma = pltpu.SemaphoreType.DMA
    results = pl.pallas_call(
        functools.partial(exchange_kernel, sizes, metal_map.shape),
        out_shape=[
            jax.ShapeDtypeStruct((STEPS, 6, OWN, OWN, depth), f32),
            jax.ShapeDtypeStruct((16, depth), f32),
            jax.ShapeDtypeStruct((MS, STEPS, 3, 8, 8, depth), f32),
            jax.ShapeDtypeStruct((POLES * STEPS, depth), f32),
            jax.ShapeDtypeStruct((FIELDS, OWN * OWN, depth), f32),
        ],
        in_specs=[hbm] * 7,
        out_specs=[vmem] * 5,
        scratch_shapes=[
            pltpu.VMEM((2, FIELDS, EDGE * OWN, depth), f32),
            *[pltpu.VMEM((6, PADX, PADY, depth), f32)] * STEPS,
            pltpu.VMEM((FIELDS, ROW, depth), f32),
            pltpu.VMEM((len(TO_PREVIOUS), OWN, depth), f32),
            pltpu.VMEM((len(TO_PREVIOUS), OWN, depth), f32),
            pltpu.VMEM((len(TO_NEXT), OWN, depth), f32),
            pltpu.VMEM((len(TO_NEXT), OWN, depth), f32),
            pltpu.VMEM((4, CORNER_ROWS, depth), f32),
            pltpu.VMEM((4, CORNER_ROWS, depth), f32),
            pltpu.VMEM((4, PADY, depth), f32),
            pltpu.VMEM((128, depth), f32),
            pltpu.VMEM((a_size, 1, depth), f32),
            pltpu.VMEM((b_size, 1, depth), f32),
            pltpu.SMEM(metal_map.shape, jnp.int32),
            pltpu.SMEM((POLES,), f32),
            pltpu.SMEM((POLES,), f32),
            pltpu.SMEM((POLES,), f32),
            pltpu.SemaphoreType.REGULAR((2,)),
            dma((7,)),
            dma((8,)),
            dma((8,)),
            dma((2,)),
            dma((2,)),
        ],
        compiler_params=pltpu.CompilerParams(
            collective_id=0, has_side_effects=True, vmem_limit_bytes=VMEM_LIMIT
        ),
    )(*[stay(part) for part in start], stay(eps_inv.reshape(OWN * OWN, depth)), *model)

    own, gram, tiles, kicks, raw = results

    return pl.pallas_call(
        functools.partial(finish_kernel, cell_count),
        out_shape=[
            jax.ShapeDtypeStruct(u_electric.shape, f32),
            jax.ShapeDtypeStruct(u_magnetic.shape, f32),
            jax.ShapeDtypeStruct((MS, 2, POLES, 3, 8, 8, depth), f32),
            jax.ShapeDtypeStruct((STEPS, 3), f32),
        ],
        in_specs=[vmem] * 5,
        out_specs=[any_spec] * 4,
        scratch_shapes=[
            pltpu.VMEM((STEPS, 3), f32),
            pltpu.VMEM((56, depth), f32),
            pltpu.VMEM((6, OWN, OWN, depth), f32),
            pltpu.VMEM((MS, 2, POLES, 3, 8, 8, depth), f32),
            dma((3 * MS,)),
            dma((3,)),
        ],
        compiler_params=pltpu.CompilerParams(vmem_limit_bytes=VMEM_LIMIT),
    )(raw, own, gram, tiles, kicks)


def solution(mesh):
    sizes = layout(mesh.shape["gx"], mesh.shape["gy"])
    placed = (
        P(None, "gx", "gy", None),
        P(None, "gx", "gy", None),
        P("gx", "gy", None),
        P(),
        P(),
        P(),
        P(),
    )
    return jax.shard_map(
        functools.partial(body, sizes),
        mesh=mesh,
        in_specs=placed,
        out_specs=(
            P(None, "gx", "gy", None),
            P(None, "gx", "gy", None),
            P(("gx", "gy"), None, None, None, None, None, None),
            P(),
        ),
        check_vma=False,
    )
```

```python
import functools

import jax
import jax.numpy as jnp
from jax import lax
from jax.experimental import pallas as pl
from jax.experimental.pallas import tpu as pltpu
from jax.sharding import PartitionSpec as P

POLES = 6
STEPS = 4
MS = 2
EPSILON = 1e-06
MESH = pl.DeviceIdType.MESH

EDGE = 2
OWN = 16
PADX = OWN + 2 * EDGE
PADY = 24
HIGH = 18
LOW = 20
STRIP = 16
FIELDS = 7
TO_PREVIOUS = [(f, 0) for f in range(FIELDS)] + [(f, 1) for f in (0, 2, 3, 4, 5, 6)]
TO_NEXT = [(f, 1) for f in range(FIELDS)] + [(f, 0) for f in (0, 1, 2, 3, 5)]
ROW = PADX * PADY
CORNER_ROWS = 32
CHUNK = 5
PAIRS = [(i, j) for i in range(STEPS + 1) for j in range(i, STEPS + 1)]
VMEM_LIMIT = 40 * 1024 * 1024


def layout(gx_size, gy_size):
    cores = 2
    z_size = min(8, gy_size // 2)
    return gx_size // cores, cores, gy_size // z_size, z_size


def rings(sizes):
    result = []
    for axis, size in (("x", sizes[0]), ("y", sizes[2]), ("z", sizes[3])):
        near = sorted({1 % size, size - 1} - {0})
        far = sorted({2 % size, (size - 2) % size} - {0}) if size > 3 else []
        result.append((axis, size, near, far))
    return result


def farthest_first(first, second):
    def hops(step, size):
        return min(step, size - step)

    steps = [(a, b) for a in range(first) for b in range(second) if a or b]
    return sorted(steps, key=lambda step: -hops(step[0], first) - hops(step[1], second))


def next_y(value):
    return pltpu.roll(value, PADY - 1, 0)


def prev_y(value):
    return pltpu.roll(value, 1, 0)


def next_z(value):
    return pltpu.roll(value, value.shape[1] - 1, 1)


def prev_z(value):
    return pltpu.roll(value, 1, 1)


def settle(buffer, semaphore):
    pltpu.make_async_copy(buffer, buffer, semaphore).wait()


def exchange_kernel(
    sizes,
    tiles,
    u_e,
    u_h,
    eps_in,
    metal_in,
    omega_in,
    gamma_in,
    strength_in,
    own_out,
    gram_out,
    tiles_out,
    kicks_out,
    raw,
    face_in,
    k1,
    k2,
    k3,
    k4,
    u,
    previous_out,
    previous_in,
    next_out,
    next_in,
    corner_out,
    corner_in,
    mask,
    acc_rows,
    sum_a,
    sum_b,
    metal,
    omega,
    gamma,
    strength,
    heard,
    load_sem,
    face_send,
    face_recv,
    stage_send,
    stage_recv,
):
    x_size, cores, y_size, z_size = sizes
    gx_size, gy_size = x_size * cores, y_size * z_size
    gx = lax.axis_index("gx")
    gy = lax.axis_index("gy")

    loads = [
        pltpu.make_async_copy(u_e, raw.at[pl.ds(0, 3)], load_sem.at[0]),
        pltpu.make_async_copy(u_h, raw.at[pl.ds(3, 3)], load_sem.at[1]),
        pltpu.make_async_copy(eps_in, raw.at[6], load_sem.at[2]),
        pltpu.make_async_copy(metal_in, metal, load_sem.at[3]),
        pltpu.make_async_copy(omega_in, omega, load_sem.at[4]),
        pltpu.make_async_copy(gamma_in, gamma, load_sem.at[5]),
        pltpu.make_async_copy(strength_in, strength, load_sem.at[6]),
    ]
    for load in loads:
        load.start()

    def ring(position, size):
        return [position] + [lax.rem(position + step, size) for step in range(1, size)]

    def device(x, core, y, z):
        return (x * cores + core, y * z_size + z)

    around_x = {0: gx, -1: lax.rem(gx + gx_size - 1, gx_size), 1: lax.rem(gx + 1, gx_size)}
    around_y = {0: gy, -1: lax.rem(gy + gy_size - 1, gy_size), 1: lax.rem(gy + 1, gy_size)}

    def neighbour(dx, dy):
        return (around_x[dx], around_y[dy])

    my_x, my_core = lax.div(gx, cores), lax.rem(gx, cores)
    my_y, my_z = lax.div(gy, z_size), lax.rem(gy, z_size)
    ring_x, ring_core = ring(my_x, x_size), ring(my_core, cores)
    ring_y, ring_z = ring(my_y, y_size), ring(my_z, z_size)

    def along(axis, step, core=0):
        return device(
            ring_x[step if axis == "x" else 0],
            ring_core[core],
            ring_y[step if axis == "y" else 0],
            ring_z[step if axis == "z" else 0],
        )

    def signal(semaphore, target):
        pl.semaphore_signal(semaphore, inc=1, device_id=target, device_id_type=MESH)

    beside = [(0, -1), (0, 1), (-1, 0), (1, 0)]
    near = [(axis, step, 0) for axis, _, steps, _ in rings(sizes) for step in steps]
    near += [(axis, step, 1) for axis, step, _ in near if axis == "z"]
    far = [(axis, step) for axis, _, _, steps in rings(sizes) for step in steps]
    barrier = pltpu.get_barrier_semaphore()
    for dx, dy in beside:
        signal(barrier, neighbour(dx, dy))
    for place in near:
        signal(barrier, along(*place))

    for load in loads:
        load.wait()

    for number, (f, layer) in enumerate(TO_PREVIOUS):
        previous_out[number] = raw[f, pl.ds(layer, OWN, stride=OWN), :]
    for number, (f, layer) in enumerate(TO_NEXT):
        next_out[number] = raw[f, pl.ds(OWN - 2 + layer, OWN, stride=OWN), :]
    corners = [(0, 0), (0, 1), (1, 0), (1, 1)]
    for number, (side_x, side_y) in enumerate(corners):
        for f in range(FIELDS):
            for layer in range(2):
                if side_x != side_y:
                    x = (0 if side_x == 0 else OWN - 2) + layer
                    y = 0 if side_y == 0 else OWN - 2
                    cells = raw[f, pl.ds(x * OWN + y, 2), :]
                    corner_out[number, pl.ds(f * 4 + layer * 2, 2), :] = cells
                elif layer == 0:
                    cell = 0 if side_x == 0 else OWN * OWN - 1
                    corner_out[number, pl.ds(f, 1), :] = raw[f, pl.ds(cell, 1), :]

    pl.semaphore_wait(barrier, len(beside) + len(near))

    copies = []

    def send(src, dst, device):
        number = len(copies)
        copy = pltpu.make_async_remote_copy(
            src_ref=src,
            dst_ref=dst,
            send_sem=face_send.at[number],
            recv_sem=face_recv.at[number],
            device_id=device,
            device_id_type=MESH,
        )
        copy.start()
        copies.append(copy)

    send(previous_out, previous_in, neighbour(0, -1))
    send(next_out, next_in, neighbour(0, 1))
    everything = pl.ds(0, FIELDS)
    layers = EDGE * OWN
    send(raw.at[everything, pl.ds(0, layers)], face_in.at[0], neighbour(-1, 0))
    send(raw.at[everything, pl.ds(OWN * OWN - layers, layers)], face_in.at[1], neighbour(1, 0))
    for dx, dy in beside[2:]:
        signal(heard.at[0], neighbour(dx, dy))
    for place in near:
        signal(heard.at[0], along(*place))

    tile_rows = [lax.rem(2 * gx + s - 1 + tiles[0], tiles[0]) for s in range(4)]
    tile_cols = [lax.rem(2 * gy + t - 1 + tiles[1], tiles[1]) for t in range(4)]
    place = lax.broadcasted_iota(jnp.int32, (8, 128), 0)
    for s in range(4):
        flag = [
            jnp.full((8, 128), metal[tile_rows[s], tile_cols[t]].astype(jnp.float32)) for t in range(4)
        ]
        mask[s, 0:8] = jnp.where(place < 6, flag[1], flag[2])
        mask[s, 8:16] = jnp.where(place < 2, flag[1], flag[2])
        beyond = jnp.where(place < 4, flag[3], flag[0])
        mask[s, 16:24] = jnp.where(place < 2, flag[2], jnp.where(place < 6, beyond, flag[1]))

    response = [jnp.float32(0.0)] * 3
    for p in range(POLES):
        g0 = strength[p]
        g1 = -gamma[p] * g0
        g2 = -(omega[p] * omega[p]) * g0 - gamma[p] * g1
        response = [response[0] + g0, response[1] + g1, response[2] + g2]

    def put_row(f, x, low, high):
        first = pl.multiple_of(x * PADY, 8)
        low_by_6, low_by_2 = pltpu.roll(low, 6, 0), pltpu.roll(low, 2, 0)
        high_by_6, high_by_2 = pltpu.roll(high, 6, 0), pltpu.roll(high, 2, 0)
        u[f, pl.ds(first, 8), :] = jnp.where(place < 6, low_by_6, high_by_6)
        u[f, pl.ds(first + 8, 8), :] = jnp.where(place < 2, low_by_2, high_by_2)
        u[f, pl.ds(first + 16, 8), :] = jnp.where(place < 4, high_by_2, low_by_6)

    def copy_own(x, carry):
        first = pl.multiple_of(x * OWN, 8)
        for f in range(FIELDS):
            put_row(f, x + EDGE, raw[f, pl.ds(first, 8), :], raw[f, pl.ds(first + 8, 8), :])
        return carry

    lax.fori_loop(0, OWN, copy_own, 0)

    pl.semaphore_wait(heard.at[0], len(beside[2:]) + len(near))
    for axis, step in far:
        signal(heard.at[1], along(axis, step))
    for number, (side_x, side_y) in enumerate(corners):
        rows = pl.ds(0, 8 if side_x == side_y else CORNER_ROWS)
        send(
            corner_out.at[number, rows],
            corner_in.at[number, rows],
            neighbour(2 * side_x - 1, 2 * side_y - 1),
        )

    class Padded:
        def __getitem__(self, at):
            f, x = at
            return u[f, pl.ds(pl.multiple_of(x * PADY, 8), PADY), :]

    start = Padded()
    states = [start, k1, k2, k3, k4]

    def electric(step, x):
        old = states[step - 1]
        hx, hy, hz = old[3, x], old[4, x], old[5, x]
        hy_back, hz_back = old[4, x - 1], old[5, x - 1]
        curl = [
            (hz - prev_y(hz)) - (hy - prev_z(hy)),
            (hx - prev_z(hx)) - (hz - hz_back),
            (hy - hy_back) - (hx - prev_y(hx)),
        ]
        eps = start[6, x]
        if step > 1:
            metal_here = mask[(x + 6) // 8]
            for c in range(3):
                current = response[step - 2] * start[c, x]
                for j in range(1, step - 1):
                    current = current + response[step - 2 - j] * states[j][c, x]
                curl[c] = curl[c] - metal_here * current
        return [eps * part for part in curl]

    def magnetic(step, x):
        old = states[step - 1]
        ex, ey, ez = old[0, x], old[1, x], old[2, x]
        ey_next, ez_next = old[1, x + 1], old[2, x + 1]
        return [
            (next_z(ey) - ey) - (next_y(ez) - ez),
            (ez_next - ez) - (next_z(ex) - ex),
            (next_y(ex) - ex) - (ey_next - ey),
        ]

    def write_rows(step, starts, shift):
        new = states[step]
        parts = [(x, electric(step, x), magnetic(step, x - shift)) for x in starts]
        for x, of_e, of_h in parts:
            for c in range(3):
                new[c, x] = of_e[c]
                new[3 + c, x - shift] = of_h[c]

    def interior(step, low, high, shift):
        rest = high - low - CHUNK
        chunks = -(-rest // CHUNK) + 1

        def rows(i, carry):
            first = low + (i * rest) // (chunks - 1)
            write_rows(step, [first + k for k in range(CHUNK)], shift)
            return carry

        lax.fori_loop(0, chunks, rows, 0)

    def edges(step, low, high, shift):
        write_rows(step, [low, low + 1, high, high + 1], shift)

    def state_at(j, c, x, first, count):
        if j == 0:
            return u[c, pl.ds(x * PADY + first, count), :]
        return states[j][c, x, pl.ds(first, count), :]

    def strip(j, c, x):
        if j == 0:
            return u[c, pl.ds(pl.multiple_of(x * PADY + STRIP, 8), 8), :]
        return states[j][c, x, pl.ds(STRIP, 8), :]

    def strip_prev(j, c, x, value):
        return jnp.where(place == 0, state_at(j, c, x, STRIP - 1, 1), pltpu.roll(value, 1, 0))

    def strip_next(j, c, x, value):
        return jnp.where(place == 7, state_at(j, c, x, 0, 1), pltpu.roll(value, 7, 0))

    def strip_electric(step, x):
        old = step - 1
        hx, hy, hz = (strip(old, c, x) for c in (3, 4, 5))
        hy_back, hz_back = strip(old, 4, x - 1), strip(old, 5, x - 1)
        curl = [
            (hz - strip_prev(old, 5, x, hz)) - (hy - prev_z(hy)),
            (hx - prev_z(hx)) - (hz - hz_back),
            (hy - hy_back) - (hx - strip_prev(old, 3, x, hx)),
        ]
        if step > 1:
            metal_here = mask[(x + 6) // 8, pl.ds(STRIP, 8), :]
            for c in range(3):
                current = response[step - 2] * strip(0, c, x)
                for j in range(1, step - 1):
                    current = current + response[step - 2 - j] * strip(j, c, x)
                curl[c] = curl[c] - metal_here * current
        eps = strip(0, 6, x)
        return [eps * part for part in curl]

    def strip_magnetic(step, x):
        old = step - 1
        ex, ey, ez = (strip(old, c, x) for c in (0, 1, 2))
        ey_next, ez_next = strip(old, 1, x + 1), strip(old, 2, x + 1)
        return [
            (next_z(ey) - ey) - (strip_next(old, 2, x, ez) - ez),
            (ez_next - ez) - (next_z(ex) - ex),
            (strip_next(old, 0, x, ex) - ex) - (ey_next - ey),
        ]

    def write_strips(step, starts, shift):
        new = states[step]
        parts = [(x, strip_electric(step, x), strip_magnetic(step, x - shift)) for x in starts]
        for x, of_e, of_h in parts:
            for c in range(3):
                new[c, x, pl.ds(STRIP, 8), :] = of_e[c]
                new[3 + c, x - shift, pl.ds(STRIP, 8), :] = of_h[c]

    def interior_strips(step, low, high, shift):
        write_strips(step, list(range(low, high)), shift)

    def edge_strips(step, low, high, shift):
        write_strips(step, [low, low + 1, high, high + 1], shift)

    zero = jnp.zeros((8, 128), jnp.float32)

    def products(first, x, sums):
        sums = list(sums)
        cells = pl.ds(first, 8)
        for c in range(6):
            values = [u[c, pl.ds(pl.multiple_of(x * PADY + first, 8), 8), :]]
            values += [state[c, x, cells, :] for state in states[1:]]
            for number, (i, j) in enumerate(PAIRS):
                sums[number] = sums[number] + values[i] * values[j]
        return tuple(sums)

    ends = jnp.logical_or(place < 2, place >= 6)

    def strip_products(pairs, sums):
        sums = list(sums)
        for x, other in pairs:
            for c in range(6):
                values = [
                    jnp.where(ends, strip(j, c, x), pltpu.roll(strip(j, c, other), 4, 0))
                    for j in range(STEPS + 1)
                ]
                for number, (i, j) in enumerate(PAIRS):
                    sums[number] = sums[number] + values[i] * values[j]
        return tuple(sums)

    def interior_products(first, sums):
        return lax.fori_loop(
            EDGE + 2, EDGE + OWN - 2, lambda x, sums: products(first, x, sums), sums
        )

    def edge_products(first, sums):
        return lax.fori_loop(
            0,
            2 * EDGE,
            lambda i, sums: products(first, EDGE + i + i // 2 * (OWN - 4), sums),
            sums,
        )

    def keep(sums, wanted, into):
        for number, part in enumerate(sums):
            at = pl.ds(8 * number, 8)
            part = jnp.where(wanted, part, 0.0)
            acc_rows[at, :] = part + acc_rows[at, :] if into else part

    none = (zero,) * len(PAIRS)
    interior(1, EDGE + 1, EDGE + OWN, 1)
    interior(2, EDGE + 1, EDGE + OWN - 1, 0)
    interior(3, EDGE + 2, EDGE + OWN - 1, 1)
    interior(4, EDGE + 2, EDGE + OWN - 2, 0)
    keep(interior_products(0, none), place < 6, False)
    keep(interior_products(8, none), place >= 2, True)
    acc_rows[pl.ds(8 * len(PAIRS), 8), :] = zero

    for copy in copies[2:4]:
        copy.wait_recv()
    for f in range(FIELDS):
        for side, first in ((0, EDGE + OWN), (1, 0)):
            for layer in range(2):
                low = face_in[side, f, pl.ds(layer * OWN, 8), :]
                high = face_in[side, f, pl.ds(layer * OWN + 8, 8), :]
                put_row(f, first + layer, low, high)
    edges(1, 1, EDGE + OWN, 1)
    edges(2, 1, EDGE + OWN - 1, 0)
    edges(3, EDGE, EDGE + OWN - 1, 1)
    edges(4, EDGE, EDGE + OWN - 2, 0)
    keep(edge_products(0, none), place < 6, True)
    keep(edge_products(8, none), place >= 2, True)

    for copy in copies[:2]:
        copy.wait_recv()
    for number, (f, layer) in enumerate(TO_PREVIOUS):
        u[f, pl.ds(EDGE * PADY + HIGH + layer, OWN, stride=PADY), :] = previous_in[number]
    for number, (f, layer) in enumerate(TO_NEXT):
        u[f, pl.ds(EDGE * PADY + LOW + layer, OWN, stride=PADY), :] = next_in[number]
    interior_strips(1, EDGE + 1, EDGE + OWN, 1)
    interior_strips(2, EDGE + 1, EDGE + OWN - 1, 0)
    interior_strips(3, EDGE + 2, EDGE + OWN - 1, 1)
    interior_strips(4, EDGE + 2, EDGE + OWN - 2, 0)
    sums = lax.fori_loop(
        0,
        3,
        lambda i, sums: strip_products([(4 + 4 * i, 5 + 4 * i), (6 + 4 * i, 7 + 4 * i)], sums),
        none,
    )

    for copy in copies[4:]:
        copy.wait_recv()
    for number, (side_x, side_y) in enumerate(corners):
        for f in range(FIELDS):
            for layer in range(2):
                x = (EDGE + OWN if side_x == 0 else 0) + layer
                y = HIGH if side_y == 0 else LOW
                if side_x != side_y:
                    source = corner_in[number, pl.ds(f * 4 + layer * 2, 2), :]
                    u[f, pl.ds(x * PADY + y, 2), :] = source
                elif layer == side_x:
                    u[f, pl.ds(x * PADY + y + layer, 1), :] = corner_in[number, pl.ds(f, 1), :]
    edge_strips(1, 1, EDGE + OWN, 1)
    edge_strips(2, 1, EDGE + OWN - 1, 0)
    edge_strips(3, EDGE, EDGE + OWN - 1, 1)
    edge_strips(4, EDGE, EDGE + OWN - 2, 0)
    keep(strip_products([(2, 3), (16, 17)], sums), place < 8, True)

    total = acc_rows[pl.ds(0, 16, stride=8), :]
    for s in range(1, 8):
        total = total + acc_rows[pl.ds(s, 16, stride=8), :]
    diagonal = lax.broadcasted_iota(jnp.int32, (16, 128), 0) == lax.broadcasted_iota(jnp.int32, (16, 128), 1)

    def to_row(column):
        return jnp.sum(jnp.where(diagonal, column, 0.0), axis=0, keepdims=True)

    def gather_metal():
        flags = [metal[tile_rows[1 + t // 2], tile_cols[1 + t % 2]] for t in range(4)]
        present = [flag.astype(jnp.float32) for flag in flags]
        before = jnp.float32(0.0)
        chosen = [[None] * 4 for _ in range(MS)]
        for t in range(4):
            taken = [present[t] * (1.0 - before), present[t] * before]
            before = before + present[t]
            for slot in range(MS):
                chosen[slot][t] = taken[slot]

        def rows(x, carry):
            for c in range(3):
                for j in range(STEPS):
                    parts = []
                    for t in range(4):
                        at = 8 * (t // 2) + x
                        y = 8 * (t % 2)
                        if j == 0:
                            parts.append(raw[c, pl.ds(pl.multiple_of(at * OWN + y, 8), 8), :])
                        else:
                            parts.append(own_out[j - 1, c, at, pl.ds(y, 8), :])
                    for slot in range(MS):
                        value = chosen[slot][0] * parts[0]
                        for t in range(1, 4):
                            value = value + chosen[slot][t] * parts[t]
                        tiles_out[slot, j, c, x] = value
            return carry

        lax.fori_loop(0, 8, rows, 0)
        for p in range(POLES):
            kicks = [strength[p]]
            kicks.append(-gamma[p] * kicks[0])
            for k in range(2, STEPS):
                kicks.append(-(omega[p] * omega[p]) * kicks[k - 2] - gamma[p] * kicks[k - 1])
            for k in range(STEPS):
                kicks_out[pl.ds(p * STEPS + k, 1), :] = jnp.full((1, 128), kicks[k])

    def order_own():
        def rows(x, carry):
            for j, state in enumerate(states[1:]):
                for c in range(6):
                    tile = [state[c, x + EDGE, pl.ds(8 * t, 8), :] for t in range(3)]
                    own_out[j, c, x, pl.ds(0, 8), :] = jnp.where(
                        place < 2, pltpu.roll(tile[2], 2, 0), pltpu.roll(tile[0], 2, 0)
                    )
                    own_out[j, c, x, pl.ds(8, 8), :] = jnp.where(
                        place < 6, pltpu.roll(tile[1], 6, 0), pltpu.roll(tile[2], 6, 0)
                    )
            return carry

        lax.fori_loop(0, OWN, rows, 0)

    row = to_row(jnp.sum(total, axis=1, keepdims=True))
    if far:
        pl.semaphore_wait(heard.at[1], len(far))
    me_a = my_core * z_size + my_z
    me_b = my_x * y_size + my_y
    targets_a = [
        device(my_x, ring_core[c], my_y, ring_z[z]) for c, z in farthest_first(cores, z_size)
    ]
    targets_b = [
        device(ring_x[x], my_core, ring_y[y], my_z) for x, y in farthest_first(x_size, y_size)
    ]
    for stage, (slots, me, targets) in enumerate(((sum_a, me_a, targets_a), (sum_b, me_b, targets_b))):
        slots[me] = row
        for target in targets:
            pltpu.make_async_remote_copy(
                src_ref=slots.at[me],
                dst_ref=slots.at[me],
                send_sem=stage_send.at[stage],
                recv_sem=stage_recv.at[stage],
                device_id=target,
                device_id_type=MESH,
            ).start()
        if stage == 0:
            order_own()
        else:
            gather_metal()
        settle(slots.at[pl.ds(0, len(targets))], stage_recv.at[stage])
        row = slots[0]
        for member in range(1, len(targets) + 1):
            row = row + slots[member]
    gram_out[...] = jnp.broadcast_to(
        jnp.sum(jnp.where(diagonal, row, 0.0), axis=1, keepdims=True), (16, 128)
    )

    for copy in copies:
        copy.wait_send()
    for stage, (slots, targets) in enumerate(((sum_a, targets_a), (sum_b, targets_b))):
        settle(slots.at[pl.ds(0, len(targets))], stage_send.at[stage])


def finish_kernel(
    cell_count,
    k0,
    own,
    gram,
    tiles,
    kicks,
    out_e,
    out_h,
    out_poles,
    out_coefficients,
    coefficients,
    table,
    fields,
    poles,
    pole_sem,
    store_sem,
):
    stores = []

    def store(src, dst):
        copy = pltpu.make_async_copy(src, dst, store_sem.at[len(stores)])
        copy.start()
        stores.append(copy)

    inner = {}
    for number, (i, j) in enumerate(PAIRS):
        inner[i, j] = inner[j, i] = gram[pl.ds(number, 1), :] * (1.0 / cell_count)
    unit = 1.0 / jnp.sqrt(inner[0, 0] + EPSILON)
    weights = [unit]
    lane = lax.broadcasted_iota(jnp.int32, (1, 128), 1)
    for step in range(1, STEPS + 1):
        image = [None] + weights

        def total(terms):
            return functools.reduce(jnp.add, terms)

        along_q = unit * total([image[j] * inner[0, j] for j in range(1, step + 1)])
        rest = [-along_q * unit] + image[1:]
        along_v = jnp.zeros_like(unit)
        if step > 1:
            along_v = total(
                [
                    image[j] * total([weights[i] * inner[i, j] for i in range(step)])
                    for j in range(1, step + 1)
                ]
            )
            for i in range(step):
                rest[i] = rest[i] - along_v * weights[i]
        squared = total(
            [rest[i] * total([rest[j] * inner[i, j] for j in range(step + 1)]) for i in range(step + 1)]
        )
        norm = jnp.sqrt(jnp.maximum(squared, 0.0) + EPSILON)
        scale = 1.0 / norm
        weights = [part * scale for part in rest]
        line = jnp.where(lane == 0, along_q, jnp.where(lane == 1, along_v, norm))
        coefficients[pl.ds(step - 1, 1), :] = line[:, :3]

    store(coefficients, out_coefficients)

    for p in range(POLES):
        kick = [kicks[pl.ds(p * STEPS + k, 1), :] for k in range(STEPS)]
        for j in range(STEPS):
            parts = [weights[k] * kick[k - 1 - j] for k in range(j + 1, STEPS + 1)]
            table[pl.ds(p * 8 + j, 1), :] = functools.reduce(jnp.add, parts)
        for j in range(STEPS - 1):
            parts = [weights[k] * kick[k - 2 - j] for k in range(j + 2, STEPS + 1)]
            table[pl.ds(p * 8 + 4 + j, 1), :] = functools.reduce(jnp.add, parts)
    for j in range(STEPS + 1):
        table[pl.ds(48 + j, 1), :] = weights[j]

    def entry(number):
        return jnp.broadcast_to(table[pl.ds(number, 1), :], (8, 128))

    def pole_part(i):
        return (i // 3, pl.ds(0, 2), pl.ds(0, POLES), i % 3)

    def pole_cells(i, carry):
        slot, c = i // 3, i % 3
        for x in range(8):
            field = [tiles[slot, j, c, x] for j in range(STEPS)]
            for p in range(POLES):
                poles[slot, 1, p, c, x] = functools.reduce(
                    jnp.add, [entry(p * 8 + j) * field[j] for j in range(STEPS)]
                )
                poles[slot, 0, p, c, x] = functools.reduce(
                    jnp.add, [entry(p * 8 + 4 + j) * field[j] for j in range(STEPS - 1)]
                )
        pltpu.make_async_copy(
            poles.at[pole_part(i)], out_poles.at[pole_part(i)], pole_sem.at[i]
        ).start()
        return carry

    lax.fori_loop(0, 3 * MS, pole_cells, 0)

    for half, out in enumerate((out_e, out_h)):

        def field_cells(i, carry):
            for x in [4 * i + k for k in range(4)]:
                for c in range(3 * half, 3 * half + 3):
                    cells = pl.ds(pl.multiple_of(x * OWN, 8), OWN)
                    value = table[pl.ds(48, 1), :] * k0[c, cells, :]
                    for j in range(STEPS):
                        value = value + table[pl.ds(49 + j, 1), :] * own[j, c, x]
                    fields[c, x] = value
            return carry

        lax.fori_loop(0, OWN // 4, field_cells, 0)
        store(fields.at[pl.ds(3 * half, 3)], out)
    for i in range(3 * MS):
        pltpu.make_async_copy(poles.at[pole_part(i)], out_poles.at[pole_part(i)], pole_sem.at[i]).wait()
    for copy in stores:
        copy.wait()


def body(sizes, u_electric, u_magnetic, eps_inv, metal_map, pole_omega, pole_gamma, pole_strength):
    depth = u_electric.shape[3]
    cell_count = 6.0 * OWN * OWN * depth * sizes[0] * sizes[1] * sizes[2] * sizes[3]
    f32 = jnp.float32
    any_spec = pl.BlockSpec(memory_space=pl.ANY)
    hbm = pl.BlockSpec(memory_space=pltpu.HBM)
    vmem = pl.BlockSpec(memory_space=pltpu.VMEM)
    a_size = sizes[1] * sizes[3]
    b_size = sizes[0] * sizes[2]

    def stay(value):
        return pltpu.with_memory_space_constraint(value, pltpu.HBM)

    start = [u_electric.reshape(3, OWN * OWN, depth), u_magnetic.reshape(3, OWN * OWN, depth)]
    model = [stay(part) for part in (metal_map, pole_omega, pole_gamma, pole_strength)]
    dma = pltpu.SemaphoreType.DMA
    results = pl.pallas_call(
        functools.partial(exchange_kernel, sizes, metal_map.shape),
        out_shape=[
            jax.ShapeDtypeStruct((STEPS, 6, OWN, OWN, depth), f32),
            jax.ShapeDtypeStruct((16, depth), f32),
            jax.ShapeDtypeStruct((MS, STEPS, 3, 8, 8, depth), f32),
            jax.ShapeDtypeStruct((POLES * STEPS, depth), f32),
            jax.ShapeDtypeStruct((FIELDS, OWN * OWN, depth), f32),
        ],
        in_specs=[hbm] * 7,
        out_specs=[vmem] * 5,
        scratch_shapes=[
            pltpu.VMEM((2, FIELDS, EDGE * OWN, depth), f32),
            *[pltpu.VMEM((6, PADX, PADY, depth), f32)] * STEPS,
            pltpu.VMEM((FIELDS, ROW, depth), f32),
            pltpu.VMEM((len(TO_PREVIOUS), OWN, depth), f32),
            pltpu.VMEM((len(TO_PREVIOUS), OWN, depth), f32),
            pltpu.VMEM((len(TO_NEXT), OWN, depth), f32),
            pltpu.VMEM((len(TO_NEXT), OWN, depth), f32),
            pltpu.VMEM((4, CORNER_ROWS, depth), f32),
            pltpu.VMEM((4, CORNER_ROWS, depth), f32),
            pltpu.VMEM((4, PADY, depth), f32),
            pltpu.VMEM((128, depth), f32),
            pltpu.VMEM((a_size, 1, depth), f32),
            pltpu.VMEM((b_size, 1, depth), f32),
            pltpu.SMEM(metal_map.shape, jnp.int32),
            pltpu.SMEM((POLES,), f32),
            pltpu.SMEM((POLES,), f32),
            pltpu.SMEM((POLES,), f32),
            pltpu.SemaphoreType.REGULAR((2,)),
            dma((7,)),
            dma((8,)),
            dma((8,)),
            dma((2,)),
            dma((2,)),
        ],
        compiler_params=pltpu.CompilerParams(
            collective_id=0, has_side_effects=True, vmem_limit_bytes=VMEM_LIMIT
        ),
    )(*[stay(part) for part in start], stay(eps_inv.reshape(OWN * OWN, depth)), *model)

    own, gram, tiles, kicks, raw = results

    return pl.pallas_call(
        functools.partial(finish_kernel, cell_count),
        out_shape=[
            jax.ShapeDtypeStruct(u_electric.shape, f32),
            jax.ShapeDtypeStruct(u_magnetic.shape, f32),
            jax.ShapeDtypeStruct((MS, 2, POLES, 3, 8, 8, depth), f32),
            jax.ShapeDtypeStruct((STEPS, 3), f32),
        ],
        in_specs=[vmem] * 5,
        out_specs=[any_spec] * 4,
        scratch_shapes=[
            pltpu.VMEM((STEPS, 3), f32),
            pltpu.VMEM((56, depth), f32),
            pltpu.VMEM((6, OWN, OWN, depth), f32),
            pltpu.VMEM((MS, 2, POLES, 3, 8, 8, depth), f32),
            dma((3 * MS,)),
            dma((3,)),
        ],
        compiler_params=pltpu.CompilerParams(vmem_limit_bytes=VMEM_LIMIT),
    )(raw, own, gram, tiles, kicks)


def solution(mesh):
    sizes = layout(mesh.shape["gx"], mesh.shape["gy"])
    placed = (
        P(None, "gx", "gy", None),
        P(None, "gx", "gy", None),
        P("gx", "gy", None),
        P(),
        P(),
        P(),
        P(),
    )
    return jax.shard_map(
        functools.partial(body, sizes),
        mesh=mesh,
        in_specs=placed,
        out_specs=(
            P(None, "gx", "gy", None),
            P(None, "gx", "gy", None),
            P(("gx", "gy"), None, None, None, None, None, None),
            P(),
        ),
        check_vma=False,
    )
```

```python
import functools

import jax
import jax.numpy as jnp
from jax import lax
from jax.experimental import pallas as pl
from jax.experimental.pallas import tpu as pltpu
from jax.sharding import PartitionSpec as P

POLES = 6
STEPS = 4
MS = 2
EPSILON = 1e-06
MESH = pl.DeviceIdType.MESH

EDGE = 2
OWN = 16
PADX = OWN + 2 * EDGE
PADY = 24
HIGH = 18
LOW = 20
STRIP = 16
FIELDS = 7
TO_PREVIOUS = [(f, 0) for f in range(FIELDS)] + [(f, 1) for f in (0, 2, 3, 4, 5, 6)]
TO_NEXT = [(f, 1) for f in range(FIELDS)] + [(f, 0) for f in (0, 1, 2, 3, 5)]
ROW = PADX * PADY
CORNER_ROWS = 32
CHUNK = 5
PAIRS = [(i, j) for i in range(STEPS + 1) for j in range(i, STEPS + 1)]
VMEM_LIMIT = 40 * 1024 * 1024


def layout(gx_size, gy_size):
    cores = 2
    z_size = min(8, gy_size // 2)
    return gx_size // cores, cores, gy_size // z_size, z_size


def rings(sizes):
    result = []
    for axis, size in (("x", sizes[0]), ("y", sizes[2]), ("z", sizes[3])):
        near = sorted({1 % size, size - 1} - {0})
        far = sorted({2 % size, (size - 2) % size} - {0}) if size > 3 else []
        result.append((axis, size, near, far))
    return result


def farthest_first(first, second):
    def hops(step, size):
        return min(step, size - step)

    steps = [(a, b) for a in range(first) for b in range(second) if a or b]
    return sorted(steps, key=lambda step: -hops(step[0], first) - hops(step[1], second))


def next_y(value):
    return pltpu.roll(value, PADY - 1, 0)


def prev_y(value):
    return pltpu.roll(value, 1, 0)


def next_z(value):
    return pltpu.roll(value, value.shape[1] - 1, 1)


def prev_z(value):
    return pltpu.roll(value, 1, 1)


def settle(buffer, semaphore):
    pltpu.make_async_copy(buffer, buffer, semaphore).wait()


def exchange_kernel(
    sizes,
    tiles,
    u_e,
    u_h,
    eps_in,
    metal_in,
    omega_in,
    gamma_in,
    strength_in,
    own_out,
    gram_out,
    tiles_out,
    kicks_out,
    raw,
    face_in,
    k1,
    k2,
    k3,
    k4,
    u,
    previous_out,
    previous_in,
    next_out,
    next_in,
    corner_out,
    corner_in,
    mask,
    acc_rows,
    sum_a,
    sum_b,
    metal,
    omega,
    gamma,
    strength,
    heard,
    load_sem,
    face_send,
    face_recv,
    stage_send,
    stage_recv,
):
    x_size, cores, y_size, z_size = sizes
    gx_size, gy_size = x_size * cores, y_size * z_size
    gx = lax.axis_index("gx")
    gy = lax.axis_index("gy")

    loads = [
        pltpu.make_async_copy(u_e, raw.at[pl.ds(0, 3)], load_sem.at[0]),
        pltpu.make_async_copy(u_h, raw.at[pl.ds(3, 3)], load_sem.at[1]),
        pltpu.make_async_copy(eps_in, raw.at[6], load_sem.at[2]),
        pltpu.make_async_copy(metal_in, metal, load_sem.at[3]),
        pltpu.make_async_copy(omega_in, omega, load_sem.at[4]),
        pltpu.make_async_copy(gamma_in, gamma, load_sem.at[5]),
        pltpu.make_async_copy(strength_in, strength, load_sem.at[6]),
    ]
    for load in loads:
        load.start()

    def ring(position, size):
        return [position] + [lax.rem(position + step, size) for step in range(1, size)]

    def device(x, core, y, z):
        return (x * cores + core, y * z_size + z)

    around_x = {0: gx, -1: lax.rem(gx + gx_size - 1, gx_size), 1: lax.rem(gx + 1, gx_size)}
    around_y = {0: gy, -1: lax.rem(gy + gy_size - 1, gy_size), 1: lax.rem(gy + 1, gy_size)}

    def neighbour(dx, dy):
        return (around_x[dx], around_y[dy])

    my_x, my_core = lax.div(gx, cores), lax.rem(gx, cores)
    my_y, my_z = lax.div(gy, z_size), lax.rem(gy, z_size)
    ring_x, ring_core = ring(my_x, x_size), ring(my_core, cores)
    ring_y, ring_z = ring(my_y, y_size), ring(my_z, z_size)

    def along(axis, step, core=0):
        return device(
            ring_x[step if axis == "x" else 0],
            ring_core[core],
            ring_y[step if axis == "y" else 0],
            ring_z[step if axis == "z" else 0],
        )

    def signal(semaphore, target):
        pl.semaphore_signal(semaphore, inc=1, device_id=target, device_id_type=MESH)

    beside = [(0, -1), (0, 1), (-1, 0), (1, 0)]
    near = [(axis, step, 0) for axis, _, steps, _ in rings(sizes) for step in steps]
    near += [(axis, step, 1) for axis, step, _ in near if axis == "z"]
    far = [(axis, step) for axis, _, _, steps in rings(sizes) for step in steps]
    barrier = pltpu.get_barrier_semaphore()
    for dx, dy in beside:
        signal(barrier, neighbour(dx, dy))
    for place in near:
        signal(barrier, along(*place))

    for load in loads:
        load.wait()

    for number, (f, layer) in enumerate(TO_PREVIOUS):
        previous_out[number] = raw[f, pl.ds(layer, OWN, stride=OWN), :]
    for number, (f, layer) in enumerate(TO_NEXT):
        next_out[number] = raw[f, pl.ds(OWN - 2 + layer, OWN, stride=OWN), :]
    corners = [(0, 0), (0, 1), (1, 0), (1, 1)]
    for number, (side_x, side_y) in enumerate(corners):
        for f in range(FIELDS):
            for layer in range(2):
                if side_x != side_y:
                    x = (0 if side_x == 0 else OWN - 2) + layer
                    y = 0 if side_y == 0 else OWN - 2
                    cells = raw[f, pl.ds(x * OWN + y, 2), :]
                    corner_out[number, pl.ds(f * 4 + layer * 2, 2), :] = cells
                elif layer == 0:
                    cell = 0 if side_x == 0 else OWN * OWN - 1
                    corner_out[number, pl.ds(f, 1), :] = raw[f, pl.ds(cell, 1), :]

    pl.semaphore_wait(barrier, len(beside) + len(near))

    copies = []

    def send(src, dst, device):
        number = len(copies)
        copy = pltpu.make_async_remote_copy(
            src_ref=src,
            dst_ref=dst,
            send_sem=face_send.at[number],
            recv_sem=face_recv.at[number],
            device_id=device,
            device_id_type=MESH,
        )
        copy.start()
        copies.append(copy)

    send(previous_out, previous_in, neighbour(0, -1))
    send(next_out, next_in, neighbour(0, 1))
    everything = pl.ds(0, FIELDS)
    layers = EDGE * OWN
    send(raw.at[everything, pl.ds(0, layers)], face_in.at[0], neighbour(-1, 0))
    send(raw.at[everything, pl.ds(OWN * OWN - layers, layers)], face_in.at[1], neighbour(1, 0))
    for dx, dy in beside[2:]:
        signal(heard.at[0], neighbour(dx, dy))
    for place in near:
        signal(heard.at[0], along(*place))

    tile_rows = [lax.rem(2 * gx + s - 1 + tiles[0], tiles[0]) for s in range(4)]
    tile_cols = [lax.rem(2 * gy + t - 1 + tiles[1], tiles[1]) for t in range(4)]
    place = lax.broadcasted_iota(jnp.int32, (8, 128), 0)
    for s in range(4):
        flag = [
            jnp.full((8, 128), metal[tile_rows[s], tile_cols[t]].astype(jnp.float32)) for t in range(4)
        ]
        mask[s, 0:8] = jnp.where(place < 6, flag[1], flag[2])
        mask[s, 8:16] = jnp.where(place < 2, flag[1], flag[2])
        beyond = jnp.where(place < 4, flag[3], flag[0])
        mask[s, 16:24] = jnp.where(place < 2, flag[2], jnp.where(place < 6, beyond, flag[1]))

    response = [jnp.float32(0.0)] * 3
    for p in range(POLES):
        g0 = strength[p]
        g1 = -gamma[p] * g0
        g2 = -(omega[p] * omega[p]) * g0 - gamma[p] * g1
        response = [response[0] + g0, response[1] + g1, response[2] + g2]

    def put_row(f, x, low, high):
        first = pl.multiple_of(x * PADY, 8)
        low_by_6, low_by_2 = pltpu.roll(low, 6, 0), pltpu.roll(low, 2, 0)
        high_by_6, high_by_2 = pltpu.roll(high, 6, 0), pltpu.roll(high, 2, 0)
        u[f, pl.ds(first, 8), :] = jnp.where(place < 6, low_by_6, high_by_6)
        u[f, pl.ds(first + 8, 8), :] = jnp.where(place < 2, low_by_2, high_by_2)
        u[f, pl.ds(first + 16, 8), :] = jnp.where(place < 4, high_by_2, low_by_6)

    def copy_own(x, carry):
        first = pl.multiple_of(x * OWN, 8)
        for f in range(FIELDS):
            put_row(f, x + EDGE, raw[f, pl.ds(first, 8), :], raw[f, pl.ds(first + 8, 8), :])
        return carry

    lax.fori_loop(0, OWN, copy_own, 0)

    pl.semaphore_wait(heard.at[0], len(beside[2:]) + len(near))
    for axis, step in far:
        signal(heard.at[1], along(axis, step))
    for number, (side_x, side_y) in enumerate(corners):
        rows = pl.ds(0, 8 if side_x == side_y else CORNER_ROWS)
        send(
            corner_out.at[number, rows],
            corner_in.at[number, rows],
            neighbour(2 * side_x - 1, 2 * side_y - 1),
        )

    class Padded:
        def __getitem__(self, at):
            f, x = at
            return u[f, pl.ds(pl.multiple_of(x * PADY, 8), PADY), :]

    start = Padded()
    states = [start, k1, k2, k3, k4]

    def electric(step, x):
        old = states[step - 1]
        hx, hy, hz = old[3, x], old[4, x], old[5, x]
        hy_back, hz_back = old[4, x - 1], old[5, x - 1]
        curl = [
            (hz - prev_y(hz)) - (hy - prev_z(hy)),
            (hx - prev_z(hx)) - (hz - hz_back),
            (hy - hy_back) - (hx - prev_y(hx)),
        ]
        eps = start[6, x]
        if step > 1:
            metal_here = mask[(x + 6) // 8]
            for c in range(3):
                current = response[step - 2] * start[c, x]
                for j in range(1, step - 1):
                    current = current + response[step - 2 - j] * states[j][c, x]
                curl[c] = curl[c] - metal_here * current
        return [eps * part for part in curl]

    def magnetic(step, x):
        old = states[step - 1]
        ex, ey, ez = old[0, x], old[1, x], old[2, x]
        ey_next, ez_next = old[1, x + 1], old[2, x + 1]
        return [
            (next_z(ey) - ey) - (next_y(ez) - ez),
            (ez_next - ez) - (next_z(ex) - ex),
            (next_y(ex) - ex) - (ey_next - ey),
        ]

    def write_rows(step, starts, shift):
        new = states[step]
        parts = [(x, electric(step, x), magnetic(step, x - shift)) for x in starts]
        for x, of_e, of_h in parts:
            for c in range(3):
                new[c, x] = of_e[c]
                new[3 + c, x - shift] = of_h[c]

    def interior(step, low, high, shift):
        rest = high - low - CHUNK
        chunks = -(-rest // CHUNK) + 1

        def rows(i, carry):
            first = low + (i * rest) // (chunks - 1)
            write_rows(step, [first + k for k in range(CHUNK)], shift)
            return carry

        lax.fori_loop(0, chunks, rows, 0)

    def edges(step, low, high, shift):
        write_rows(step, [low, low + 1, high, high + 1], shift)

    def state_at(j, c, x, first, count):
        if j == 0:
            return u[c, pl.ds(x * PADY + first, count), :]
        return states[j][c, x, pl.ds(first, count), :]

    def strip(j, c, x):
        if j == 0:
            return u[c, pl.ds(pl.multiple_of(x * PADY + STRIP, 8), 8), :]
        return states[j][c, x, pl.ds(STRIP, 8), :]

    def strip_prev(j, c, x, value):
        return jnp.where(place == 0, state_at(j, c, x, STRIP - 1, 1), pltpu.roll(value, 1, 0))

    def strip_next(j, c, x, value):
        return jnp.where(place == 7, state_at(j, c, x, 0, 1), pltpu.roll(value, 7, 0))

    def strip_electric(step, x):
        old = step - 1
        hx, hy, hz = (strip(old, c, x) for c in (3, 4, 5))
        hy_back, hz_back = strip(old, 4, x - 1), strip(old, 5, x - 1)
        curl = [
            (hz - strip_prev(old, 5, x, hz)) - (hy - prev_z(hy)),
            (hx - prev_z(hx)) - (hz - hz_back),
            (hy - hy_back) - (hx - strip_prev(old, 3, x, hx)),
        ]
        if step > 1:
            metal_here = mask[(x + 6) // 8, pl.ds(STRIP, 8), :]
            for c in range(3):
                current = response[step - 2] * strip(0, c, x)
                for j in range(1, step - 1):
                    current = current + response[step - 2 - j] * strip(j, c, x)
                curl[c] = curl[c] - metal_here * current
        eps = strip(0, 6, x)
        return [eps * part for part in curl]

    def strip_magnetic(step, x):
        old = step - 1
        ex, ey, ez = (strip(old, c, x) for c in (0, 1, 2))
        ey_next, ez_next = strip(old, 1, x + 1), strip(old, 2, x + 1)
        return [
            (next_z(ey) - ey) - (strip_next(old, 2, x, ez) - ez),
            (ez_next - ez) - (next_z(ex) - ex),
            (strip_next(old, 0, x, ex) - ex) - (ey_next - ey),
        ]

    def write_strips(step, starts, shift):
        new = states[step]
        parts = [(x, strip_electric(step, x), strip_magnetic(step, x - shift)) for x in starts]
        for x, of_e, of_h in parts:
            for c in range(3):
                new[c, x, pl.ds(STRIP, 8), :] = of_e[c]
                new[3 + c, x - shift, pl.ds(STRIP, 8), :] = of_h[c]

    def interior_strips(step, low, high, shift):
        write_strips(step, list(range(low, high)), shift)

    def edge_strips(step, low, high, shift):
        write_strips(step, [low, low + 1, high, high + 1], shift)

    zero = jnp.zeros((8, 128), jnp.float32)

    def products(first, x, sums):
        sums = list(sums)
        cells = pl.ds(first, 8)
        for c in range(6):
            values = [u[c, pl.ds(pl.multiple_of(x * PADY + first, 8), 8), :]]
            values += [state[c, x, cells, :] for state in states[1:]]
            for number, (i, j) in enumerate(PAIRS):
                sums[number] = sums[number] + values[i] * values[j]
        return tuple(sums)

    ends = jnp.logical_or(place < 2, place >= 6)

    def strip_products(pairs, sums):
        sums = list(sums)
        for x, other in pairs:
            for c in range(6):
                values = [
                    jnp.where(ends, strip(j, c, x), pltpu.roll(strip(j, c, other), 4, 0))
                    for j in range(STEPS + 1)
                ]
                for number, (i, j) in enumerate(PAIRS):
                    sums[number] = sums[number] + values[i] * values[j]
        return tuple(sums)

    def interior_products(first, sums):
        return lax.fori_loop(
            EDGE + 2, EDGE + OWN - 2, lambda x, sums: products(first, x, sums), sums
        )

    def edge_products(first, sums):
        return lax.fori_loop(
            0,
            2 * EDGE,
            lambda i, sums: products(first, EDGE + i + i // 2 * (OWN - 4), sums),
            sums,
        )

    def keep(sums, wanted, into):
        for number, part in enumerate(sums):
            at = pl.ds(8 * number, 8)
            part = jnp.where(wanted, part, 0.0)
            acc_rows[at, :] = part + acc_rows[at, :] if into else part

    none = (zero,) * len(PAIRS)
    interior(1, EDGE + 1, EDGE + OWN, 1)
    interior(2, EDGE + 1, EDGE + OWN - 1, 0)
    interior(3, EDGE + 2, EDGE + OWN - 1, 1)
    interior(4, EDGE + 2, EDGE + OWN - 2, 0)
    keep(interior_products(0, none), place < 6, False)
    keep(interior_products(8, none), place >= 2, True)
    acc_rows[pl.ds(8 * len(PAIRS), 8), :] = zero

    for copy in copies[2:4]:
        copy.wait_recv()
    for f in range(FIELDS):
        for side, first in ((0, EDGE + OWN), (1, 0)):
            for layer in range(2):
                low = face_in[side, f, pl.ds(layer * OWN, 8), :]
                high = face_in[side, f, pl.ds(layer * OWN + 8, 8), :]
                put_row(f, first + layer, low, high)
    edges(1, 1, EDGE + OWN, 1)
    edges(2, 1, EDGE + OWN - 1, 0)
    edges(3, EDGE, EDGE + OWN - 1, 1)
    edges(4, EDGE, EDGE + OWN - 2, 0)
    keep(edge_products(0, none), place < 6, True)
    keep(edge_products(8, none), place >= 2, True)

    for copy in copies[:2]:
        copy.wait_recv()
    for number, (f, layer) in enumerate(TO_PREVIOUS):
        u[f, pl.ds(EDGE * PADY + HIGH + layer, OWN, stride=PADY), :] = previous_in[number]
    for number, (f, layer) in enumerate(TO_NEXT):
        u[f, pl.ds(EDGE * PADY + LOW + layer, OWN, stride=PADY), :] = next_in[number]
    interior_strips(1, EDGE + 1, EDGE + OWN, 1)
    interior_strips(2, EDGE + 1, EDGE + OWN - 1, 0)
    interior_strips(3, EDGE + 2, EDGE + OWN - 1, 1)
    interior_strips(4, EDGE + 2, EDGE + OWN - 2, 0)

    for copy in copies[4:]:
        copy.wait_recv()
    for number, (side_x, side_y) in enumerate(corners):
        for f in range(FIELDS):
            for layer in range(2):
                x = (EDGE + OWN if side_x == 0 else 0) + layer
                y = HIGH if side_y == 0 else LOW
                if side_x != side_y:
                    source = corner_in[number, pl.ds(f * 4 + layer * 2, 2), :]
                    u[f, pl.ds(x * PADY + y, 2), :] = source
                elif layer == side_x:
                    u[f, pl.ds(x * PADY + y + layer, 1), :] = corner_in[number, pl.ds(f, 1), :]
    edge_strips(1, 1, EDGE + OWN, 1)
    edge_strips(2, 1, EDGE + OWN - 1, 0)
    edge_strips(3, EDGE, EDGE + OWN - 1, 1)
    edge_strips(4, EDGE, EDGE + OWN - 2, 0)
    sums = strip_products([(x, x + 1) for x in range(EDGE + 2, EDGE + OWN - 2, 2)], none)
    keep(strip_products([(2, 3), (16, 17)], sums), place < 8, True)

    total = acc_rows[pl.ds(0, 16, stride=8), :]
    for s in range(1, 8):
        total = total + acc_rows[pl.ds(s, 16, stride=8), :]
    diagonal = lax.broadcasted_iota(jnp.int32, (16, 128), 0) == lax.broadcasted_iota(jnp.int32, (16, 128), 1)

    def to_row(column):
        return jnp.sum(jnp.where(diagonal, column, 0.0), axis=0, keepdims=True)

    def gather_metal():
        flags = [metal[tile_rows[1 + t // 2], tile_cols[1 + t % 2]] for t in range(4)]
        present = [flag.astype(jnp.float32) for flag in flags]
        before = jnp.float32(0.0)
        chosen = [[None] * 4 for _ in range(MS)]
        for t in range(4):
            taken = [present[t] * (1.0 - before), present[t] * before]
            before = before + present[t]
            for slot in range(MS):
                chosen[slot][t] = taken[slot]

        def rows(x, carry):
            for c in range(3):
                for j in range(STEPS):
                    parts = []
                    for t in range(4):
                        at = 8 * (t // 2) + x
                        y = 8 * (t % 2)
                        if j == 0:
                            parts.append(raw[c, pl.ds(pl.multiple_of(at * OWN + y, 8), 8), :])
                        else:
                            parts.append(own_out[j - 1, c, at, pl.ds(y, 8), :])
                    for slot in range(MS):
                        value = chosen[slot][0] * parts[0]
                        for t in range(1, 4):
                            value = value + chosen[slot][t] * parts[t]
                        tiles_out[slot, j, c, x] = value
            return carry

        lax.fori_loop(0, 8, rows, 0)
        for p in range(POLES):
            kicks = [strength[p]]
            kicks.append(-gamma[p] * kicks[0])
            for k in range(2, STEPS):
                kicks.append(-(omega[p] * omega[p]) * kicks[k - 2] - gamma[p] * kicks[k - 1])
            for k in range(STEPS):
                kicks_out[pl.ds(p * STEPS + k, 1), :] = jnp.full((1, 128), kicks[k])

    def order_own():
        def rows(x, carry):
            for j, state in enumerate(states[1:]):
                for c in range(6):
                    tile = [state[c, x + EDGE, pl.ds(8 * t, 8), :] for t in range(3)]
                    own_out[j, c, x, pl.ds(0, 8), :] = jnp.where(
                        place < 2, pltpu.roll(tile[2], 2, 0), pltpu.roll(tile[0], 2, 0)
                    )
                    own_out[j, c, x, pl.ds(8, 8), :] = jnp.where(
                        place < 6, pltpu.roll(tile[1], 6, 0), pltpu.roll(tile[2], 6, 0)
                    )
            return carry

        lax.fori_loop(0, OWN, rows, 0)

    row = to_row(jnp.sum(total, axis=1, keepdims=True))
    if far:
        pl.semaphore_wait(heard.at[1], len(far))
    me_a = my_core * z_size + my_z
    me_b = my_x * y_size + my_y
    targets_a = [
        device(my_x, ring_core[c], my_y, ring_z[z]) for c, z in farthest_first(cores, z_size)
    ]
    targets_b = [
        device(ring_x[x], my_core, ring_y[y], my_z) for x, y in farthest_first(x_size, y_size)
    ]
    for stage, (slots, me, targets) in enumerate(((sum_a, me_a, targets_a), (sum_b, me_b, targets_b))):
        slots[me] = row
        for target in targets:
            pltpu.make_async_remote_copy(
                src_ref=slots.at[me],
                dst_ref=slots.at[me],
                send_sem=stage_send.at[stage],
                recv_sem=stage_recv.at[stage],
                device_id=target,
                device_id_type=MESH,
            ).start()
        if stage == 0:
            order_own()
        else:
            gather_metal()
        settle(slots.at[pl.ds(0, len(targets))], stage_recv.at[stage])
        row = slots[0]
        for member in range(1, len(targets) + 1):
            row = row + slots[member]
    gram_out[...] = jnp.broadcast_to(
        jnp.sum(jnp.where(diagonal, row, 0.0), axis=1, keepdims=True), (16, 128)
    )

    for copy in copies:
        copy.wait_send()
    for stage, (slots, targets) in enumerate(((sum_a, targets_a), (sum_b, targets_b))):
        settle(slots.at[pl.ds(0, len(targets))], stage_send.at[stage])


def finish_kernel(
    cell_count,
    k0,
    own,
    gram,
    tiles,
    kicks,
    out_e,
    out_h,
    out_poles,
    out_coefficients,
    coefficients,
    table,
    fields,
    poles,
    pole_sem,
    store_sem,
):
    stores = []

    def store(src, dst):
        copy = pltpu.make_async_copy(src, dst, store_sem.at[len(stores)])
        copy.start()
        stores.append(copy)

    inner = {}
    for number, (i, j) in enumerate(PAIRS):
        inner[i, j] = inner[j, i] = gram[pl.ds(number, 1), :] * (1.0 / cell_count)
    unit = 1.0 / jnp.sqrt(inner[0, 0] + EPSILON)
    weights = [unit]
    lane = lax.broadcasted_iota(jnp.int32, (1, 128), 1)
    for step in range(1, STEPS + 1):
        image = [None] + weights

        def total(terms):
            return functools.reduce(jnp.add, terms)

        along_q = unit * total([image[j] * inner[0, j] for j in range(1, step + 1)])
        rest = [-along_q * unit] + image[1:]
        along_v = jnp.zeros_like(unit)
        if step > 1:
            along_v = total(
                [
                    image[j] * total([weights[i] * inner[i, j] for i in range(step)])
                    for j in range(1, step + 1)
                ]
            )
            for i in range(step):
                rest[i] = rest[i] - along_v * weights[i]
        squared = total(
            [rest[i] * total([rest[j] * inner[i, j] for j in range(step + 1)]) for i in range(step + 1)]
        )
        norm = jnp.sqrt(jnp.maximum(squared, 0.0) + EPSILON)
        scale = 1.0 / norm
        weights = [part * scale for part in rest]
        line = jnp.where(lane == 0, along_q, jnp.where(lane == 1, along_v, norm))
        coefficients[pl.ds(step - 1, 1), :] = line[:, :3]

    store(coefficients, out_coefficients)

    for p in range(POLES):
        kick = [kicks[pl.ds(p * STEPS + k, 1), :] for k in range(STEPS)]
        for j in range(STEPS):
            parts = [weights[k] * kick[k - 1 - j] for k in range(j + 1, STEPS + 1)]
            table[pl.ds(p * 8 + j, 1), :] = functools.reduce(jnp.add, parts)
        for j in range(STEPS - 1):
            parts = [weights[k] * kick[k - 2 - j] for k in range(j + 2, STEPS + 1)]
            table[pl.ds(p * 8 + 4 + j, 1), :] = functools.reduce(jnp.add, parts)
    for j in range(STEPS + 1):
        table[pl.ds(48 + j, 1), :] = weights[j]

    def entry(number):
        return jnp.broadcast_to(table[pl.ds(number, 1), :], (8, 128))

    def pole_part(i):
        return (i // 3, pl.ds(0, 2), pl.ds(0, POLES), i % 3)

    def pole_cells(i, carry):
        slot, c = i // 3, i % 3
        field = [[tiles[slot, j, c, x] for j in range(STEPS)] for x in range(8)]
        for p in range(POLES):
            for_j = [entry(p * 8 + j) for j in range(STEPS)]
            for_p = [entry(p * 8 + 4 + j) for j in range(STEPS - 1)]
            for x in range(8):
                poles[slot, 1, p, c, x] = functools.reduce(
                    jnp.add, [weight * part for weight, part in zip(for_j, field[x])]
                )
                poles[slot, 0, p, c, x] = functools.reduce(
                    jnp.add, [weight * part for weight, part in zip(for_p, field[x])]
                )
        pltpu.make_async_copy(
            poles.at[pole_part(i)], out_poles.at[pole_part(i)], pole_sem.at[i]
        ).start()
        return carry

    lax.fori_loop(0, 3 * MS, pole_cells, 0)

    for half, out in enumerate((out_e, out_h)):

        def field_cells(i, carry):
            for x in [4 * i + k for k in range(4)]:
                for c in range(3 * half, 3 * half + 3):
                    cells = pl.ds(pl.multiple_of(x * OWN, 8), OWN)
                    value = table[pl.ds(48, 1), :] * k0[c, cells, :]
                    for j in range(STEPS):
                        value = value + table[pl.ds(49 + j, 1), :] * own[j, c, x]
                    fields[c, x] = value
            return carry

        lax.fori_loop(0, OWN // 4, field_cells, 0)
        store(fields.at[pl.ds(3 * half, 3)], out)
    for i in range(3 * MS):
        pltpu.make_async_copy(poles.at[pole_part(i)], out_poles.at[pole_part(i)], pole_sem.at[i]).wait()
    for copy in stores:
        copy.wait()


def body(sizes, u_electric, u_magnetic, eps_inv, metal_map, pole_omega, pole_gamma, pole_strength):
    depth = u_electric.shape[3]
    cell_count = 6.0 * OWN * OWN * depth * sizes[0] * sizes[1] * sizes[2] * sizes[3]
    f32 = jnp.float32
    any_spec = pl.BlockSpec(memory_space=pl.ANY)
    hbm = pl.BlockSpec(memory_space=pltpu.HBM)
    vmem = pl.BlockSpec(memory_space=pltpu.VMEM)
    a_size = sizes[1] * sizes[3]
    b_size = sizes[0] * sizes[2]

    def stay(value):
        return pltpu.with_memory_space_constraint(value, pltpu.HBM)

    start = [u_electric.reshape(3, OWN * OWN, depth), u_magnetic.reshape(3, OWN * OWN, depth)]
    model = [stay(part) for part in (metal_map, pole_omega, pole_gamma, pole_strength)]
    dma = pltpu.SemaphoreType.DMA
    results = pl.pallas_call(
        functools.partial(exchange_kernel, sizes, metal_map.shape),
        out_shape=[
            jax.ShapeDtypeStruct((STEPS, 6, OWN, OWN, depth), f32),
            jax.ShapeDtypeStruct((16, depth), f32),
            jax.ShapeDtypeStruct((MS, STEPS, 3, 8, 8, depth), f32),
            jax.ShapeDtypeStruct((POLES * STEPS, depth), f32),
            jax.ShapeDtypeStruct((FIELDS, OWN * OWN, depth), f32),
        ],
        in_specs=[hbm] * 7,
        out_specs=[vmem] * 5,
        scratch_shapes=[
            pltpu.VMEM((2, FIELDS, EDGE * OWN, depth), f32),
            *[pltpu.VMEM((6, PADX, PADY, depth), f32)] * STEPS,
            pltpu.VMEM((FIELDS, ROW, depth), f32),
            pltpu.VMEM((len(TO_PREVIOUS), OWN, depth), f32),
            pltpu.VMEM((len(TO_PREVIOUS), OWN, depth), f32),
            pltpu.VMEM((len(TO_NEXT), OWN, depth), f32),
            pltpu.VMEM((len(TO_NEXT), OWN, depth), f32),
            pltpu.VMEM((4, CORNER_ROWS, depth), f32),
            pltpu.VMEM((4, CORNER_ROWS, depth), f32),
            pltpu.VMEM((4, PADY, depth), f32),
            pltpu.VMEM((128, depth), f32),
            pltpu.VMEM((a_size, 1, depth), f32),
            pltpu.VMEM((b_size, 1, depth), f32),
            pltpu.SMEM(metal_map.shape, jnp.int32),
            pltpu.SMEM((POLES,), f32),
            pltpu.SMEM((POLES,), f32),
            pltpu.SMEM((POLES,), f32),
            pltpu.SemaphoreType.REGULAR((2,)),
            dma((7,)),
            dma((8,)),
            dma((8,)),
            dma((2,)),
            dma((2,)),
        ],
        compiler_params=pltpu.CompilerParams(
            collective_id=0, has_side_effects=True, vmem_limit_bytes=VMEM_LIMIT
        ),
    )(*[stay(part) for part in start], stay(eps_inv.reshape(OWN * OWN, depth)), *model)

    own, gram, tiles, kicks, raw = results

    return pl.pallas_call(
        functools.partial(finish_kernel, cell_count),
        out_shape=[
            jax.ShapeDtypeStruct(u_electric.shape, f32),
            jax.ShapeDtypeStruct(u_magnetic.shape, f32),
            jax.ShapeDtypeStruct((MS, 2, POLES, 3, 8, 8, depth), f32),
            jax.ShapeDtypeStruct((STEPS, 3), f32),
        ],
        in_specs=[vmem] * 5,
        out_specs=[any_spec] * 4,
        scratch_shapes=[
            pltpu.VMEM((STEPS, 3), f32),
            pltpu.VMEM((56, depth), f32),
            pltpu.VMEM((6, OWN, OWN, depth), f32),
            pltpu.VMEM((MS, 2, POLES, 3, 8, 8, depth), f32),
            dma((3 * MS,)),
            dma((3,)),
        ],
        compiler_params=pltpu.CompilerParams(vmem_limit_bytes=VMEM_LIMIT),
    )(raw, own, gram, tiles, kicks)


def solution(mesh):
    sizes = layout(mesh.shape["gx"], mesh.shape["gy"])
    placed = (
        P(None, "gx", "gy", None),
        P(None, "gx", "gy", None),
        P("gx", "gy", None),
        P(),
        P(),
        P(),
        P(),
    )
    return jax.shard_map(
        functools.partial(body, sizes),
        mesh=mesh,
        in_specs=placed,
        out_specs=(
            P(None, "gx", "gy", None),
            P(None, "gx", "gy", None),
            P(("gx", "gy"), None, None, None, None, None, None),
            P(),
        ),
        check_vma=False,
    )
```

```python
import functools

import jax
import jax.numpy as jnp
from jax import lax
from jax.experimental import pallas as pl
from jax.experimental.pallas import tpu as pltpu
from jax.sharding import PartitionSpec as P

POLES = 6
STEPS = 4
MS = 2
EPSILON = 1e-06
MESH = pl.DeviceIdType.MESH

EDGE = 2
OWN = 16
PADX = OWN + 2 * EDGE
PADY = 24
HIGH = 18
LOW = 20
STRIP = 16
FIELDS = 7
TO_PREVIOUS = [(f, 0) for f in range(FIELDS)] + [(f, 1) for f in (0, 2, 3, 4, 5, 6)]
TO_NEXT = [(f, 1) for f in range(FIELDS)] + [(f, 0) for f in (0, 1, 2, 3, 5)]
ROW = PADX * PADY
CORNER_ROWS = 32
CHUNK = 5
PAIRS = [(i, j) for i in range(STEPS + 1) for j in range(i, STEPS + 1)]
VMEM_LIMIT = 40 * 1024 * 1024


def layout(gx_size, gy_size):
    cores = 2
    z_size = min(8, gy_size // 2)
    return gx_size // cores, cores, gy_size // z_size, z_size


def rings(sizes):
    result = []
    for axis, size in (("x", sizes[0]), ("y", sizes[2]), ("z", sizes[3])):
        near = sorted({1 % size, size - 1} - {0})
        far = sorted({2 % size, (size - 2) % size} - {0}) if size > 3 else []
        result.append((axis, size, near, far))
    return result


def farthest_first(first, second):
    def hops(step, size):
        return min(step, size - step)

    steps = [(a, b) for a in range(first) for b in range(second) if a or b]
    return sorted(steps, key=lambda step: -hops(step[0], first) - hops(step[1], second))


def next_y(value):
    return pltpu.roll(value, PADY - 1, 0)


def prev_y(value):
    return pltpu.roll(value, 1, 0)


def next_z(value):
    return pltpu.roll(value, value.shape[1] - 1, 1)


def prev_z(value):
    return pltpu.roll(value, 1, 1)


def settle(buffer, semaphore):
    pltpu.make_async_copy(buffer, buffer, semaphore).wait()


def exchange_kernel(
    sizes,
    tiles,
    u_e,
    u_h,
    eps_in,
    metal_in,
    omega_in,
    gamma_in,
    strength_in,
    own_out,
    gram_out,
    tiles_out,
    kicks_out,
    raw,
    face_in,
    k1,
    k2,
    k3,
    k4,
    u,
    previous_out,
    previous_in,
    next_out,
    next_in,
    corner_out,
    corner_in,
    mask,
    acc_rows,
    sum_a,
    sum_b,
    metal,
    omega,
    gamma,
    strength,
    heard,
    load_sem,
    face_send,
    face_recv,
    stage_send,
    stage_recv,
):
    x_size, cores, y_size, z_size = sizes
    gx_size, gy_size = x_size * cores, y_size * z_size
    gx = lax.axis_index("gx")
    gy = lax.axis_index("gy")

    loads = [
        pltpu.make_async_copy(u_e, raw.at[pl.ds(0, 3)], load_sem.at[0]),
        pltpu.make_async_copy(u_h, raw.at[pl.ds(3, 3)], load_sem.at[1]),
        pltpu.make_async_copy(eps_in, raw.at[6], load_sem.at[2]),
        pltpu.make_async_copy(metal_in, metal, load_sem.at[3]),
        pltpu.make_async_copy(omega_in, omega, load_sem.at[4]),
        pltpu.make_async_copy(gamma_in, gamma, load_sem.at[5]),
        pltpu.make_async_copy(strength_in, strength, load_sem.at[6]),
    ]
    def ring(position, size):
        return [position] + [lax.rem(position + step, size) for step in range(1, size)]

    def device(x, core, y, z):
        return (x * cores + core, y * z_size + z)

    around_x = {0: gx, -1: lax.rem(gx + gx_size - 1, gx_size), 1: lax.rem(gx + 1, gx_size)}
    around_y = {0: gy, -1: lax.rem(gy + gy_size - 1, gy_size), 1: lax.rem(gy + 1, gy_size)}

    def neighbour(dx, dy):
        return (around_x[dx], around_y[dy])

    my_x, my_core = lax.div(gx, cores), lax.rem(gx, cores)
    my_y, my_z = lax.div(gy, z_size), lax.rem(gy, z_size)
    ring_x, ring_core = ring(my_x, x_size), ring(my_core, cores)
    ring_y, ring_z = ring(my_y, y_size), ring(my_z, z_size)

    def along(axis, step, core=0):
        return device(
            ring_x[step if axis == "x" else 0],
            ring_core[core],
            ring_y[step if axis == "y" else 0],
            ring_z[step if axis == "z" else 0],
        )

    def signal(semaphore, target):
        pl.semaphore_signal(semaphore, inc=1, device_id=target, device_id_type=MESH)

    beside = [(0, -1), (0, 1), (-1, 0), (1, 0)]
    near = [(axis, step, 0) for axis, _, steps, _ in rings(sizes) for step in steps]
    near += [(axis, step, 1) for axis, step, _ in near if axis == "z"]
    far = [(axis, step) for axis, _, _, steps in rings(sizes) for step in steps]
    barrier = pltpu.get_barrier_semaphore()
    for dx, dy in beside:
        signal(barrier, neighbour(dx, dy))
    for place in near:
        signal(barrier, along(*place))
    for load in loads:
        load.start()

    for load in loads:
        load.wait()

    for number, (f, layer) in enumerate(TO_PREVIOUS):
        previous_out[number] = raw[f, pl.ds(layer, OWN, stride=OWN), :]
    for number, (f, layer) in enumerate(TO_NEXT):
        next_out[number] = raw[f, pl.ds(OWN - 2 + layer, OWN, stride=OWN), :]
    corners = [(0, 0), (0, 1), (1, 0), (1, 1)]
    for number, (side_x, side_y) in enumerate(corners):
        for f in range(FIELDS):
            for layer in range(2):
                if side_x != side_y:
                    x = (0 if side_x == 0 else OWN - 2) + layer
                    y = 0 if side_y == 0 else OWN - 2
                    cells = raw[f, pl.ds(x * OWN + y, 2), :]
                    corner_out[number, pl.ds(f * 4 + layer * 2, 2), :] = cells
                elif layer == 0:
                    cell = 0 if side_x == 0 else OWN * OWN - 1
                    corner_out[number, pl.ds(f, 1), :] = raw[f, pl.ds(cell, 1), :]

    pl.semaphore_wait(barrier, len(beside) + len(near))

    copies = []

    def send(src, dst, device):
        number = len(copies)
        copy = pltpu.make_async_remote_copy(
            src_ref=src,
            dst_ref=dst,
            send_sem=face_send.at[number],
            recv_sem=face_recv.at[number],
            device_id=device,
            device_id_type=MESH,
        )
        copy.start()
        copies.append(copy)

    send(previous_out, previous_in, neighbour(0, -1))
    send(next_out, next_in, neighbour(0, 1))
    everything = pl.ds(0, FIELDS)
    layers = EDGE * OWN
    send(raw.at[everything, pl.ds(0, layers)], face_in.at[0], neighbour(-1, 0))
    send(raw.at[everything, pl.ds(OWN * OWN - layers, layers)], face_in.at[1], neighbour(1, 0))
    for dx, dy in beside[2:]:
        signal(heard.at[0], neighbour(dx, dy))
    for place in near:
        signal(heard.at[0], along(*place))

    tile_rows = [lax.rem(2 * gx + s - 1 + tiles[0], tiles[0]) for s in range(4)]
    tile_cols = [lax.rem(2 * gy + t - 1 + tiles[1], tiles[1]) for t in range(4)]
    place = lax.broadcasted_iota(jnp.int32, (8, 128), 0)
    for s in range(4):
        flag = [
            jnp.full((8, 128), metal[tile_rows[s], tile_cols[t]].astype(jnp.float32)) for t in range(4)
        ]
        mask[s, 0:8] = jnp.where(place < 6, flag[1], flag[2])
        mask[s, 8:16] = jnp.where(place < 2, flag[1], flag[2])
        beyond = jnp.where(place < 4, flag[3], flag[0])
        mask[s, 16:24] = jnp.where(place < 2, flag[2], jnp.where(place < 6, beyond, flag[1]))

    response = [jnp.float32(0.0)] * 3
    for p in range(POLES):
        g0 = strength[p]
        g1 = -gamma[p] * g0
        g2 = -(omega[p] * omega[p]) * g0 - gamma[p] * g1
        response = [response[0] + g0, response[1] + g1, response[2] + g2]

    def put_row(f, x, low, high):
        first = pl.multiple_of(x * PADY, 8)
        low_by_6, low_by_2 = pltpu.roll(low, 6, 0), pltpu.roll(low, 2, 0)
        high_by_6, high_by_2 = pltpu.roll(high, 6, 0), pltpu.roll(high, 2, 0)
        u[f, pl.ds(first, 8), :] = jnp.where(place < 6, low_by_6, high_by_6)
        u[f, pl.ds(first + 8, 8), :] = jnp.where(place < 2, low_by_2, high_by_2)
        u[f, pl.ds(first + 16, 8), :] = jnp.where(place < 4, high_by_2, low_by_6)

    def copy_own(x, carry):
        first = pl.multiple_of(x * OWN, 8)
        for f in range(FIELDS):
            put_row(f, x + EDGE, raw[f, pl.ds(first, 8), :], raw[f, pl.ds(first + 8, 8), :])
        return carry

    lax.fori_loop(0, OWN, copy_own, 0)

    pl.semaphore_wait(heard.at[0], len(beside[2:]) + len(near))
    for axis, step in far:
        signal(heard.at[1], along(axis, step))
    for number, (side_x, side_y) in enumerate(corners):
        rows = pl.ds(0, 8 if side_x == side_y else CORNER_ROWS)
        send(
            corner_out.at[number, rows],
            corner_in.at[number, rows],
            neighbour(2 * side_x - 1, 2 * side_y - 1),
        )

    class Padded:
        def __getitem__(self, at):
            f, x = at
            return u[f, pl.ds(pl.multiple_of(x * PADY, 8), PADY), :]

    start = Padded()
    states = [start, k1, k2, k3, k4]

    def electric(step, x):
        old = states[step - 1]
        hx, hy, hz = old[3, x], old[4, x], old[5, x]
        hy_back, hz_back = old[4, x - 1], old[5, x - 1]
        curl = [
            (hz - prev_y(hz)) - (hy - prev_z(hy)),
            (hx - prev_z(hx)) - (hz - hz_back),
            (hy - hy_back) - (hx - prev_y(hx)),
        ]
        eps = start[6, x]
        if step > 1:
            metal_here = mask[(x + 6) // 8]
            for c in range(3):
                current = response[step - 2] * start[c, x]
                for j in range(1, step - 1):
                    current = current + response[step - 2 - j] * states[j][c, x]
                curl[c] = curl[c] - metal_here * current
        return [eps * part for part in curl]

    def magnetic(step, x):
        old = states[step - 1]
        ex, ey, ez = old[0, x], old[1, x], old[2, x]
        ey_next, ez_next = old[1, x + 1], old[2, x + 1]
        return [
            (next_z(ey) - ey) - (next_y(ez) - ez),
            (ez_next - ez) - (next_z(ex) - ex),
            (next_y(ex) - ex) - (ey_next - ey),
        ]

    def write_rows(step, starts, shift):
        new = states[step]
        parts = [(x, electric(step, x), magnetic(step, x - shift)) for x in starts]
        for x, of_e, of_h in parts:
            for c in range(3):
                new[c, x] = of_e[c]
                new[3 + c, x - shift] = of_h[c]

    def interior(step, low, high, shift):
        rest = high - low - CHUNK
        chunks = -(-rest // CHUNK) + 1

        def rows(i, carry):
            first = low + (i * rest) // (chunks - 1)
            write_rows(step, [first + k for k in range(CHUNK)], shift)
            return carry

        lax.fori_loop(0, chunks, rows, 0)

    def edges(step, low, high, shift):
        write_rows(step, [low, low + 1, high, high + 1], shift)

    def state_at(j, c, x, first, count):
        if j == 0:
            return u[c, pl.ds(x * PADY + first, count), :]
        return states[j][c, x, pl.ds(first, count), :]

    def strip(j, c, x):
        if j == 0:
            return u[c, pl.ds(pl.multiple_of(x * PADY + STRIP, 8), 8), :]
        return states[j][c, x, pl.ds(STRIP, 8), :]

    def strip_prev(j, c, x, value):
        return jnp.where(place == 0, state_at(j, c, x, STRIP - 1, 1), pltpu.roll(value, 1, 0))

    def strip_next(j, c, x, value):
        return jnp.where(place == 7, state_at(j, c, x, 0, 1), pltpu.roll(value, 7, 0))

    def strip_electric(step, x):
        old = step - 1
        hx, hy, hz = (strip(old, c, x) for c in (3, 4, 5))
        hy_back, hz_back = strip(old, 4, x - 1), strip(old, 5, x - 1)
        curl = [
            (hz - strip_prev(old, 5, x, hz)) - (hy - prev_z(hy)),
            (hx - prev_z(hx)) - (hz - hz_back),
            (hy - hy_back) - (hx - strip_prev(old, 3, x, hx)),
        ]
        if step > 1:
            metal_here = mask[(x + 6) // 8, pl.ds(STRIP, 8), :]
            for c in range(3):
                current = response[step - 2] * strip(0, c, x)
                for j in range(1, step - 1):
                    current = current + response[step - 2 - j] * strip(j, c, x)
                curl[c] = curl[c] - metal_here * current
        eps = strip(0, 6, x)
        return [eps * part for part in curl]

    def strip_magnetic(step, x):
        old = step - 1
        ex, ey, ez = (strip(old, c, x) for c in (0, 1, 2))
        ey_next, ez_next = strip(old, 1, x + 1), strip(old, 2, x + 1)
        return [
            (next_z(ey) - ey) - (strip_next(old, 2, x, ez) - ez),
            (ez_next - ez) - (next_z(ex) - ex),
            (strip_next(old, 0, x, ex) - ex) - (ey_next - ey),
        ]

    def write_strips(step, starts, shift):
        new = states[step]
        parts = [(x, strip_electric(step, x), strip_magnetic(step, x - shift)) for x in starts]
        for x, of_e, of_h in parts:
            for c in range(3):
                new[c, x, pl.ds(STRIP, 8), :] = of_e[c]
                new[3 + c, x - shift, pl.ds(STRIP, 8), :] = of_h[c]

    def interior_strips(step, low, high, shift):
        write_strips(step, list(range(low, high)), shift)

    zero = jnp.zeros((8, 128), jnp.float32)

    def products(first, x, sums):
        sums = list(sums)
        cells = pl.ds(first, 8)
        for c in range(6):
            values = [u[c, pl.ds(pl.multiple_of(x * PADY + first, 8), 8), :]]
            values += [state[c, x, cells, :] for state in states[1:]]
            for number, (i, j) in enumerate(PAIRS):
                sums[number] = sums[number] + values[i] * values[j]
        return tuple(sums)

    ends = jnp.logical_or(place < 2, place >= 6)

    def strip_products(pairs, sums):
        sums = list(sums)
        for x, other in pairs:
            for c in range(6):
                values = [
                    jnp.where(ends, strip(j, c, x), pltpu.roll(strip(j, c, other), 4, 0))
                    for j in range(STEPS + 1)
                ]
                for number, (i, j) in enumerate(PAIRS):
                    sums[number] = sums[number] + values[i] * values[j]
        return tuple(sums)

    def interior_products(first, sums):
        return lax.fori_loop(
            EDGE + 2, EDGE + OWN - 2, lambda x, sums: products(first, x, sums), sums
        )

    def edge_products(first, sums):
        return lax.fori_loop(
            0,
            2 * EDGE,
            lambda i, sums: products(first, EDGE + i + i // 2 * (OWN - 4), sums),
            sums,
        )

    def keep(sums, wanted, into):
        for number, part in enumerate(sums):
            at = pl.ds(8 * number, 8)
            part = jnp.where(wanted, part, 0.0)
            acc_rows[at, :] = part + acc_rows[at, :] if into else part

    none = (zero,) * len(PAIRS)
    interior(1, EDGE + 1, EDGE + OWN, 1)
    interior(2, EDGE + 1, EDGE + OWN - 1, 0)
    interior(3, EDGE + 2, EDGE + OWN - 1, 1)
    interior(4, EDGE + 2, EDGE + OWN - 2, 0)
    keep(interior_products(0, none), place < 6, False)
    keep(interior_products(8, none), place >= 2, True)
    acc_rows[pl.ds(8 * len(PAIRS), 8), :] = zero

    for copy in copies[:2]:
        copy.wait_recv()
    for number, (f, layer) in enumerate(TO_PREVIOUS):
        u[f, pl.ds(EDGE * PADY + HIGH + layer, OWN, stride=PADY), :] = previous_in[number]
    for number, (f, layer) in enumerate(TO_NEXT):
        u[f, pl.ds(EDGE * PADY + LOW + layer, OWN, stride=PADY), :] = next_in[number]
    interior_strips(1, EDGE + 1, EDGE + OWN, 1)
    interior_strips(2, EDGE + 1, EDGE + OWN - 1, 0)
    interior_strips(3, EDGE + 2, EDGE + OWN - 1, 1)
    interior_strips(4, EDGE + 2, EDGE + OWN - 2, 0)
    sums = lax.fori_loop(
        0,
        3,
        lambda i, sums: strip_products([(4 + 4 * i, 5 + 4 * i), (6 + 4 * i, 7 + 4 * i)], sums),
        none,
    )

    for copy in copies[2:]:
        copy.wait_recv()
    for f in range(FIELDS):
        for side, first in ((0, EDGE + OWN), (1, 0)):
            for layer in range(2):
                low = face_in[side, f, pl.ds(layer * OWN, 8), :]
                high = face_in[side, f, pl.ds(layer * OWN + 8, 8), :]
                put_row(f, first + layer, low, high)
    for number, (side_x, side_y) in enumerate(corners):
        for f in range(FIELDS):
            for layer in range(2):
                x = (EDGE + OWN if side_x == 0 else 0) + layer
                y = HIGH if side_y == 0 else LOW
                if side_x != side_y:
                    source = corner_in[number, pl.ds(f * 4 + layer * 2, 2), :]
                    u[f, pl.ds(x * PADY + y, 2), :] = source
                elif layer == side_x:
                    u[f, pl.ds(x * PADY + y + layer, 1), :] = corner_in[number, pl.ds(f, 1), :]
    edges(1, 1, EDGE + OWN, 1)
    edges(2, 1, EDGE + OWN - 1, 0)
    edges(3, EDGE, EDGE + OWN - 1, 1)
    edges(4, EDGE, EDGE + OWN - 2, 0)
    keep(edge_products(0, none), place < 6, True)
    keep(edge_products(8, none), place >= 2, True)
    keep(strip_products([(2, 3), (16, 17)], sums), place < 8, True)

    total = acc_rows[pl.ds(0, 16, stride=8), :]
    for s in range(1, 8):
        total = total + acc_rows[pl.ds(s, 16, stride=8), :]
    diagonal = lax.broadcasted_iota(jnp.int32, (16, 128), 0) == lax.broadcasted_iota(jnp.int32, (16, 128), 1)

    def to_row(column):
        return jnp.sum(jnp.where(diagonal, column, 0.0), axis=0, keepdims=True)

    def gather_metal():
        flags = [metal[tile_rows[1 + t // 2], tile_cols[1 + t % 2]] for t in range(4)]
        present = [flag.astype(jnp.float32) for flag in flags]
        before = jnp.float32(0.0)
        chosen = [[None] * 4 for _ in range(MS)]
        for t in range(4):
            taken = [present[t] * (1.0 - before), present[t] * before]
            before = before + present[t]
            for slot in range(MS):
                chosen[slot][t] = taken[slot]

        def rows(x, carry):
            for c in range(3):
                for j in range(STEPS):
                    parts = []
                    for t in range(4):
                        at = 8 * (t // 2) + x
                        y = 8 * (t % 2)
                        if j == 0:
                            parts.append(raw[c, pl.ds(pl.multiple_of(at * OWN + y, 8), 8), :])
                        else:
                            parts.append(own_out[j - 1, c, at, pl.ds(y, 8), :])
                    for slot in range(MS):
                        value = chosen[slot][0] * parts[0]
                        for t in range(1, 4):
                            value = value + chosen[slot][t] * parts[t]
                        tiles_out[slot, j, c, x] = value
            return carry

        lax.fori_loop(0, 8, rows, 0)
        for p in range(POLES):
            kicks = [strength[p]]
            kicks.append(-gamma[p] * kicks[0])
            for k in range(2, STEPS):
                kicks.append(-(omega[p] * omega[p]) * kicks[k - 2] - gamma[p] * kicks[k - 1])
            for k in range(STEPS):
                kicks_out[pl.ds(p * STEPS + k, 1), :] = jnp.full((1, 128), kicks[k])

    def order_own():
        def rows(x, carry):
            for j, state in enumerate(states[1:]):
                for c in range(6):
                    tile = [state[c, x + EDGE, pl.ds(8 * t, 8), :] for t in range(3)]
                    own_out[j, c, x, pl.ds(0, 8), :] = jnp.where(
                        place < 2, pltpu.roll(tile[2], 2, 0), pltpu.roll(tile[0], 2, 0)
                    )
                    own_out[j, c, x, pl.ds(8, 8), :] = jnp.where(
                        place < 6, pltpu.roll(tile[1], 6, 0), pltpu.roll(tile[2], 6, 0)
                    )
            return carry

        lax.fori_loop(0, OWN, rows, 0)

    row = to_row(jnp.sum(total, axis=1, keepdims=True))
    if far:
        pl.semaphore_wait(heard.at[1], len(far))
    me_a = my_core * z_size + my_z
    me_b = my_x * y_size + my_y
    targets_a = [
        device(my_x, ring_core[c], my_y, ring_z[z]) for c, z in farthest_first(cores, z_size)
    ]
    targets_b = [
        device(ring_x[x], my_core, ring_y[y], my_z) for x, y in farthest_first(x_size, y_size)
    ]
    for stage, (slots, me, targets) in enumerate(((sum_a, me_a, targets_a), (sum_b, me_b, targets_b))):
        slots[me] = row
        for target in targets:
            pltpu.make_async_remote_copy(
                src_ref=slots.at[me],
                dst_ref=slots.at[me],
                send_sem=stage_send.at[stage],
                recv_sem=stage_recv.at[stage],
                device_id=target,
                device_id_type=MESH,
            ).start()
        if stage == 0:
            order_own()
        else:
            gather_metal()
        settle(slots.at[pl.ds(0, len(targets))], stage_recv.at[stage])
        row = slots[0]
        for member in range(1, len(targets) + 1):
            row = row + slots[member]
    gram_out[...] = jnp.broadcast_to(
        jnp.sum(jnp.where(diagonal, row, 0.0), axis=1, keepdims=True), (16, 128)
    )

    for copy in copies:
        copy.wait_send()
    for stage, (slots, targets) in enumerate(((sum_a, targets_a), (sum_b, targets_b))):
        settle(slots.at[pl.ds(0, len(targets))], stage_send.at[stage])


def finish_kernel(
    cell_count,
    k0,
    own,
    gram,
    tiles,
    kicks,
    out_e,
    out_h,
    out_poles,
    out_coefficients,
    coefficients,
    table,
    fields,
    poles,
    pole_sem,
    store_sem,
):
    stores = []

    def store(src, dst):
        copy = pltpu.make_async_copy(src, dst, store_sem.at[len(stores)])
        copy.start()
        stores.append(copy)

    inner = {}
    for number, (i, j) in enumerate(PAIRS):
        inner[i, j] = inner[j, i] = gram[pl.ds(number, 1), :] * (1.0 / cell_count)
    unit = 1.0 / jnp.sqrt(inner[0, 0] + EPSILON)
    weights = [unit]
    lane = lax.broadcasted_iota(jnp.int32, (1, 128), 1)
    for step in range(1, STEPS + 1):
        image = [None] + weights

        def total(terms):
            return functools.reduce(jnp.add, terms)

        along_q = unit * total([image[j] * inner[0, j] for j in range(1, step + 1)])
        rest = [-along_q * unit] + image[1:]
        along_v = jnp.zeros_like(unit)
        if step > 1:
            along_v = total(
                [
                    image[j] * total([weights[i] * inner[i, j] for i in range(step)])
                    for j in range(1, step + 1)
                ]
            )
            for i in range(step):
                rest[i] = rest[i] - along_v * weights[i]
        squared = total(
            [rest[i] * total([rest[j] * inner[i, j] for j in range(step + 1)]) for i in range(step + 1)]
        )
        norm = jnp.sqrt(jnp.maximum(squared, 0.0) + EPSILON)
        scale = 1.0 / norm
        weights = [part * scale for part in rest]
        line = jnp.where(lane == 0, along_q, jnp.where(lane == 1, along_v, norm))
        coefficients[pl.ds(step - 1, 1), :] = line[:, :3]

    store(coefficients, out_coefficients)

    for p in range(POLES):
        kick = [kicks[pl.ds(p * STEPS + k, 1), :] for k in range(STEPS)]
        for j in range(STEPS):
            parts = [weights[k] * kick[k - 1 - j] for k in range(j + 1, STEPS + 1)]
            table[pl.ds(p * 8 + j, 1), :] = functools.reduce(jnp.add, parts)
        for j in range(STEPS - 1):
            parts = [weights[k] * kick[k - 2 - j] for k in range(j + 2, STEPS + 1)]
            table[pl.ds(p * 8 + 4 + j, 1), :] = functools.reduce(jnp.add, parts)
    for j in range(STEPS + 1):
        table[pl.ds(48 + j, 1), :] = weights[j]

    def entry(number):
        return jnp.broadcast_to(table[pl.ds(number, 1), :], (8, 128))

    def pole_part(i):
        return (i // 3, pl.ds(0, 2), pl.ds(0, POLES), i % 3)

    def pole_cells(i, carry):
        slot, c = i // 3, i % 3
        for x in range(8):
            field = [tiles[slot, j, c, x] for j in range(STEPS)]
            for p in range(POLES):
                poles[slot, 1, p, c, x] = functools.reduce(
                    jnp.add, [entry(p * 8 + j) * field[j] for j in range(STEPS)]
                )
                poles[slot, 0, p, c, x] = functools.reduce(
                    jnp.add, [entry(p * 8 + 4 + j) * field[j] for j in range(STEPS - 1)]
                )
        pltpu.make_async_copy(
            poles.at[pole_part(i)], out_poles.at[pole_part(i)], pole_sem.at[i]
        ).start()
        return carry

    lax.fori_loop(0, 3 * MS, pole_cells, 0)

    for half, out in enumerate((out_e, out_h)):

        def field_cells(i, carry):
            for x in [4 * i + k for k in range(4)]:
                for c in range(3 * half, 3 * half + 3):
                    cells = pl.ds(pl.multiple_of(x * OWN, 8), OWN)
                    value = table[pl.ds(48, 1), :] * k0[c, cells, :]
                    for j in range(STEPS):
                        value = value + table[pl.ds(49 + j, 1), :] * own[j, c, x]
                    fields[c, x] = value
            return carry

        lax.fori_loop(0, OWN // 4, field_cells, 0)
        store(fields.at[pl.ds(3 * half, 3)], out)
    for i in range(3 * MS):
        pltpu.make_async_copy(poles.at[pole_part(i)], out_poles.at[pole_part(i)], pole_sem.at[i]).wait()
    for copy in stores:
        copy.wait()


def body(sizes, u_electric, u_magnetic, eps_inv, metal_map, pole_omega, pole_gamma, pole_strength):
    depth = u_electric.shape[3]
    cell_count = 6.0 * OWN * OWN * depth * sizes[0] * sizes[1] * sizes[2] * sizes[3]
    f32 = jnp.float32
    any_spec = pl.BlockSpec(memory_space=pl.ANY)
    hbm = pl.BlockSpec(memory_space=pltpu.HBM)
    vmem = pl.BlockSpec(memory_space=pltpu.VMEM)
    a_size = sizes[1] * sizes[3]
    b_size = sizes[0] * sizes[2]

    def stay(value):
        return pltpu.with_memory_space_constraint(value, pltpu.HBM)

    start = [u_electric.reshape(3, OWN * OWN, depth), u_magnetic.reshape(3, OWN * OWN, depth)]
    model = [stay(part) for part in (metal_map, pole_omega, pole_gamma, pole_strength)]
    dma = pltpu.SemaphoreType.DMA
    results = pl.pallas_call(
        functools.partial(exchange_kernel, sizes, metal_map.shape),
        out_shape=[
            jax.ShapeDtypeStruct((STEPS, 6, OWN, OWN, depth), f32),
            jax.ShapeDtypeStruct((16, depth), f32),
            jax.ShapeDtypeStruct((MS, STEPS, 3, 8, 8, depth), f32),
            jax.ShapeDtypeStruct((POLES * STEPS, depth), f32),
            jax.ShapeDtypeStruct((FIELDS, OWN * OWN, depth), f32),
        ],
        in_specs=[hbm] * 7,
        out_specs=[vmem] * 5,
        scratch_shapes=[
            pltpu.VMEM((2, FIELDS, EDGE * OWN, depth), f32),
            *[pltpu.VMEM((6, PADX, PADY, depth), f32)] * STEPS,
            pltpu.VMEM((FIELDS, ROW, depth), f32),
            pltpu.VMEM((len(TO_PREVIOUS), OWN, depth), f32),
            pltpu.VMEM((len(TO_PREVIOUS), OWN, depth), f32),
            pltpu.VMEM((len(TO_NEXT), OWN, depth), f32),
            pltpu.VMEM((len(TO_NEXT), OWN, depth), f32),
            pltpu.VMEM((4, CORNER_ROWS, depth), f32),
            pltpu.VMEM((4, CORNER_ROWS, depth), f32),
            pltpu.VMEM((4, PADY, depth), f32),
            pltpu.VMEM((128, depth), f32),
            pltpu.VMEM((a_size, 1, depth), f32),
            pltpu.VMEM((b_size, 1, depth), f32),
            pltpu.SMEM(metal_map.shape, jnp.int32),
            pltpu.SMEM((POLES,), f32),
            pltpu.SMEM((POLES,), f32),
            pltpu.SMEM((POLES,), f32),
            pltpu.SemaphoreType.REGULAR((2,)),
            dma((7,)),
            dma((8,)),
            dma((8,)),
            dma((2,)),
            dma((2,)),
        ],
        compiler_params=pltpu.CompilerParams(
            collective_id=0, has_side_effects=True, vmem_limit_bytes=VMEM_LIMIT
        ),
    )(*[stay(part) for part in start], stay(eps_inv.reshape(OWN * OWN, depth)), *model)

    own, gram, tiles, kicks, raw = results

    return pl.pallas_call(
        functools.partial(finish_kernel, cell_count),
        out_shape=[
            jax.ShapeDtypeStruct(u_electric.shape, f32),
            jax.ShapeDtypeStruct(u_magnetic.shape, f32),
            jax.ShapeDtypeStruct((MS, 2, POLES, 3, 8, 8, depth), f32),
            jax.ShapeDtypeStruct((STEPS, 3), f32),
        ],
        in_specs=[vmem] * 5,
        out_specs=[any_spec] * 4,
        scratch_shapes=[
            pltpu.VMEM((STEPS, 3), f32),
            pltpu.VMEM((56, depth), f32),
            pltpu.VMEM((6, OWN, OWN, depth), f32),
            pltpu.VMEM((MS, 2, POLES, 3, 8, 8, depth), f32),
            dma((3 * MS,)),
            dma((3,)),
        ],
        compiler_params=pltpu.CompilerParams(vmem_limit_bytes=VMEM_LIMIT),
    )(raw, own, gram, tiles, kicks)


def solution(mesh):
    sizes = layout(mesh.shape["gx"], mesh.shape["gy"])
    placed = (
        P(None, "gx", "gy", None),
        P(None, "gx", "gy", None),
        P("gx", "gy", None),
        P(),
        P(),
        P(),
        P(),
    )
    return jax.shard_map(
        functools.partial(body, sizes),
        mesh=mesh,
        in_specs=placed,
        out_specs=(
            P(None, "gx", "gy", None),
            P(None, "gx", "gy", None),
            P(("gx", "gy"), None, None, None, None, None, None),
            P(),
        ),
        check_vma=False,
    )
```

```python
import functools

import jax
import jax.numpy as jnp
from jax import lax
from jax.experimental import pallas as pl
from jax.experimental.pallas import tpu as pltpu
from jax.sharding import PartitionSpec as P

POLES = 6
STEPS = 4
MS = 2
EPSILON = 1e-06
MESH = pl.DeviceIdType.MESH

EDGE = 2
OWN = 16
PADX = OWN + 2 * EDGE
PADY = 24
HIGH = 18
LOW = 20
STRIP = 16
FIELDS = 7
TO_PREVIOUS = [(f, 0) for f in range(FIELDS)] + [(f, 1) for f in (0, 2, 3, 4, 5, 6)]
TO_NEXT = [(f, 1) for f in range(FIELDS)] + [(f, 0) for f in (0, 1, 2, 3, 5)]
ROW = PADX * PADY
CORNER_ROWS = 32
CHUNK = 5
PAIRS = [(i, j) for i in range(STEPS + 1) for j in range(i, STEPS + 1)]
VMEM_LIMIT = 40 * 1024 * 1024


def layout(gx_size, gy_size):
    cores = 2
    z_size = min(8, gy_size // 2)
    return gx_size // cores, cores, gy_size // z_size, z_size


def rings(sizes):
    result = []
    for axis, size in (("x", sizes[0]), ("y", sizes[2]), ("z", sizes[3])):
        near = sorted({1 % size, size - 1} - {0})
        far = sorted({2 % size, (size - 2) % size} - {0}) if size > 3 else []
        result.append((axis, size, near, far))
    return result


def farthest_first(first, second):
    def hops(step, size):
        return min(step, size - step)

    steps = [(a, b) for a in range(first) for b in range(second) if a or b]
    return sorted(steps, key=lambda step: -hops(step[0], first) - hops(step[1], second))


def next_y(value):
    return pltpu.roll(value, PADY - 1, 0)


def prev_y(value):
    return pltpu.roll(value, 1, 0)


def next_z(value):
    return pltpu.roll(value, value.shape[1] - 1, 1)


def prev_z(value):
    return pltpu.roll(value, 1, 1)


def settle(buffer, semaphore):
    pltpu.make_async_copy(buffer, buffer, semaphore).wait()


def exchange_kernel(
    sizes,
    tiles,
    u_e,
    u_h,
    eps_in,
    metal_in,
    omega_in,
    gamma_in,
    strength_in,
    own_out,
    gram_out,
    tiles_out,
    kicks_out,
    raw,
    face_in,
    k1,
    k2,
    k3,
    k4,
    u,
    previous_out,
    previous_in,
    next_out,
    next_in,
    corner_out,
    corner_in,
    mask,
    acc_rows,
    sum_a,
    sum_b,
    metal,
    omega,
    gamma,
    strength,
    heard,
    load_sem,
    face_send,
    face_recv,
    stage_send,
    stage_recv,
):
    x_size, cores, y_size, z_size = sizes
    gx_size, gy_size = x_size * cores, y_size * z_size
    gx = lax.axis_index("gx")
    gy = lax.axis_index("gy")

    loads = [
        pltpu.make_async_copy(u_e, raw.at[pl.ds(0, 3)], load_sem.at[0]),
        pltpu.make_async_copy(u_h, raw.at[pl.ds(3, 3)], load_sem.at[1]),
        pltpu.make_async_copy(eps_in, raw.at[6], load_sem.at[2]),
        pltpu.make_async_copy(metal_in, metal, load_sem.at[3]),
        pltpu.make_async_copy(omega_in, omega, load_sem.at[4]),
        pltpu.make_async_copy(gamma_in, gamma, load_sem.at[5]),
        pltpu.make_async_copy(strength_in, strength, load_sem.at[6]),
    ]
    def ring(position, size):
        return [position] + [lax.rem(position + step, size) for step in range(1, size)]

    def device(x, core, y, z):
        return (x * cores + core, y * z_size + z)

    around_x = {0: gx, -1: lax.rem(gx + gx_size - 1, gx_size), 1: lax.rem(gx + 1, gx_size)}
    around_y = {0: gy, -1: lax.rem(gy + gy_size - 1, gy_size), 1: lax.rem(gy + 1, gy_size)}

    def neighbour(dx, dy):
        return (around_x[dx], around_y[dy])

    my_x, my_core = lax.div(gx, cores), lax.rem(gx, cores)
    my_y, my_z = lax.div(gy, z_size), lax.rem(gy, z_size)
    ring_x, ring_core = ring(my_x, x_size), ring(my_core, cores)
    ring_y, ring_z = ring(my_y, y_size), ring(my_z, z_size)

    def along(axis, step, core=0):
        return device(
            ring_x[step if axis == "x" else 0],
            ring_core[core],
            ring_y[step if axis == "y" else 0],
            ring_z[step if axis == "z" else 0],
        )

    def signal(semaphore, target):
        pl.semaphore_signal(semaphore, inc=1, device_id=target, device_id_type=MESH)

    corners = [(0, 0), (0, 1), (1, 0), (1, 1)]
    beside = [(2 * side_x - 1, 2 * side_y - 1) for side_x, side_y in corners]
    beside += [(0, -1), (0, 1), (-1, 0), (1, 0)]
    near = [(axis, step, 0) for axis, _, steps, _ in rings(sizes) for step in steps]
    near += [(axis, step, 1) for axis, step, _ in near if axis == "z"]
    far = [(axis, step) for axis, _, _, steps in rings(sizes) for step in steps]
    barrier = pltpu.get_barrier_semaphore()
    for dx, dy in beside:
        signal(barrier, neighbour(dx, dy))
    for place in near:
        signal(barrier, along(*place))
    for load in loads:
        load.start()

    for load in loads:
        load.wait()

    for number, (f, layer) in enumerate(TO_PREVIOUS):
        previous_out[number] = raw[f, pl.ds(layer, OWN, stride=OWN), :]
    for number, (f, layer) in enumerate(TO_NEXT):
        next_out[number] = raw[f, pl.ds(OWN - 2 + layer, OWN, stride=OWN), :]
    for number, (side_x, side_y) in enumerate(corners):
        for f in range(FIELDS):
            for layer in range(2):
                if side_x != side_y:
                    x = (0 if side_x == 0 else OWN - 2) + layer
                    y = 0 if side_y == 0 else OWN - 2
                    cells = raw[f, pl.ds(x * OWN + y, 2), :]
                    corner_out[number, pl.ds(f * 4 + layer * 2, 2), :] = cells
                elif layer == 0:
                    cell = 0 if side_x == 0 else OWN * OWN - 1
                    corner_out[number, pl.ds(f, 1), :] = raw[f, pl.ds(cell, 1), :]

    pl.semaphore_wait(barrier, len(beside) + len(near))

    copies = []

    def send(src, dst, device):
        number = len(copies)
        copy = pltpu.make_async_remote_copy(
            src_ref=src,
            dst_ref=dst,
            send_sem=face_send.at[number],
            recv_sem=face_recv.at[number],
            device_id=device,
            device_id_type=MESH,
        )
        copy.start()
        copies.append(copy)

    send(previous_out, previous_in, neighbour(0, -1))
    send(next_out, next_in, neighbour(0, 1))
    for number, (side_x, side_y) in enumerate(corners):
        rows = pl.ds(0, 8 if side_x == side_y else CORNER_ROWS)
        send(
            corner_out.at[number, rows],
            corner_in.at[number, rows],
            neighbour(2 * side_x - 1, 2 * side_y - 1),
        )
    everything = pl.ds(0, FIELDS)
    layers = EDGE * OWN
    send(raw.at[everything, pl.ds(0, layers)], face_in.at[0], neighbour(-1, 0))
    send(raw.at[everything, pl.ds(OWN * OWN - layers, layers)], face_in.at[1], neighbour(1, 0))
    for place in near:
        signal(heard.at[0], along(*place))

    tile_rows = [lax.rem(2 * gx + s - 1 + tiles[0], tiles[0]) for s in range(4)]
    tile_cols = [lax.rem(2 * gy + t - 1 + tiles[1], tiles[1]) for t in range(4)]
    place = lax.broadcasted_iota(jnp.int32, (8, 128), 0)
    for s in range(4):
        flag = [
            jnp.full((8, 128), metal[tile_rows[s], tile_cols[t]].astype(jnp.float32)) for t in range(4)
        ]
        mask[s, 0:8] = jnp.where(place < 6, flag[1], flag[2])
        mask[s, 8:16] = jnp.where(place < 2, flag[1], flag[2])
        beyond = jnp.where(place < 4, flag[3], flag[0])
        mask[s, 16:24] = jnp.where(place < 2, flag[2], jnp.where(place < 6, beyond, flag[1]))

    response = [jnp.float32(0.0)] * 3
    for p in range(POLES):
        g0 = strength[p]
        g1 = -gamma[p] * g0
        g2 = -(omega[p] * omega[p]) * g0 - gamma[p] * g1
        response = [response[0] + g0, response[1] + g1, response[2] + g2]

    def put_row(f, x, low, high):
        first = pl.multiple_of(x * PADY, 8)
        low_by_6, low_by_2 = pltpu.roll(low, 6, 0), pltpu.roll(low, 2, 0)
        high_by_6, high_by_2 = pltpu.roll(high, 6, 0), pltpu.roll(high, 2, 0)
        u[f, pl.ds(first, 8), :] = jnp.where(place < 6, low_by_6, high_by_6)
        u[f, pl.ds(first + 8, 8), :] = jnp.where(place < 2, low_by_2, high_by_2)
        u[f, pl.ds(first + 16, 8), :] = jnp.where(place < 4, high_by_2, low_by_6)

    def copy_own(x, carry):
        first = pl.multiple_of(x * OWN, 8)
        for f in range(FIELDS):
            put_row(f, x + EDGE, raw[f, pl.ds(first, 8), :], raw[f, pl.ds(first + 8, 8), :])
        return carry

    lax.fori_loop(0, OWN, copy_own, 0)

    pl.semaphore_wait(heard.at[0], len(near))
    for axis, step in far:
        signal(heard.at[1], along(axis, step))
    class Padded:
        def __getitem__(self, at):
            f, x = at
            return u[f, pl.ds(pl.multiple_of(x * PADY, 8), PADY), :]

    start = Padded()
    states = [start, k1, k2, k3, k4]

    def electric(step, x):
        old = states[step - 1]
        hx, hy, hz = old[3, x], old[4, x], old[5, x]
        hy_back, hz_back = old[4, x - 1], old[5, x - 1]
        curl = [
            (hz - prev_y(hz)) - (hy - prev_z(hy)),
            (hx - prev_z(hx)) - (hz - hz_back),
            (hy - hy_back) - (hx - prev_y(hx)),
        ]
        eps = start[6, x]
        if step > 1:
            metal_here = mask[(x + 6) // 8]
            for c in range(3):
                current = response[step - 2] * start[c, x]
                for j in range(1, step - 1):
                    current = current + response[step - 2 - j] * states[j][c, x]
                curl[c] = curl[c] - metal_here * current
        return [eps * part for part in curl]

    def magnetic(step, x):
        old = states[step - 1]
        ex, ey, ez = old[0, x], old[1, x], old[2, x]
        ey_next, ez_next = old[1, x + 1], old[2, x + 1]
        return [
            (next_z(ey) - ey) - (next_y(ez) - ez),
            (ez_next - ez) - (next_z(ex) - ex),
            (next_y(ex) - ex) - (ey_next - ey),
        ]

    def write_rows(step, starts, shift):
        new = states[step]
        parts = [(x, electric(step, x), magnetic(step, x - shift)) for x in starts]
        for x, of_e, of_h in parts:
            for c in range(3):
                new[c, x] = of_e[c]
                new[3 + c, x - shift] = of_h[c]

    def interior(step, low, high, shift):
        rest = high - low - CHUNK
        chunks = -(-rest // CHUNK) + 1

        def rows(i, carry):
            first = low + (i * rest) // (chunks - 1)
            write_rows(step, [first + k for k in range(CHUNK)], shift)
            return carry

        lax.fori_loop(0, chunks, rows, 0)

    def edges(step, low, high, shift):
        write_rows(step, [low, low + 1, high, high + 1], shift)

    def state_at(j, c, x, first, count):
        if j == 0:
            return u[c, pl.ds(x * PADY + first, count), :]
        return states[j][c, x, pl.ds(first, count), :]

    def strip(j, c, x):
        if j == 0:
            return u[c, pl.ds(pl.multiple_of(x * PADY + STRIP, 8), 8), :]
        return states[j][c, x, pl.ds(STRIP, 8), :]

    def strip_prev(j, c, x, value):
        return jnp.where(place == 0, state_at(j, c, x, STRIP - 1, 1), pltpu.roll(value, 1, 0))

    def strip_next(j, c, x, value):
        return jnp.where(place == 7, state_at(j, c, x, 0, 1), pltpu.roll(value, 7, 0))

    def strip_electric(step, x):
        old = step - 1
        hx, hy, hz = (strip(old, c, x) for c in (3, 4, 5))
        hy_back, hz_back = strip(old, 4, x - 1), strip(old, 5, x - 1)
        curl = [
            (hz - strip_prev(old, 5, x, hz)) - (hy - prev_z(hy)),
            (hx - prev_z(hx)) - (hz - hz_back),
            (hy - hy_back) - (hx - strip_prev(old, 3, x, hx)),
        ]
        if step > 1:
            metal_here = mask[(x + 6) // 8, pl.ds(STRIP, 8), :]
            for c in range(3):
                current = response[step - 2] * strip(0, c, x)
                for j in range(1, step - 1):
                    current = current + response[step - 2 - j] * strip(j, c, x)
                curl[c] = curl[c] - metal_here * current
        eps = strip(0, 6, x)
        return [eps * part for part in curl]

    def strip_magnetic(step, x):
        old = step - 1
        ex, ey, ez = (strip(old, c, x) for c in (0, 1, 2))
        ey_next, ez_next = strip(old, 1, x + 1), strip(old, 2, x + 1)
        return [
            (next_z(ey) - ey) - (strip_next(old, 2, x, ez) - ez),
            (ez_next - ez) - (next_z(ex) - ex),
            (strip_next(old, 0, x, ex) - ex) - (ey_next - ey),
        ]

    def write_strips(step, starts, shift):
        new = states[step]
        parts = [(x, strip_electric(step, x), strip_magnetic(step, x - shift)) for x in starts]
        for x, of_e, of_h in parts:
            for c in range(3):
                new[c, x, pl.ds(STRIP, 8), :] = of_e[c]
                new[3 + c, x - shift, pl.ds(STRIP, 8), :] = of_h[c]

    def interior_strips(step, low, high, shift):
        write_strips(step, list(range(low, high)), shift)

    zero = jnp.zeros((8, 128), jnp.float32)

    def products(first, x, sums):
        sums = list(sums)
        cells = pl.ds(first, 8)
        for c in range(6):
            values = [u[c, pl.ds(pl.multiple_of(x * PADY + first, 8), 8), :]]
            values += [state[c, x, cells, :] for state in states[1:]]
            for number, (i, j) in enumerate(PAIRS):
                sums[number] = sums[number] + values[i] * values[j]
        return tuple(sums)

    ends = jnp.logical_or(place < 2, place >= 6)

    def strip_products(pairs, sums):
        sums = list(sums)
        for x, other in pairs:
            for c in range(6):
                values = [
                    jnp.where(ends, strip(j, c, x), pltpu.roll(strip(j, c, other), 4, 0))
                    for j in range(STEPS + 1)
                ]
                for number, (i, j) in enumerate(PAIRS):
                    sums[number] = sums[number] + values[i] * values[j]
        return tuple(sums)

    def interior_products(first, sums):
        return lax.fori_loop(
            EDGE + 2, EDGE + OWN - 2, lambda x, sums: products(first, x, sums), sums
        )

    def edge_products(first, sums):
        return lax.fori_loop(
            0,
            2 * EDGE,
            lambda i, sums: products(first, EDGE + i + i // 2 * (OWN - 4), sums),
            sums,
        )

    def keep(sums, wanted, into):
        for number, part in enumerate(sums):
            at = pl.ds(8 * number, 8)
            part = jnp.where(wanted, part, 0.0)
            acc_rows[at, :] = part + acc_rows[at, :] if into else part

    none = (zero,) * len(PAIRS)
    interior(1, EDGE + 1, EDGE + OWN, 1)
    interior(2, EDGE + 1, EDGE + OWN - 1, 0)
    interior(3, EDGE + 2, EDGE + OWN - 1, 1)
    interior(4, EDGE + 2, EDGE + OWN - 2, 0)
    keep(interior_products(0, none), place < 6, False)
    keep(interior_products(8, none), place >= 2, True)
    acc_rows[pl.ds(8 * len(PAIRS), 8), :] = zero

    for copy in copies[:2]:
        copy.wait_recv()
    for number, (f, layer) in enumerate(TO_PREVIOUS):
        u[f, pl.ds(EDGE * PADY + HIGH + layer, OWN, stride=PADY), :] = previous_in[number]
    for number, (f, layer) in enumerate(TO_NEXT):
        u[f, pl.ds(EDGE * PADY + LOW + layer, OWN, stride=PADY), :] = next_in[number]
    interior_strips(1, EDGE + 1, EDGE + OWN, 1)
    interior_strips(2, EDGE + 1, EDGE + OWN - 1, 0)
    interior_strips(3, EDGE + 2, EDGE + OWN - 1, 1)
    interior_strips(4, EDGE + 2, EDGE + OWN - 2, 0)
    sums = lax.fori_loop(
        0,
        3,
        lambda i, sums: strip_products([(4 + 4 * i, 5 + 4 * i), (6 + 4 * i, 7 + 4 * i)], sums),
        none,
    )

    for copy in copies[2:]:
        copy.wait_recv()
    for f in range(FIELDS):
        for side, first in ((0, EDGE + OWN), (1, 0)):
            for layer in range(2):
                low = face_in[side, f, pl.ds(layer * OWN, 8), :]
                high = face_in[side, f, pl.ds(layer * OWN + 8, 8), :]
                put_row(f, first + layer, low, high)
    for number, (side_x, side_y) in enumerate(corners):
        for f in range(FIELDS):
            for layer in range(2):
                x = (EDGE + OWN if side_x == 0 else 0) + layer
                y = HIGH if side_y == 0 else LOW
                if side_x != side_y:
                    source = corner_in[number, pl.ds(f * 4 + layer * 2, 2), :]
                    u[f, pl.ds(x * PADY + y, 2), :] = source
                elif layer == side_x:
                    u[f, pl.ds(x * PADY + y + layer, 1), :] = corner_in[number, pl.ds(f, 1), :]
    edges(1, 1, EDGE + OWN, 1)
    edges(2, 1, EDGE + OWN - 1, 0)
    edges(3, EDGE, EDGE + OWN - 1, 1)
    edges(4, EDGE, EDGE + OWN - 2, 0)
    keep(edge_products(0, none), place < 6, True)
    keep(edge_products(8, none), place >= 2, True)
    keep(strip_products([(2, 3), (16, 17)], sums), place < 8, True)

    total = acc_rows[pl.ds(0, 16, stride=8), :]
    for s in range(1, 8):
        total = total + acc_rows[pl.ds(s, 16, stride=8), :]
    diagonal = lax.broadcasted_iota(jnp.int32, (16, 128), 0) == lax.broadcasted_iota(jnp.int32, (16, 128), 1)

    def to_row(column):
        return jnp.sum(jnp.where(diagonal, column, 0.0), axis=0, keepdims=True)

    def gather_metal():
        flags = [metal[tile_rows[1 + t // 2], tile_cols[1 + t % 2]] for t in range(4)]
        present = [flag.astype(jnp.float32) for flag in flags]
        before = jnp.float32(0.0)
        chosen = [[None] * 4 for _ in range(MS)]
        for t in range(4):
            taken = [present[t] * (1.0 - before), present[t] * before]
            before = before + present[t]
            for slot in range(MS):
                chosen[slot][t] = taken[slot]

        def rows(x, carry):
            for c in range(3):
                for j in range(STEPS):
                    parts = []
                    for t in range(4):
                        at = 8 * (t // 2) + x
                        y = 8 * (t % 2)
                        if j == 0:
                            parts.append(raw[c, pl.ds(pl.multiple_of(at * OWN + y, 8), 8), :])
                        else:
                            parts.append(own_out[j - 1, c, at, pl.ds(y, 8), :])
                    for slot in range(MS):
                        value = chosen[slot][0] * parts[0]
                        for t in range(1, 4):
                            value = value + chosen[slot][t] * parts[t]
                        tiles_out[slot, j, c, x] = value
            return carry

        lax.fori_loop(0, 8, rows, 0)
        for p in range(POLES):
            kicks = [strength[p]]
            kicks.append(-gamma[p] * kicks[0])
            for k in range(2, STEPS):
                kicks.append(-(omega[p] * omega[p]) * kicks[k - 2] - gamma[p] * kicks[k - 1])
            for k in range(STEPS):
                kicks_out[pl.ds(p * STEPS + k, 1), :] = jnp.full((1, 128), kicks[k])

    def order_own():
        def rows(x, carry):
            for j, state in enumerate(states[1:]):
                for c in range(6):
                    tile = [state[c, x + EDGE, pl.ds(8 * t, 8), :] for t in range(3)]
                    own_out[j, c, x, pl.ds(0, 8), :] = jnp.where(
                        place < 2, pltpu.roll(tile[2], 2, 0), pltpu.roll(tile[0], 2, 0)
                    )
                    own_out[j, c, x, pl.ds(8, 8), :] = jnp.where(
                        place < 6, pltpu.roll(tile[1], 6, 0), pltpu.roll(tile[2], 6, 0)
                    )
            return carry

        lax.fori_loop(0, OWN, rows, 0)

    row = to_row(jnp.sum(total, axis=1, keepdims=True))
    if far:
        pl.semaphore_wait(heard.at[1], len(far))
    me_a = my_core * z_size + my_z
    me_b = my_x * y_size + my_y
    targets_a = [
        device(my_x, ring_core[c], my_y, ring_z[z]) for c, z in farthest_first(cores, z_size)
    ]
    targets_b = [
        device(ring_x[x], my_core, ring_y[y], my_z) for x, y in farthest_first(x_size, y_size)
    ]
    for stage, (slots, me, targets) in enumerate(((sum_a, me_a, targets_a), (sum_b, me_b, targets_b))):
        slots[me] = row
        for target in targets:
            pltpu.make_async_remote_copy(
                src_ref=slots.at[me],
                dst_ref=slots.at[me],
                send_sem=stage_send.at[stage],
                recv_sem=stage_recv.at[stage],
                device_id=target,
                device_id_type=MESH,
            ).start()
        if stage == 0:
            order_own()
        else:
            gather_metal()
        settle(slots.at[pl.ds(0, len(targets))], stage_recv.at[stage])
        row = slots[0]
        for member in range(1, len(targets) + 1):
            row = row + slots[member]
    gram_out[...] = jnp.broadcast_to(
        jnp.sum(jnp.where(diagonal, row, 0.0), axis=1, keepdims=True), (16, 128)
    )

    for copy in copies:
        copy.wait_send()
    for stage, (slots, targets) in enumerate(((sum_a, targets_a), (sum_b, targets_b))):
        settle(slots.at[pl.ds(0, len(targets))], stage_send.at[stage])


def finish_kernel(
    cell_count,
    k0,
    own,
    gram,
    tiles,
    kicks,
    out_e,
    out_h,
    out_poles,
    out_coefficients,
    coefficients,
    table,
    fields,
    poles,
    pole_sem,
    store_sem,
):
    stores = []

    def store(src, dst):
        copy = pltpu.make_async_copy(src, dst, store_sem.at[len(stores)])
        copy.start()
        stores.append(copy)

    inner = {}
    for number, (i, j) in enumerate(PAIRS):
        inner[i, j] = inner[j, i] = gram[pl.ds(number, 1), :] * (1.0 / cell_count)
    unit = 1.0 / jnp.sqrt(inner[0, 0] + EPSILON)
    weights = [unit]
    lane = lax.broadcasted_iota(jnp.int32, (1, 128), 1)
    for step in range(1, STEPS + 1):
        image = [None] + weights

        def total(terms):
            return functools.reduce(jnp.add, terms)

        along_q = unit * total([image[j] * inner[0, j] for j in range(1, step + 1)])
        rest = [-along_q * unit] + image[1:]
        along_v = jnp.zeros_like(unit)
        if step > 1:
            along_v = total(
                [
                    image[j] * total([weights[i] * inner[i, j] for i in range(step)])
                    for j in range(1, step + 1)
                ]
            )
            for i in range(step):
                rest[i] = rest[i] - along_v * weights[i]
        squared = total(
            [rest[i] * total([rest[j] * inner[i, j] for j in range(step + 1)]) for i in range(step + 1)]
        )
        norm = jnp.sqrt(jnp.maximum(squared, 0.0) + EPSILON)
        scale = 1.0 / norm
        weights = [part * scale for part in rest]
        line = jnp.where(lane == 0, along_q, jnp.where(lane == 1, along_v, norm))
        coefficients[pl.ds(step - 1, 1), :] = line[:, :3]

    store(coefficients, out_coefficients)

    for p in range(POLES):
        kick = [kicks[pl.ds(p * STEPS + k, 1), :] for k in range(STEPS)]
        for j in range(STEPS):
            parts = [weights[k] * kick[k - 1 - j] for k in range(j + 1, STEPS + 1)]
            table[pl.ds(p * 8 + j, 1), :] = functools.reduce(jnp.add, parts)
        for j in range(STEPS - 1):
            parts = [weights[k] * kick[k - 2 - j] for k in range(j + 2, STEPS + 1)]
            table[pl.ds(p * 8 + 4 + j, 1), :] = functools.reduce(jnp.add, parts)
    for j in range(STEPS + 1):
        table[pl.ds(48 + j, 1), :] = weights[j]

    def entry(number):
        return jnp.broadcast_to(table[pl.ds(number, 1), :], (8, 128))

    def pole_part(i):
        return (i // 3, pl.ds(0, 2), pl.ds(0, POLES), i % 3)

    def pole_cells(i, carry):
        slot, c = i // 3, i % 3
        for x in range(8):
            field = [tiles[slot, j, c, x] for j in range(STEPS)]
            for p in range(POLES):
                poles[slot, 1, p, c, x] = functools.reduce(
                    jnp.add, [entry(p * 8 + j) * field[j] for j in range(STEPS)]
                )
                poles[slot, 0, p, c, x] = functools.reduce(
                    jnp.add, [entry(p * 8 + 4 + j) * field[j] for j in range(STEPS - 1)]
                )
        pltpu.make_async_copy(
            poles.at[pole_part(i)], out_poles.at[pole_part(i)], pole_sem.at[i]
        ).start()
        return carry

    lax.fori_loop(0, 3 * MS, pole_cells, 0)

    for half, out in enumerate((out_e, out_h)):

        def field_cells(i, carry):
            for x in [4 * i + k for k in range(4)]:
                for c in range(3 * half, 3 * half + 3):
                    cells = pl.ds(pl.multiple_of(x * OWN, 8), OWN)
                    value = table[pl.ds(48, 1), :] * k0[c, cells, :]
                    for j in range(STEPS):
                        value = value + table[pl.ds(49 + j, 1), :] * own[j, c, x]
                    fields[c, x] = value
            return carry

        lax.fori_loop(0, OWN // 4, field_cells, 0)
        store(fields.at[pl.ds(3 * half, 3)], out)
    for i in range(3 * MS):
        pltpu.make_async_copy(poles.at[pole_part(i)], out_poles.at[pole_part(i)], pole_sem.at[i]).wait()
    for copy in stores:
        copy.wait()


def body(sizes, u_electric, u_magnetic, eps_inv, metal_map, pole_omega, pole_gamma, pole_strength):
    depth = u_electric.shape[3]
    cell_count = 6.0 * OWN * OWN * depth * sizes[0] * sizes[1] * sizes[2] * sizes[3]
    f32 = jnp.float32
    any_spec = pl.BlockSpec(memory_space=pl.ANY)
    hbm = pl.BlockSpec(memory_space=pltpu.HBM)
    vmem = pl.BlockSpec(memory_space=pltpu.VMEM)
    a_size = sizes[1] * sizes[3]
    b_size = sizes[0] * sizes[2]

    def stay(value):
        return pltpu.with_memory_space_constraint(value, pltpu.HBM)

    start = [u_electric.reshape(3, OWN * OWN, depth), u_magnetic.reshape(3, OWN * OWN, depth)]
    model = [stay(part) for part in (metal_map, pole_omega, pole_gamma, pole_strength)]
    dma = pltpu.SemaphoreType.DMA
    results = pl.pallas_call(
        functools.partial(exchange_kernel, sizes, metal_map.shape),
        out_shape=[
            jax.ShapeDtypeStruct((STEPS, 6, OWN, OWN, depth), f32),
            jax.ShapeDtypeStruct((16, depth), f32),
            jax.ShapeDtypeStruct((MS, STEPS, 3, 8, 8, depth), f32),
            jax.ShapeDtypeStruct((POLES * STEPS, depth), f32),
            jax.ShapeDtypeStruct((FIELDS, OWN * OWN, depth), f32),
        ],
        in_specs=[hbm] * 7,
        out_specs=[vmem] * 5,
        scratch_shapes=[
            pltpu.VMEM((2, FIELDS, EDGE * OWN, depth), f32),
            *[pltpu.VMEM((6, PADX, PADY, depth), f32)] * STEPS,
            pltpu.VMEM((FIELDS, ROW, depth), f32),
            pltpu.VMEM((len(TO_PREVIOUS), OWN, depth), f32),
            pltpu.VMEM((len(TO_PREVIOUS), OWN, depth), f32),
            pltpu.VMEM((len(TO_NEXT), OWN, depth), f32),
            pltpu.VMEM((len(TO_NEXT), OWN, depth), f32),
            pltpu.VMEM((4, CORNER_ROWS, depth), f32),
            pltpu.VMEM((4, CORNER_ROWS, depth), f32),
            pltpu.VMEM((4, PADY, depth), f32),
            pltpu.VMEM((128, depth), f32),
            pltpu.VMEM((a_size, 1, depth), f32),
            pltpu.VMEM((b_size, 1, depth), f32),
            pltpu.SMEM(metal_map.shape, jnp.int32),
            pltpu.SMEM((POLES,), f32),
            pltpu.SMEM((POLES,), f32),
            pltpu.SMEM((POLES,), f32),
            pltpu.SemaphoreType.REGULAR((2,)),
            dma((7,)),
            dma((8,)),
            dma((8,)),
            dma((2,)),
            dma((2,)),
        ],
        compiler_params=pltpu.CompilerParams(
            collective_id=0, has_side_effects=True, vmem_limit_bytes=VMEM_LIMIT
        ),
    )(*[stay(part) for part in start], stay(eps_inv.reshape(OWN * OWN, depth)), *model)

    own, gram, tiles, kicks, raw = results

    return pl.pallas_call(
        functools.partial(finish_kernel, cell_count),
        out_shape=[
            jax.ShapeDtypeStruct(u_electric.shape, f32),
            jax.ShapeDtypeStruct(u_magnetic.shape, f32),
            jax.ShapeDtypeStruct((MS, 2, POLES, 3, 8, 8, depth), f32),
            jax.ShapeDtypeStruct((STEPS, 3), f32),
        ],
        in_specs=[vmem] * 5,
        out_specs=[any_spec] * 4,
        scratch_shapes=[
            pltpu.VMEM((STEPS, 3), f32),
            pltpu.VMEM((56, depth), f32),
            pltpu.VMEM((6, OWN, OWN, depth), f32),
            pltpu.VMEM((MS, 2, POLES, 3, 8, 8, depth), f32),
            dma((3 * MS,)),
            dma((3,)),
        ],
        compiler_params=pltpu.CompilerParams(vmem_limit_bytes=VMEM_LIMIT),
    )(raw, own, gram, tiles, kicks)


def solution(mesh):
    sizes = layout(mesh.shape["gx"], mesh.shape["gy"])
    placed = (
        P(None, "gx", "gy", None),
        P(None, "gx", "gy", None),
        P("gx", "gy", None),
        P(),
        P(),
        P(),
        P(),
    )
    return jax.shard_map(
        functools.partial(body, sizes),
        mesh=mesh,
        in_specs=placed,
        out_specs=(
            P(None, "gx", "gy", None),
            P(None, "gx", "gy", None),
            P(("gx", "gy"), None, None, None, None, None, None),
            P(),
        ),
        check_vma=False,
    )
```

```python
import functools

import jax
import jax.numpy as jnp
from jax import lax
from jax.experimental import pallas as pl
from jax.experimental.pallas import tpu as pltpu
from jax.sharding import PartitionSpec as P

POLES = 6
STEPS = 4
MS = 2
EPSILON = 1e-06
MESH = pl.DeviceIdType.MESH

EDGE = 2
OWN = 16
PADX = OWN + 2 * EDGE
PADY = 24
HIGH = 18
LOW = 20
STRIP = 16
FIELDS = 7
TO_PREVIOUS = [(f, 0) for f in range(FIELDS)] + [(f, 1) for f in (0, 2, 3, 4, 5, 6)]
TO_NEXT = [(f, 1) for f in range(FIELDS)] + [(f, 0) for f in (0, 1, 2, 3, 5)]
ROW = PADX * PADY
CORNER_ROWS = 32
CHUNK = 5
PAIRS = [(i, j) for i in range(STEPS + 1) for j in range(i, STEPS + 1)]
VMEM_LIMIT = 40 * 1024 * 1024


def layout(gx_size, gy_size):
    cores = 2
    z_size = min(8, gy_size // 2)
    return gx_size // cores, cores, gy_size // z_size, z_size


def rings(sizes):
    result = []
    for axis, size in (("x", sizes[0]), ("y", sizes[2]), ("z", sizes[3])):
        near = sorted({1 % size, size - 1} - {0})
        far = sorted({2 % size, (size - 2) % size} - {0}) if size > 3 else []
        result.append((axis, size, near, far))
    return result


def farthest_first(first, second):
    def hops(step, size):
        return min(step, size - step)

    steps = [(a, b) for a in range(first) for b in range(second) if a or b]
    return sorted(steps, key=lambda step: -hops(step[0], first) - hops(step[1], second))


def next_y(value):
    return pltpu.roll(value, PADY - 1, 0)


def prev_y(value):
    return pltpu.roll(value, 1, 0)


def next_z(value):
    return pltpu.roll(value, value.shape[1] - 1, 1)


def prev_z(value):
    return pltpu.roll(value, 1, 1)


def settle(buffer, semaphore):
    pltpu.make_async_copy(buffer, buffer, semaphore).wait()


def exchange_kernel(
    sizes,
    tiles,
    u_e,
    u_h,
    eps_in,
    metal_in,
    omega_in,
    gamma_in,
    strength_in,
    own_out,
    gram_out,
    tiles_out,
    kicks_out,
    raw,
    face_in,
    k1,
    k2,
    k3,
    k4,
    u,
    previous_out,
    previous_in,
    next_out,
    next_in,
    corner_out,
    corner_in,
    mask,
    acc_rows,
    sum_a,
    sum_b,
    metal,
    omega,
    gamma,
    strength,
    heard,
    load_sem,
    face_send,
    face_recv,
    stage_send,
    stage_recv,
):
    x_size, cores, y_size, z_size = sizes
    gx_size, gy_size = x_size * cores, y_size * z_size
    gx = lax.axis_index("gx")
    gy = lax.axis_index("gy")

    loads = [
        pltpu.make_async_copy(u_e, raw.at[pl.ds(0, 3)], load_sem.at[0]),
        pltpu.make_async_copy(u_h, raw.at[pl.ds(3, 3)], load_sem.at[1]),
        pltpu.make_async_copy(eps_in, raw.at[6], load_sem.at[2]),
        pltpu.make_async_copy(metal_in, metal, load_sem.at[3]),
        pltpu.make_async_copy(omega_in, omega, load_sem.at[4]),
        pltpu.make_async_copy(gamma_in, gamma, load_sem.at[5]),
        pltpu.make_async_copy(strength_in, strength, load_sem.at[6]),
    ]
    for load in loads:
        load.start()

    def ring(position, size):
        return [position] + [lax.rem(position + step, size) for step in range(1, size)]

    def device(x, core, y, z):
        return (x * cores + core, y * z_size + z)

    around_x = {0: gx, -1: lax.rem(gx + gx_size - 1, gx_size), 1: lax.rem(gx + 1, gx_size)}
    around_y = {0: gy, -1: lax.rem(gy + gy_size - 1, gy_size), 1: lax.rem(gy + 1, gy_size)}

    def neighbour(dx, dy):
        return (around_x[dx], around_y[dy])

    my_x, my_core = lax.div(gx, cores), lax.rem(gx, cores)
    my_y, my_z = lax.div(gy, z_size), lax.rem(gy, z_size)
    ring_x, ring_core = ring(my_x, x_size), ring(my_core, cores)
    ring_y, ring_z = ring(my_y, y_size), ring(my_z, z_size)

    def along(axis, step, core=0):
        return device(
            ring_x[step if axis == "x" else 0],
            ring_core[core],
            ring_y[step if axis == "y" else 0],
            ring_z[step if axis == "z" else 0],
        )

    def signal(semaphore, target):
        pl.semaphore_signal(semaphore, inc=1, device_id=target, device_id_type=MESH)

    beside = [(0, -1), (0, 1), (-1, 0), (1, 0)]
    near = [(axis, step, 0) for axis, _, steps, _ in rings(sizes) for step in steps]
    near += [(axis, step, 1) for axis, step, _ in near if axis == "z"]
    far = [(axis, step) for axis, _, _, steps in rings(sizes) for step in steps]
    barrier = pltpu.get_barrier_semaphore()
    for dx, dy in beside:
        signal(barrier, neighbour(dx, dy))
    for place in near:
        signal(barrier, along(*place))

    for load in loads:
        load.wait()

    for number, (f, layer) in enumerate(TO_PREVIOUS):
        previous_out[number] = raw[f, pl.ds(layer, OWN, stride=OWN), :]
    for number, (f, layer) in enumerate(TO_NEXT):
        next_out[number] = raw[f, pl.ds(OWN - 2 + layer, OWN, stride=OWN), :]
    corners = [(0, 0), (0, 1), (1, 0), (1, 1)]
    for number, (side_x, side_y) in enumerate(corners):
        for f in range(FIELDS):
            for layer in range(2):
                if side_x != side_y:
                    x = (0 if side_x == 0 else OWN - 2) + layer
                    y = 0 if side_y == 0 else OWN - 2
                    cells = raw[f, pl.ds(x * OWN + y, 2), :]
                    corner_out[number, pl.ds(f * 4 + layer * 2, 2), :] = cells
                elif layer == 0:
                    cell = 0 if side_x == 0 else OWN * OWN - 1
                    corner_out[number, pl.ds(f, 1), :] = raw[f, pl.ds(cell, 1), :]

    pl.semaphore_wait(barrier, len(beside) + len(near))

    copies = []

    def send(src, dst, device):
        number = len(copies)
        copy = pltpu.make_async_remote_copy(
            src_ref=src,
            dst_ref=dst,
            send_sem=face_send.at[number],
            recv_sem=face_recv.at[number],
            device_id=device,
            device_id_type=MESH,
        )
        copy.start()
        copies.append(copy)

    send(previous_out, previous_in, neighbour(0, -1))
    send(next_out, next_in, neighbour(0, 1))
    everything = pl.ds(0, FIELDS)
    layers = EDGE * OWN
    send(raw.at[everything, pl.ds(0, layers)], face_in.at[0], neighbour(-1, 0))
    send(raw.at[everything, pl.ds(OWN * OWN - layers, layers)], face_in.at[1], neighbour(1, 0))
    for dx, dy in beside[2:]:
        signal(heard.at[2], neighbour(dx, dy))
    for place in near:
        signal(heard.at[0], along(*place))

    tile_rows = [lax.rem(2 * gx + s - 1 + tiles[0], tiles[0]) for s in range(4)]
    tile_cols = [lax.rem(2 * gy + t - 1 + tiles[1], tiles[1]) for t in range(4)]
    place = lax.broadcasted_iota(jnp.int32, (8, 128), 0)
    for s in range(4):
        flag = [
            jnp.full((8, 128), metal[tile_rows[s], tile_cols[t]].astype(jnp.float32)) for t in range(4)
        ]
        mask[s, 0:8] = jnp.where(place < 6, flag[1], flag[2])
        mask[s, 8:16] = jnp.where(place < 2, flag[1], flag[2])
        beyond = jnp.where(place < 4, flag[3], flag[0])
        mask[s, 16:24] = jnp.where(place < 2, flag[2], jnp.where(place < 6, beyond, flag[1]))

    response = [jnp.float32(0.0)] * 3
    for p in range(POLES):
        g0 = strength[p]
        g1 = -gamma[p] * g0
        g2 = -(omega[p] * omega[p]) * g0 - gamma[p] * g1
        response = [response[0] + g0, response[1] + g1, response[2] + g2]

    def put_row(f, x, low, high):
        first = pl.multiple_of(x * PADY, 8)
        low_by_6, low_by_2 = pltpu.roll(low, 6, 0), pltpu.roll(low, 2, 0)
        high_by_6, high_by_2 = pltpu.roll(high, 6, 0), pltpu.roll(high, 2, 0)
        u[f, pl.ds(first, 8), :] = jnp.where(place < 6, low_by_6, high_by_6)
        u[f, pl.ds(first + 8, 8), :] = jnp.where(place < 2, low_by_2, high_by_2)
        u[f, pl.ds(first + 16, 8), :] = jnp.where(place < 4, high_by_2, low_by_6)

    def copy_own(x, carry):
        first = pl.multiple_of(x * OWN, 8)
        for f in range(FIELDS):
            put_row(f, x + EDGE, raw[f, pl.ds(first, 8), :], raw[f, pl.ds(first + 8, 8), :])
        return carry

    lax.fori_loop(0, OWN, copy_own, 0)

    class Padded:
        def __getitem__(self, at):
            f, x = at
            return u[f, pl.ds(pl.multiple_of(x * PADY, 8), PADY), :]

    start = Padded()
    states = [start, k1, k2, k3, k4]

    def electric(step, x):
        old = states[step - 1]
        hx, hy, hz = old[3, x], old[4, x], old[5, x]
        hy_back, hz_back = old[4, x - 1], old[5, x - 1]
        curl = [
            (hz - prev_y(hz)) - (hy - prev_z(hy)),
            (hx - prev_z(hx)) - (hz - hz_back),
            (hy - hy_back) - (hx - prev_y(hx)),
        ]
        eps = start[6, x]
        if step > 1:
            metal_here = mask[(x + 6) // 8]
            for c in range(3):
                current = response[step - 2] * start[c, x]
                for j in range(1, step - 1):
                    current = current + response[step - 2 - j] * states[j][c, x]
                curl[c] = curl[c] - metal_here * current
        return [eps * part for part in curl]

    def magnetic(step, x):
        old = states[step - 1]
        ex, ey, ez = old[0, x], old[1, x], old[2, x]
        ey_next, ez_next = old[1, x + 1], old[2, x + 1]
        return [
            (next_z(ey) - ey) - (next_y(ez) - ez),
            (ez_next - ez) - (next_z(ex) - ex),
            (next_y(ex) - ex) - (ey_next - ey),
        ]

    def write_rows(step, starts, shift):
        new = states[step]
        parts = [(x, electric(step, x), magnetic(step, x - shift)) for x in starts]
        for x, of_e, of_h in parts:
            for c in range(3):
                new[c, x] = of_e[c]
                new[3 + c, x - shift] = of_h[c]

    def interior(step, low, high, shift):
        rest = high - low - CHUNK
        chunks = -(-rest // CHUNK) + 1

        def rows(i, carry):
            first = low + (i * rest) // (chunks - 1)
            write_rows(step, [first + k for k in range(CHUNK)], shift)
            return carry

        lax.fori_loop(0, chunks, rows, 0)

    def edges(step, low, high, shift):
        write_rows(step, [low, low + 1, high, high + 1], shift)

    def state_at(j, c, x, first, count):
        if j == 0:
            return u[c, pl.ds(x * PADY + first, count), :]
        return states[j][c, x, pl.ds(first, count), :]

    def strip(j, c, x):
        if j == 0:
            return u[c, pl.ds(pl.multiple_of(x * PADY + STRIP, 8), 8), :]
        return states[j][c, x, pl.ds(STRIP, 8), :]

    def strip_prev(j, c, x, value):
        return jnp.where(place == 0, state_at(j, c, x, STRIP - 1, 1), pltpu.roll(value, 1, 0))

    def strip_next(j, c, x, value):
        return jnp.where(place == 7, state_at(j, c, x, 0, 1), pltpu.roll(value, 7, 0))

    def strip_electric(step, x):
        old = step - 1
        hx, hy, hz = (strip(old, c, x) for c in (3, 4, 5))
        hy_back, hz_back = strip(old, 4, x - 1), strip(old, 5, x - 1)
        curl = [
            (hz - strip_prev(old, 5, x, hz)) - (hy - prev_z(hy)),
            (hx - prev_z(hx)) - (hz - hz_back),
            (hy - hy_back) - (hx - strip_prev(old, 3, x, hx)),
        ]
        if step > 1:
            metal_here = mask[(x + 6) // 8, pl.ds(STRIP, 8), :]
            for c in range(3):
                current = response[step - 2] * strip(0, c, x)
                for j in range(1, step - 1):
                    current = current + response[step - 2 - j] * strip(j, c, x)
                curl[c] = curl[c] - metal_here * current
        eps = strip(0, 6, x)
        return [eps * part for part in curl]

    def strip_magnetic(step, x):
        old = step - 1
        ex, ey, ez = (strip(old, c, x) for c in (0, 1, 2))
        ey_next, ez_next = strip(old, 1, x + 1), strip(old, 2, x + 1)
        return [
            (next_z(ey) - ey) - (strip_next(old, 2, x, ez) - ez),
            (ez_next - ez) - (next_z(ex) - ex),
            (strip_next(old, 0, x, ex) - ex) - (ey_next - ey),
        ]

    def write_strips(step, starts, shift):
        new = states[step]
        parts = [(x, strip_electric(step, x), strip_magnetic(step, x - shift)) for x in starts]
        for x, of_e, of_h in parts:
            for c in range(3):
                new[c, x, pl.ds(STRIP, 8), :] = of_e[c]
                new[3 + c, x - shift, pl.ds(STRIP, 8), :] = of_h[c]

    def interior_strips(step, low, high, shift):
        write_strips(step, list(range(low, high)), shift)

    def edge_strips(step, low, high, shift):
        write_strips(step, [low, low + 1, high, high + 1], shift)

    zero = jnp.zeros((8, 128), jnp.float32)

    def products(first, x, sums):
        sums = list(sums)
        cells = pl.ds(first, 8)
        for c in range(6):
            values = [u[c, pl.ds(pl.multiple_of(x * PADY + first, 8), 8), :]]
            values += [state[c, x, cells, :] for state in states[1:]]
            for number, (i, j) in enumerate(PAIRS):
                sums[number] = sums[number] + values[i] * values[j]
        return tuple(sums)

    ends = jnp.logical_or(place < 2, place >= 6)

    def strip_products(pairs, sums):
        sums = list(sums)
        for x, other in pairs:
            for c in range(6):
                values = [
                    jnp.where(ends, strip(j, c, x), pltpu.roll(strip(j, c, other), 4, 0))
                    for j in range(STEPS + 1)
                ]
                for number, (i, j) in enumerate(PAIRS):
                    sums[number] = sums[number] + values[i] * values[j]
        return tuple(sums)

    def interior_products(first, sums):
        return lax.fori_loop(
            EDGE + 2, EDGE + OWN - 2, lambda x, sums: products(first, x, sums), sums
        )

    def edge_products(first, sums):
        return lax.fori_loop(
            0,
            2 * EDGE,
            lambda i, sums: products(first, EDGE + i + i // 2 * (OWN - 4), sums),
            sums,
        )

    def keep(sums, wanted, into):
        for number, part in enumerate(sums):
            at = pl.ds(8 * number, 8)
            part = jnp.where(wanted, part, 0.0)
            acc_rows[at, :] = part + acc_rows[at, :] if into else part

    none = (zero,) * len(PAIRS)
    interior(1, EDGE + 1, EDGE + OWN, 1)
    interior(2, EDGE + 1, EDGE + OWN - 1, 0)
    interior(3, EDGE + 2, EDGE + OWN - 1, 1)
    interior(4, EDGE + 2, EDGE + OWN - 2, 0)
    pl.semaphore_wait(heard.at[2], len(beside[2:]))
    for number, (side_x, side_y) in enumerate(corners):
        rows = pl.ds(0, 8 if side_x == side_y else CORNER_ROWS)
        send(
            corner_out.at[number, rows],
            corner_in.at[number, rows],
            neighbour(2 * side_x - 1, 2 * side_y - 1),
        )
    pl.semaphore_wait(heard.at[0], len(near))
    for axis, step in far:
        signal(heard.at[1], along(axis, step))
    keep(interior_products(0, none), place < 6, False)
    keep(interior_products(8, none), place >= 2, True)
    acc_rows[pl.ds(8 * len(PAIRS), 8), :] = zero

    for copy in copies[2:4]:
        copy.wait_recv()
    for f in range(FIELDS):
        for side, first in ((0, EDGE + OWN), (1, 0)):
            for layer in range(2):
                low = face_in[side, f, pl.ds(layer * OWN, 8), :]
                high = face_in[side, f, pl.ds(layer * OWN + 8, 8), :]
                put_row(f, first + layer, low, high)
    edges(1, 1, EDGE + OWN, 1)
    edges(2, 1, EDGE + OWN - 1, 0)
    edges(3, EDGE, EDGE + OWN - 1, 1)
    edges(4, EDGE, EDGE + OWN - 2, 0)
    keep(edge_products(0, none), place < 6, True)
    keep(edge_products(8, none), place >= 2, True)

    for copy in copies[:2]:
        copy.wait_recv()
    for number, (f, layer) in enumerate(TO_PREVIOUS):
        u[f, pl.ds(EDGE * PADY + HIGH + layer, OWN, stride=PADY), :] = previous_in[number]
    for number, (f, layer) in enumerate(TO_NEXT):
        u[f, pl.ds(EDGE * PADY + LOW + layer, OWN, stride=PADY), :] = next_in[number]
    interior_strips(1, EDGE + 1, EDGE + OWN, 1)
    interior_strips(2, EDGE + 1, EDGE + OWN - 1, 0)
    interior_strips(3, EDGE + 2, EDGE + OWN - 1, 1)
    interior_strips(4, EDGE + 2, EDGE + OWN - 2, 0)
    sums = lax.fori_loop(
        0,
        3,
        lambda i, sums: strip_products([(4 + 4 * i, 5 + 4 * i), (6 + 4 * i, 7 + 4 * i)], sums),
        none,
    )

    for copy in copies[4:]:
        copy.wait_recv()
    for number, (side_x, side_y) in enumerate(corners):
        for f in range(FIELDS):
            for layer in range(2):
                x = (EDGE + OWN if side_x == 0 else 0) + layer
                y = HIGH if side_y == 0 else LOW
                if side_x != side_y:
                    source = corner_in[number, pl.ds(f * 4 + layer * 2, 2), :]
                    u[f, pl.ds(x * PADY + y, 2), :] = source
                elif layer == side_x:
                    u[f, pl.ds(x * PADY + y + layer, 1), :] = corner_in[number, pl.ds(f, 1), :]
    edge_strips(1, 1, EDGE + OWN, 1)
    edge_strips(2, 1, EDGE + OWN - 1, 0)
    edge_strips(3, EDGE, EDGE + OWN - 1, 1)
    edge_strips(4, EDGE, EDGE + OWN - 2, 0)
    keep(strip_products([(2, 3), (16, 17)], sums), place < 8, True)

    total = acc_rows[pl.ds(0, 16, stride=8), :]
    for s in range(1, 8):
        total = total + acc_rows[pl.ds(s, 16, stride=8), :]
    diagonal = lax.broadcasted_iota(jnp.int32, (16, 128), 0) == lax.broadcasted_iota(jnp.int32, (16, 128), 1)

    def to_row(column):
        return jnp.sum(jnp.where(diagonal, column, 0.0), axis=0, keepdims=True)

    def gather_metal():
        flags = [metal[tile_rows[1 + t // 2], tile_cols[1 + t % 2]] for t in range(4)]
        present = [flag.astype(jnp.float32) for flag in flags]
        before = jnp.float32(0.0)
        chosen = [[None] * 4 for _ in range(MS)]
        for t in range(4):
            taken = [present[t] * (1.0 - before), present[t] * before]
            before = before + present[t]
            for slot in range(MS):
                chosen[slot][t] = taken[slot]

        def rows(x, carry):
            for c in range(3):
                for j in range(STEPS):
                    parts = []
                    for t in range(4):
                        at = 8 * (t // 2) + x
                        y = 8 * (t % 2)
                        if j == 0:
                            parts.append(raw[c, pl.ds(pl.multiple_of(at * OWN + y, 8), 8), :])
                        else:
                            parts.append(own_out[j - 1, c, at, pl.ds(y, 8), :])
                    for slot in range(MS):
                        value = chosen[slot][0] * parts[0]
                        for t in range(1, 4):
                            value = value + chosen[slot][t] * parts[t]
                        tiles_out[slot, j, c, x] = value
            return carry

        lax.fori_loop(0, 8, rows, 0)
        for p in range(POLES):
            kicks = [strength[p]]
            kicks.append(-gamma[p] * kicks[0])
            for k in range(2, STEPS):
                kicks.append(-(omega[p] * omega[p]) * kicks[k - 2] - gamma[p] * kicks[k - 1])
            for k in range(STEPS):
                kicks_out[pl.ds(p * STEPS + k, 1), :] = jnp.full((1, 128), kicks[k])

    def order_own():
        def rows(x, carry):
            for j, state in enumerate(states[1:]):
                for c in range(6):
                    tile = [state[c, x + EDGE, pl.ds(8 * t, 8), :] for t in range(3)]
                    own_out[j, c, x, pl.ds(0, 8), :] = jnp.where(
                        place < 2, pltpu.roll(tile[2], 2, 0), pltpu.roll(tile[0], 2, 0)
                    )
                    own_out[j, c, x, pl.ds(8, 8), :] = jnp.where(
                        place < 6, pltpu.roll(tile[1], 6, 0), pltpu.roll(tile[2], 6, 0)
                    )
            return carry

        lax.fori_loop(0, OWN, rows, 0)

    row = to_row(jnp.sum(total, axis=1, keepdims=True))
    if far:
        pl.semaphore_wait(heard.at[1], len(far))
    me_a = my_core * z_size + my_z
    me_b = my_x * y_size + my_y
    targets_a = [
        device(my_x, ring_core[c], my_y, ring_z[z]) for c, z in farthest_first(cores, z_size)
    ]
    targets_b = [
        device(ring_x[x], my_core, ring_y[y], my_z) for x, y in farthest_first(x_size, y_size)
    ]
    for stage, (slots, me, targets) in enumerate(((sum_a, me_a, targets_a), (sum_b, me_b, targets_b))):
        slots[me] = row
        for target in targets:
            pltpu.make_async_remote_copy(
                src_ref=slots.at[me],
                dst_ref=slots.at[me],
                send_sem=stage_send.at[stage],
                recv_sem=stage_recv.at[stage],
                device_id=target,
                device_id_type=MESH,
            ).start()
        if stage == 0:
            order_own()
        else:
            gather_metal()
        settle(slots.at[pl.ds(0, len(targets))], stage_recv.at[stage])
        row = slots[0]
        for member in range(1, len(targets) + 1):
            row = row + slots[member]
    gram_out[...] = jnp.broadcast_to(
        jnp.sum(jnp.where(diagonal, row, 0.0), axis=1, keepdims=True), (16, 128)
    )

    for copy in copies:
        copy.wait_send()
    for stage, (slots, targets) in enumerate(((sum_a, targets_a), (sum_b, targets_b))):
        settle(slots.at[pl.ds(0, len(targets))], stage_send.at[stage])


def finish_kernel(
    cell_count,
    k0,
    own,
    gram,
    tiles,
    kicks,
    out_e,
    out_h,
    out_poles,
    out_coefficients,
    coefficients,
    table,
    fields,
    poles,
    pole_sem,
    store_sem,
):
    stores = []

    def store(src, dst):
        copy = pltpu.make_async_copy(src, dst, store_sem.at[len(stores)])
        copy.start()
        stores.append(copy)

    inner = {}
    for number, (i, j) in enumerate(PAIRS):
        inner[i, j] = inner[j, i] = gram[pl.ds(number, 1), :] * (1.0 / cell_count)
    unit = 1.0 / jnp.sqrt(inner[0, 0] + EPSILON)
    weights = [unit]
    lane = lax.broadcasted_iota(jnp.int32, (1, 128), 1)
    for step in range(1, STEPS + 1):
        image = [None] + weights

        def total(terms):
            return functools.reduce(jnp.add, terms)

        along_q = unit * total([image[j] * inner[0, j] for j in range(1, step + 1)])
        rest = [-along_q * unit] + image[1:]
        along_v = jnp.zeros_like(unit)
        if step > 1:
            along_v = total(
                [
                    image[j] * total([weights[i] * inner[i, j] for i in range(step)])
                    for j in range(1, step + 1)
                ]
            )
            for i in range(step):
                rest[i] = rest[i] - along_v * weights[i]
        squared = total(
            [rest[i] * total([rest[j] * inner[i, j] for j in range(step + 1)]) for i in range(step + 1)]
        )
        norm = jnp.sqrt(jnp.maximum(squared, 0.0) + EPSILON)
        scale = 1.0 / norm
        weights = [part * scale for part in rest]
        line = jnp.where(lane == 0, along_q, jnp.where(lane == 1, along_v, norm))
        coefficients[pl.ds(step - 1, 1), :] = line[:, :3]

    store(coefficients, out_coefficients)

    for p in range(POLES):
        kick = [kicks[pl.ds(p * STEPS + k, 1), :] for k in range(STEPS)]
        for j in range(STEPS):
            parts = [weights[k] * kick[k - 1 - j] for k in range(j + 1, STEPS + 1)]
            table[pl.ds(p * 8 + j, 1), :] = functools.reduce(jnp.add, parts)
        for j in range(STEPS - 1):
            parts = [weights[k] * kick[k - 2 - j] for k in range(j + 2, STEPS + 1)]
            table[pl.ds(p * 8 + 4 + j, 1), :] = functools.reduce(jnp.add, parts)
    for j in range(STEPS + 1):
        table[pl.ds(48 + j, 1), :] = weights[j]

    def entry(number):
        return jnp.broadcast_to(table[pl.ds(number, 1), :], (8, 128))

    def pole_part(i):
        return (i // 3, pl.ds(0, 2), pl.ds(0, POLES), i % 3)

    def pole_cells(i, carry):
        slot, c = i // 3, i % 3
        for x in range(8):
            field = [tiles[slot, j, c, x] for j in range(STEPS)]
            for p in range(POLES):
                poles[slot, 1, p, c, x] = functools.reduce(
                    jnp.add, [entry(p * 8 + j) * field[j] for j in range(STEPS)]
                )
                poles[slot, 0, p, c, x] = functools.reduce(
                    jnp.add, [entry(p * 8 + 4 + j) * field[j] for j in range(STEPS - 1)]
                )
        pltpu.make_async_copy(
            poles.at[pole_part(i)], out_poles.at[pole_part(i)], pole_sem.at[i]
        ).start()
        return carry

    lax.fori_loop(0, 3 * MS, pole_cells, 0)

    for half, out in enumerate((out_e, out_h)):

        def field_cells(i, carry):
            for x in [4 * i + k for k in range(4)]:
                for c in range(3 * half, 3 * half + 3):
                    cells = pl.ds(pl.multiple_of(x * OWN, 8), OWN)
                    value = table[pl.ds(48, 1), :] * k0[c, cells, :]
                    for j in range(STEPS):
                        value = value + table[pl.ds(49 + j, 1), :] * own[j, c, x]
                    fields[c, x] = value
            return carry

        lax.fori_loop(0, OWN // 4, field_cells, 0)
        store(fields.at[pl.ds(3 * half, 3)], out)
    for i in range(3 * MS):
        pltpu.make_async_copy(poles.at[pole_part(i)], out_poles.at[pole_part(i)], pole_sem.at[i]).wait()
    for copy in stores:
        copy.wait()


def body(sizes, u_electric, u_magnetic, eps_inv, metal_map, pole_omega, pole_gamma, pole_strength):
    depth = u_electric.shape[3]
    cell_count = 6.0 * OWN * OWN * depth * sizes[0] * sizes[1] * sizes[2] * sizes[3]
    f32 = jnp.float32
    any_spec = pl.BlockSpec(memory_space=pl.ANY)
    hbm = pl.BlockSpec(memory_space=pltpu.HBM)
    vmem = pl.BlockSpec(memory_space=pltpu.VMEM)
    a_size = sizes[1] * sizes[3]
    b_size = sizes[0] * sizes[2]

    def stay(value):
        return pltpu.with_memory_space_constraint(value, pltpu.HBM)

    start = [u_electric.reshape(3, OWN * OWN, depth), u_magnetic.reshape(3, OWN * OWN, depth)]
    model = [stay(part) for part in (metal_map, pole_omega, pole_gamma, pole_strength)]
    dma = pltpu.SemaphoreType.DMA
    results = pl.pallas_call(
        functools.partial(exchange_kernel, sizes, metal_map.shape),
        out_shape=[
            jax.ShapeDtypeStruct((STEPS, 6, OWN, OWN, depth), f32),
            jax.ShapeDtypeStruct((16, depth), f32),
            jax.ShapeDtypeStruct((MS, STEPS, 3, 8, 8, depth), f32),
            jax.ShapeDtypeStruct((POLES * STEPS, depth), f32),
            jax.ShapeDtypeStruct((FIELDS, OWN * OWN, depth), f32),
        ],
        in_specs=[hbm] * 7,
        out_specs=[vmem] * 5,
        scratch_shapes=[
            pltpu.VMEM((2, FIELDS, EDGE * OWN, depth), f32),
            *[pltpu.VMEM((6, PADX, PADY, depth), f32)] * STEPS,
            pltpu.VMEM((FIELDS, ROW, depth), f32),
            pltpu.VMEM((len(TO_PREVIOUS), OWN, depth), f32),
            pltpu.VMEM((len(TO_PREVIOUS), OWN, depth), f32),
            pltpu.VMEM((len(TO_NEXT), OWN, depth), f32),
            pltpu.VMEM((len(TO_NEXT), OWN, depth), f32),
            pltpu.VMEM((4, CORNER_ROWS, depth), f32),
            pltpu.VMEM((4, CORNER_ROWS, depth), f32),
            pltpu.VMEM((4, PADY, depth), f32),
            pltpu.VMEM((128, depth), f32),
            pltpu.VMEM((a_size, 1, depth), f32),
            pltpu.VMEM((b_size, 1, depth), f32),
            pltpu.SMEM(metal_map.shape, jnp.int32),
            pltpu.SMEM((POLES,), f32),
            pltpu.SMEM((POLES,), f32),
            pltpu.SMEM((POLES,), f32),
            pltpu.SemaphoreType.REGULAR((3,)),
            dma((7,)),
            dma((8,)),
            dma((8,)),
            dma((2,)),
            dma((2,)),
        ],
        compiler_params=pltpu.CompilerParams(
            collective_id=0, has_side_effects=True, vmem_limit_bytes=VMEM_LIMIT
        ),
    )(*[stay(part) for part in start], stay(eps_inv.reshape(OWN * OWN, depth)), *model)

    own, gram, tiles, kicks, raw = results

    return pl.pallas_call(
        functools.partial(finish_kernel, cell_count),
        out_shape=[
            jax.ShapeDtypeStruct(u_electric.shape, f32),
            jax.ShapeDtypeStruct(u_magnetic.shape, f32),
            jax.ShapeDtypeStruct((MS, 2, POLES, 3, 8, 8, depth), f32),
            jax.ShapeDtypeStruct((STEPS, 3), f32),
        ],
        in_specs=[vmem] * 5,
        out_specs=[any_spec] * 4,
        scratch_shapes=[
            pltpu.VMEM((STEPS, 3), f32),
            pltpu.VMEM((56, depth), f32),
            pltpu.VMEM((6, OWN, OWN, depth), f32),
            pltpu.VMEM((MS, 2, POLES, 3, 8, 8, depth), f32),
            dma((3 * MS,)),
            dma((3,)),
        ],
        compiler_params=pltpu.CompilerParams(vmem_limit_bytes=VMEM_LIMIT),
    )(raw, own, gram, tiles, kicks)


def solution(mesh):
    sizes = layout(mesh.shape["gx"], mesh.shape["gy"])
    placed = (
        P(None, "gx", "gy", None),
        P(None, "gx", "gy", None),
        P("gx", "gy", None),
        P(),
        P(),
        P(),
        P(),
    )
    return jax.shard_map(
        functools.partial(body, sizes),
        mesh=mesh,
        in_specs=placed,
        out_specs=(
            P(None, "gx", "gy", None),
            P(None, "gx", "gy", None),
            P(("gx", "gy"), None, None, None, None, None, None),
            P(),
        ),
        check_vma=False,
    )
```

```python
import functools

import jax
import jax.numpy as jnp
from jax import lax
from jax.experimental import pallas as pl
from jax.experimental.pallas import tpu as pltpu
from jax.sharding import PartitionSpec as P

POLES = 6
STEPS = 4
MS = 2
EPSILON = 1e-06
MESH = pl.DeviceIdType.MESH

EDGE = 2
OWN = 16
PADX = OWN + 2 * EDGE
PADY = 24
HIGH = 18
LOW = 20
STRIP = 16
FIELDS = 7
TO_PREVIOUS = [(f, 0) for f in range(FIELDS)] + [(f, 1) for f in (0, 2, 3, 4, 5, 6)]
TO_NEXT = [(f, 1) for f in range(FIELDS)] + [(f, 0) for f in (0, 1, 2, 3, 5)]
ROW = PADX * PADY
CORNER_ROWS = 32
CHUNK = 5
PAIRS = [(i, j) for i in range(STEPS + 1) for j in range(i, STEPS + 1)]
VMEM_LIMIT = 40 * 1024 * 1024


def layout(gx_size, gy_size):
    cores = 2
    z_size = min(8, gy_size // 2)
    return gx_size // cores, cores, gy_size // z_size, z_size


def rings(sizes):
    result = []
    for axis, size in (("x", sizes[0]), ("y", sizes[2]), ("z", sizes[3])):
        near = sorted({1 % size, size - 1} - {0})
        far = sorted({2 % size, (size - 2) % size} - {0}) if size > 3 else []
        result.append((axis, size, near, far))
    return result


def farthest_first(first, second):
    def hops(step, size):
        return min(step, size - step)

    steps = [(a, b) for a in range(first) for b in range(second) if a or b]
    return sorted(steps, key=lambda step: -hops(step[0], first) - hops(step[1], second))


def next_y(value):
    return pltpu.roll(value, PADY - 1, 0)


def prev_y(value):
    return pltpu.roll(value, 1, 0)


def next_z(value):
    return pltpu.roll(value, value.shape[1] - 1, 1)


def prev_z(value):
    return pltpu.roll(value, 1, 1)


def settle(buffer, semaphore):
    pltpu.make_async_copy(buffer, buffer, semaphore).wait()


def exchange_kernel(
    sizes,
    tiles,
    u_e,
    u_h,
    eps_in,
    metal_in,
    omega_in,
    gamma_in,
    strength_in,
    own_out,
    gram_out,
    tiles_out,
    kicks_out,
    raw,
    face_in,
    k1,
    k2,
    k3,
    k4,
    u,
    previous_out,
    previous_in,
    next_out,
    next_in,
    corner_out,
    corner_in,
    mask,
    acc_rows,
    sum_a,
    sum_b,
    metal,
    omega,
    gamma,
    strength,
    heard,
    load_sem,
    face_send,
    face_recv,
    stage_send,
    stage_recv,
):
    x_size, cores, y_size, z_size = sizes
    gx_size, gy_size = x_size * cores, y_size * z_size
    gx = lax.axis_index("gx")
    gy = lax.axis_index("gy")

    loads = [
        pltpu.make_async_copy(u_e, raw.at[pl.ds(0, 3)], load_sem.at[0]),
        pltpu.make_async_copy(u_h, raw.at[pl.ds(3, 3)], load_sem.at[1]),
        pltpu.make_async_copy(eps_in, raw.at[6], load_sem.at[2]),
        pltpu.make_async_copy(metal_in, metal, load_sem.at[3]),
        pltpu.make_async_copy(omega_in, omega, load_sem.at[4]),
        pltpu.make_async_copy(gamma_in, gamma, load_sem.at[5]),
        pltpu.make_async_copy(strength_in, strength, load_sem.at[6]),
    ]
    for load in loads:
        load.start()

    def ring(position, size):
        return [position] + [lax.rem(position + step, size) for step in range(1, size)]

    def device(x, core, y, z):
        return (x * cores + core, y * z_size + z)

    around_x = {0: gx, -1: lax.rem(gx + gx_size - 1, gx_size), 1: lax.rem(gx + 1, gx_size)}
    around_y = {0: gy, -1: lax.rem(gy + gy_size - 1, gy_size), 1: lax.rem(gy + 1, gy_size)}

    def neighbour(dx, dy):
        return (around_x[dx], around_y[dy])

    my_x, my_core = lax.div(gx, cores), lax.rem(gx, cores)
    my_y, my_z = lax.div(gy, z_size), lax.rem(gy, z_size)
    ring_x, ring_core = ring(my_x, x_size), ring(my_core, cores)
    ring_y, ring_z = ring(my_y, y_size), ring(my_z, z_size)

    def along(axis, step, core=0):
        return device(
            ring_x[step if axis == "x" else 0],
            ring_core[core],
            ring_y[step if axis == "y" else 0],
            ring_z[step if axis == "z" else 0],
        )

    def signal(semaphore, target):
        pl.semaphore_signal(semaphore, inc=1, device_id=target, device_id_type=MESH)

    beside = [(0, -1), (0, 1), (-1, 0), (1, 0)]
    near = [(axis, step, 0) for axis, _, steps, _ in rings(sizes) for step in steps]
    near += [(axis, step, 1) for axis, step, _ in near if axis == "z"]
    far = [(axis, step) for axis, _, _, steps in rings(sizes) for step in steps]
    barrier = pltpu.get_barrier_semaphore()
    for dx, dy in beside:
        signal(barrier, neighbour(dx, dy))
    for place in near:
        signal(barrier, along(*place))

    for load in loads:
        load.wait()

    for number, (f, layer) in enumerate(TO_PREVIOUS):
        previous_out[number] = raw[f, pl.ds(layer, OWN, stride=OWN), :]
    for number, (f, layer) in enumerate(TO_NEXT):
        next_out[number] = raw[f, pl.ds(OWN - 2 + layer, OWN, stride=OWN), :]
    corners = [(0, 0), (0, 1), (1, 0), (1, 1)]
    for number, (side_x, side_y) in enumerate(corners):
        for f in range(FIELDS):
            for layer in range(2):
                if side_x != side_y:
                    x = (0 if side_x == 0 else OWN - 2) + layer
                    y = 0 if side_y == 0 else OWN - 2
                    cells = raw[f, pl.ds(x * OWN + y, 2), :]
                    corner_out[number, pl.ds(f * 4 + layer * 2, 2), :] = cells
                elif layer == 0:
                    cell = 0 if side_x == 0 else OWN * OWN - 1
                    corner_out[number, pl.ds(f, 1), :] = raw[f, pl.ds(cell, 1), :]

    pl.semaphore_wait(barrier, len(beside) + len(near))

    copies = []

    def send(src, dst, device):
        number = len(copies)
        copy = pltpu.make_async_remote_copy(
            src_ref=src,
            dst_ref=dst,
            send_sem=face_send.at[number],
            recv_sem=face_recv.at[number],
            device_id=device,
            device_id_type=MESH,
        )
        copy.start()
        copies.append(copy)

    send(previous_out, previous_in, neighbour(0, -1))
    send(next_out, next_in, neighbour(0, 1))
    everything = pl.ds(0, FIELDS)
    layers = EDGE * OWN
    send(raw.at[everything, pl.ds(0, layers)], face_in.at[0], neighbour(-1, 0))
    send(raw.at[everything, pl.ds(OWN * OWN - layers, layers)], face_in.at[1], neighbour(1, 0))
    for dx, dy in beside[2:]:
        signal(heard.at[2], neighbour(dx, dy))
    for place in near:
        signal(heard.at[0], along(*place))

    tile_rows = [lax.rem(2 * gx + s - 1 + tiles[0], tiles[0]) for s in range(4)]
    tile_cols = [lax.rem(2 * gy + t - 1 + tiles[1], tiles[1]) for t in range(4)]
    place = lax.broadcasted_iota(jnp.int32, (8, 128), 0)
    for s in range(4):
        flag = [
            jnp.full((8, 128), metal[tile_rows[s], tile_cols[t]].astype(jnp.float32)) for t in range(4)
        ]
        mask[s, 0:8] = jnp.where(place < 6, flag[1], flag[2])
        mask[s, 8:16] = jnp.where(place < 2, flag[1], flag[2])
        beyond = jnp.where(place < 4, flag[3], flag[0])
        mask[s, 16:24] = jnp.where(place < 2, flag[2], jnp.where(place < 6, beyond, flag[1]))

    response = [jnp.float32(0.0)] * 3
    for p in range(POLES):
        g0 = strength[p]
        g1 = -gamma[p] * g0
        g2 = -(omega[p] * omega[p]) * g0 - gamma[p] * g1
        response = [response[0] + g0, response[1] + g1, response[2] + g2]

    def put_row(f, x, low, high):
        first = pl.multiple_of(x * PADY, 8)
        low_by_6, low_by_2 = pltpu.roll(low, 6, 0), pltpu.roll(low, 2, 0)
        high_by_6, high_by_2 = pltpu.roll(high, 6, 0), pltpu.roll(high, 2, 0)
        u[f, pl.ds(first, 8), :] = jnp.where(place < 6, low_by_6, high_by_6)
        u[f, pl.ds(first + 8, 8), :] = jnp.where(place < 2, low_by_2, high_by_2)
        u[f, pl.ds(first + 16, 8), :] = jnp.where(place < 4, high_by_2, low_by_6)

    def copy_own(x, carry):
        first = pl.multiple_of(x * OWN, 8)
        for f in range(FIELDS):
            put_row(f, x + EDGE, raw[f, pl.ds(first, 8), :], raw[f, pl.ds(first + 8, 8), :])
        return carry

    lax.fori_loop(0, OWN, copy_own, 0)

    class Padded:
        def __getitem__(self, at):
            f, x = at
            return u[f, pl.ds(pl.multiple_of(x * PADY, 8), PADY), :]

    start = Padded()
    states = [start, k1, k2, k3, k4]

    def electric(step, x):
        old = states[step - 1]
        hx, hy, hz = old[3, x], old[4, x], old[5, x]
        hy_back, hz_back = old[4, x - 1], old[5, x - 1]
        curl = [
            (hz - prev_y(hz)) - (hy - prev_z(hy)),
            (hx - prev_z(hx)) - (hz - hz_back),
            (hy - hy_back) - (hx - prev_y(hx)),
        ]
        eps = start[6, x]
        if step > 1:
            metal_here = mask[(x + 6) // 8]
            for c in range(3):
                current = response[step - 2] * start[c, x]
                for j in range(1, step - 1):
                    current = current + response[step - 2 - j] * states[j][c, x]
                curl[c] = curl[c] - metal_here * current
        return [eps * part for part in curl]

    def magnetic(step, x):
        old = states[step - 1]
        ex, ey, ez = old[0, x], old[1, x], old[2, x]
        ey_next, ez_next = old[1, x + 1], old[2, x + 1]
        return [
            (next_z(ey) - ey) - (next_y(ez) - ez),
            (ez_next - ez) - (next_z(ex) - ex),
            (next_y(ex) - ex) - (ey_next - ey),
        ]

    def write_rows(step, starts, shift):
        new = states[step]
        parts = [(x, electric(step, x), magnetic(step, x - shift)) for x in starts]
        for x, of_e, of_h in parts:
            for c in range(3):
                new[c, x] = of_e[c]
                new[3 + c, x - shift] = of_h[c]

    def interior(step, low, high, shift):
        rest = high - low - CHUNK
        chunks = -(-rest // CHUNK) + 1

        def rows(i, carry):
            first = low + (i * rest) // (chunks - 1)
            write_rows(step, [first + k for k in range(CHUNK)], shift)
            return carry

        lax.fori_loop(0, chunks, rows, 0)

    def edges(step, low, high, shift):
        write_rows(step, [low, low + 1, high, high + 1], shift)

    def state_at(j, c, x, first, count):
        if j == 0:
            return u[c, pl.ds(x * PADY + first, count), :]
        return states[j][c, x, pl.ds(first, count), :]

    def strip(j, c, x):
        if j == 0:
            return u[c, pl.ds(pl.multiple_of(x * PADY + STRIP, 8), 8), :]
        return states[j][c, x, pl.ds(STRIP, 8), :]

    def strip_prev(j, c, x, value):
        return jnp.where(place == 0, state_at(j, c, x, STRIP - 1, 1), pltpu.roll(value, 1, 0))

    def strip_next(j, c, x, value):
        return jnp.where(place == 7, state_at(j, c, x, 0, 1), pltpu.roll(value, 7, 0))

    def strip_electric(step, x):
        old = step - 1
        hx, hy, hz = (strip(old, c, x) for c in (3, 4, 5))
        hy_back, hz_back = strip(old, 4, x - 1), strip(old, 5, x - 1)
        curl = [
            (hz - strip_prev(old, 5, x, hz)) - (hy - prev_z(hy)),
            (hx - prev_z(hx)) - (hz - hz_back),
            (hy - hy_back) - (hx - strip_prev(old, 3, x, hx)),
        ]
        if step > 1:
            metal_here = mask[(x + 6) // 8, pl.ds(STRIP, 8), :]
            for c in range(3):
                current = response[step - 2] * strip(0, c, x)
                for j in range(1, step - 1):
                    current = current + response[step - 2 - j] * strip(j, c, x)
                curl[c] = curl[c] - metal_here * current
        eps = strip(0, 6, x)
        return [eps * part for part in curl]

    def strip_magnetic(step, x):
        old = step - 1
        ex, ey, ez = (strip(old, c, x) for c in (0, 1, 2))
        ey_next, ez_next = strip(old, 1, x + 1), strip(old, 2, x + 1)
        return [
            (next_z(ey) - ey) - (strip_next(old, 2, x, ez) - ez),
            (ez_next - ez) - (next_z(ex) - ex),
            (strip_next(old, 0, x, ex) - ex) - (ey_next - ey),
        ]

    def write_strips(step, starts, shift):
        new = states[step]
        parts = [(x, strip_electric(step, x), strip_magnetic(step, x - shift)) for x in starts]
        for x, of_e, of_h in parts:
            for c in range(3):
                new[c, x, pl.ds(STRIP, 8), :] = of_e[c]
                new[3 + c, x - shift, pl.ds(STRIP, 8), :] = of_h[c]

    def interior_strips(step, low, high, shift):
        write_strips(step, list(range(low, high)), shift)

    def edge_strips(step, low, high, shift):
        write_strips(step, [low, low + 1, high, high + 1], shift)

    zero = jnp.zeros((8, 128), jnp.float32)

    def products(first, x, sums):
        sums = list(sums)
        cells = pl.ds(first, 8)
        for c in range(6):
            values = [u[c, pl.ds(pl.multiple_of(x * PADY + first, 8), 8), :]]
            values += [state[c, x, cells, :] for state in states[1:]]
            for number, (i, j) in enumerate(PAIRS):
                sums[number] = sums[number] + values[i] * values[j]
        return tuple(sums)

    ends = jnp.logical_or(place < 2, place >= 6)

    def strip_products(pairs, sums):
        sums = list(sums)
        for x, other in pairs:
            for c in range(6):
                values = [
                    jnp.where(ends, strip(j, c, x), pltpu.roll(strip(j, c, other), 4, 0))
                    for j in range(STEPS + 1)
                ]
                for number, (i, j) in enumerate(PAIRS):
                    sums[number] = sums[number] + values[i] * values[j]
        return tuple(sums)

    def interior_products(first, sums):
        return lax.fori_loop(
            EDGE + 2, EDGE + OWN - 2, lambda x, sums: products(first, x, sums), sums
        )

    def edge_products(first, sums):
        return lax.fori_loop(
            0,
            2 * EDGE,
            lambda i, sums: products(first, EDGE + i + i // 2 * (OWN - 4), sums),
            sums,
        )

    def keep(sums, wanted, into):
        for number, part in enumerate(sums):
            at = pl.ds(8 * number, 8)
            part = jnp.where(wanted, part, 0.0)
            acc_rows[at, :] = part + acc_rows[at, :] if into else part

    none = (zero,) * len(PAIRS)
    interior(1, EDGE + 1, EDGE + OWN, 1)
    interior(2, EDGE + 1, EDGE + OWN - 1, 0)
    interior(3, EDGE + 2, EDGE + OWN - 1, 1)
    interior(4, EDGE + 2, EDGE + OWN - 2, 0)
    keep(interior_products(0, none), place < 6, False)
    keep(interior_products(8, none), place >= 2, True)
    acc_rows[pl.ds(8 * len(PAIRS), 8), :] = zero
    pl.semaphore_wait(heard.at[2], len(beside[2:]))
    for number, (side_x, side_y) in enumerate(corners):
        rows = pl.ds(0, 8 if side_x == side_y else CORNER_ROWS)
        send(
            corner_out.at[number, rows],
            corner_in.at[number, rows],
            neighbour(2 * side_x - 1, 2 * side_y - 1),
        )
    pl.semaphore_wait(heard.at[0], len(near))
    for axis, step in far:
        signal(heard.at[1], along(axis, step))

    for copy in copies[2:4]:
        copy.wait_recv()
    for f in range(FIELDS):
        for side, first in ((0, EDGE + OWN), (1, 0)):
            for layer in range(2):
                low = face_in[side, f, pl.ds(layer * OWN, 8), :]
                high = face_in[side, f, pl.ds(layer * OWN + 8, 8), :]
                put_row(f, first + layer, low, high)
    edges(1, 1, EDGE + OWN, 1)
    edges(2, 1, EDGE + OWN - 1, 0)
    edges(3, EDGE, EDGE + OWN - 1, 1)
    edges(4, EDGE, EDGE + OWN - 2, 0)
    keep(edge_products(0, none), place < 6, True)
    keep(edge_products(8, none), place >= 2, True)

    for copy in copies[:2]:
        copy.wait_recv()
    for number, (f, layer) in enumerate(TO_PREVIOUS):
        u[f, pl.ds(EDGE * PADY + HIGH + layer, OWN, stride=PADY), :] = previous_in[number]
    for number, (f, layer) in enumerate(TO_NEXT):
        u[f, pl.ds(EDGE * PADY + LOW + layer, OWN, stride=PADY), :] = next_in[number]
    interior_strips(1, EDGE + 1, EDGE + OWN, 1)
    interior_strips(2, EDGE + 1, EDGE + OWN - 1, 0)
    interior_strips(3, EDGE + 2, EDGE + OWN - 1, 1)
    interior_strips(4, EDGE + 2, EDGE + OWN - 2, 0)
    sums = lax.fori_loop(
        0,
        3,
        lambda i, sums: strip_products([(4 + 4 * i, 5 + 4 * i), (6 + 4 * i, 7 + 4 * i)], sums),
        none,
    )

    for copy in copies[4:]:
        copy.wait_recv()
    for number, (side_x, side_y) in enumerate(corners):
        for f in range(FIELDS):
            for layer in range(2):
                x = (EDGE + OWN if side_x == 0 else 0) + layer
                y = HIGH if side_y == 0 else LOW
                if side_x != side_y:
                    source = corner_in[number, pl.ds(f * 4 + layer * 2, 2), :]
                    u[f, pl.ds(x * PADY + y, 2), :] = source
                elif layer == side_x:
                    u[f, pl.ds(x * PADY + y + layer, 1), :] = corner_in[number, pl.ds(f, 1), :]
    edge_strips(1, 1, EDGE + OWN, 1)
    edge_strips(2, 1, EDGE + OWN - 1, 0)
    edge_strips(3, EDGE, EDGE + OWN - 1, 1)
    edge_strips(4, EDGE, EDGE + OWN - 2, 0)
    keep(strip_products([(2, 3), (16, 17)], sums), place < 8, True)

    total = acc_rows[pl.ds(0, 16, stride=8), :]
    for s in range(1, 8):
        total = total + acc_rows[pl.ds(s, 16, stride=8), :]
    diagonal = lax.broadcasted_iota(jnp.int32, (16, 128), 0) == lax.broadcasted_iota(jnp.int32, (16, 128), 1)

    def to_row(column):
        return jnp.sum(jnp.where(diagonal, column, 0.0), axis=0, keepdims=True)

    def gather_metal():
        flags = [metal[tile_rows[1 + t // 2], tile_cols[1 + t % 2]] for t in range(4)]
        present = [flag.astype(jnp.float32) for flag in flags]
        before = jnp.float32(0.0)
        chosen = [[None] * 4 for _ in range(MS)]
        for t in range(4):
            taken = [present[t] * (1.0 - before), present[t] * before]
            before = before + present[t]
            for slot in range(MS):
                chosen[slot][t] = taken[slot]

        def rows(x, carry):
            for c in range(3):
                for j in range(STEPS):
                    parts = []
                    for t in range(4):
                        at = 8 * (t // 2) + x
                        y = 8 * (t % 2)
                        if j == 0:
                            parts.append(raw[c, pl.ds(pl.multiple_of(at * OWN + y, 8), 8), :])
                        else:
                            parts.append(own_out[j - 1, c, at, pl.ds(y, 8), :])
                    for slot in range(MS):
                        value = chosen[slot][0] * parts[0]
                        for t in range(1, 4):
                            value = value + chosen[slot][t] * parts[t]
                        tiles_out[slot, j, c, x] = value
            return carry

        lax.fori_loop(0, 8, rows, 0)
        for p in range(POLES):
            kicks = [strength[p]]
            kicks.append(-gamma[p] * kicks[0])
            for k in range(2, STEPS):
                kicks.append(-(omega[p] * omega[p]) * kicks[k - 2] - gamma[p] * kicks[k - 1])
            for k in range(STEPS):
                kicks_out[pl.ds(p * STEPS + k, 1), :] = jnp.full((1, 128), kicks[k])

    def order_own():
        def rows(x, carry):
            for j, state in enumerate(states[1:]):
                for c in range(6):
                    tile = [state[c, x + EDGE, pl.ds(8 * t, 8), :] for t in range(3)]
                    own_out[j, c, x, pl.ds(0, 8), :] = jnp.where(
                        place < 2, pltpu.roll(tile[2], 2, 0), pltpu.roll(tile[0], 2, 0)
                    )
                    own_out[j, c, x, pl.ds(8, 8), :] = jnp.where(
                        place < 6, pltpu.roll(tile[1], 6, 0), pltpu.roll(tile[2], 6, 0)
                    )
            return carry

        lax.fori_loop(0, OWN, rows, 0)

    row = to_row(jnp.sum(total, axis=1, keepdims=True))
    if far:
        pl.semaphore_wait(heard.at[1], len(far))
    me_a = my_core * z_size + my_z
    me_b = my_x * y_size + my_y
    targets_a = [
        device(my_x, ring_core[c], my_y, ring_z[z]) for c, z in farthest_first(cores, z_size)
    ]
    targets_b = [
        device(ring_x[x], my_core, ring_y[y], my_z) for x, y in farthest_first(x_size, y_size)
    ]
    for stage, (slots, me, targets) in enumerate(((sum_a, me_a, targets_a), (sum_b, me_b, targets_b))):
        slots[me] = row
        for target in targets:
            pltpu.make_async_remote_copy(
                src_ref=slots.at[me],
                dst_ref=slots.at[me],
                send_sem=stage_send.at[stage],
                recv_sem=stage_recv.at[stage],
                device_id=target,
                device_id_type=MESH,
            ).start()
        if stage == 0:
            order_own()
        else:
            gather_metal()
        settle(slots.at[pl.ds(0, len(targets))], stage_recv.at[stage])
        row = slots[0]
        for member in range(1, len(targets) + 1):
            row = row + slots[member]
    gram_out[...] = jnp.broadcast_to(
        jnp.sum(jnp.where(diagonal, row, 0.0), axis=1, keepdims=True), (16, 128)
    )

    for copy in copies:
        copy.wait_send()
    for stage, (slots, targets) in enumerate(((sum_a, targets_a), (sum_b, targets_b))):
        settle(slots.at[pl.ds(0, len(targets))], stage_send.at[stage])


def finish_kernel(
    cell_count,
    k0,
    own,
    gram,
    tiles,
    kicks,
    out_e,
    out_h,
    out_poles,
    out_coefficients,
    coefficients,
    table,
    fields,
    poles,
    pole_sem,
    store_sem,
):
    stores = []

    def store(src, dst):
        copy = pltpu.make_async_copy(src, dst, store_sem.at[len(stores)])
        copy.start()
        stores.append(copy)

    inner = {}
    for number, (i, j) in enumerate(PAIRS):
        inner[i, j] = inner[j, i] = gram[pl.ds(number, 1), :] * (1.0 / cell_count)
    unit = 1.0 / jnp.sqrt(inner[0, 0] + EPSILON)
    weights = [unit]
    lane = lax.broadcasted_iota(jnp.int32, (1, 128), 1)
    for step in range(1, STEPS + 1):
        image = [None] + weights

        def total(terms):
            return functools.reduce(jnp.add, terms)

        along_q = unit * total([image[j] * inner[0, j] for j in range(1, step + 1)])
        rest = [-along_q * unit] + image[1:]
        along_v = jnp.zeros_like(unit)
        if step > 1:
            along_v = total(
                [
                    image[j] * total([weights[i] * inner[i, j] for i in range(step)])
                    for j in range(1, step + 1)
                ]
            )
            for i in range(step):
                rest[i] = rest[i] - along_v * weights[i]
        squared = total(
            [rest[i] * total([rest[j] * inner[i, j] for j in range(step + 1)]) for i in range(step + 1)]
        )
        norm = jnp.sqrt(jnp.maximum(squared, 0.0) + EPSILON)
        scale = 1.0 / norm
        weights = [part * scale for part in rest]
        line = jnp.where(lane == 0, along_q, jnp.where(lane == 1, along_v, norm))
        coefficients[pl.ds(step - 1, 1), :] = line[:, :3]

    store(coefficients, out_coefficients)

    for p in range(POLES):
        kick = [kicks[pl.ds(p * STEPS + k, 1), :] for k in range(STEPS)]
        for j in range(STEPS):
            parts = [weights[k] * kick[k - 1 - j] for k in range(j + 1, STEPS + 1)]
            table[pl.ds(p * 8 + j, 1), :] = functools.reduce(jnp.add, parts)
        for j in range(STEPS - 1):
            parts = [weights[k] * kick[k - 2 - j] for k in range(j + 2, STEPS + 1)]
            table[pl.ds(p * 8 + 4 + j, 1), :] = functools.reduce(jnp.add, parts)
    for j in range(STEPS + 1):
        table[pl.ds(48 + j, 1), :] = weights[j]

    def entry(number):
        return jnp.broadcast_to(table[pl.ds(number, 1), :], (8, 128))

    def pole_part(i):
        return (i // 3, pl.ds(0, 2), pl.ds(0, POLES), i % 3)

    def pole_cells(i, carry):
        slot, c = i // 3, i % 3
        for x in range(8):
            field = [tiles[slot, j, c, x] for j in range(STEPS)]
            for p in range(POLES):
                poles[slot, 1, p, c, x] = functools.reduce(
                    jnp.add, [entry(p * 8 + j) * field[j] for j in range(STEPS)]
                )
                poles[slot, 0, p, c, x] = functools.reduce(
                    jnp.add, [entry(p * 8 + 4 + j) * field[j] for j in range(STEPS - 1)]
                )
        pltpu.make_async_copy(
            poles.at[pole_part(i)], out_poles.at[pole_part(i)], pole_sem.at[i]
        ).start()
        return carry

    lax.fori_loop(0, 3 * MS, pole_cells, 0)

    for half, out in enumerate((out_e, out_h)):

        def field_cells(i, carry):
            for x in [4 * i + k for k in range(4)]:
                for c in range(3 * half, 3 * half + 3):
                    cells = pl.ds(pl.multiple_of(x * OWN, 8), OWN)
                    value = table[pl.ds(48, 1), :] * k0[c, cells, :]
                    for j in range(STEPS):
                        value = value + table[pl.ds(49 + j, 1), :] * own[j, c, x]
                    fields[c, x] = value
            return carry

        lax.fori_loop(0, OWN // 4, field_cells, 0)
        store(fields.at[pl.ds(3 * half, 3)], out)
    for i in range(3 * MS):
        pltpu.make_async_copy(poles.at[pole_part(i)], out_poles.at[pole_part(i)], pole_sem.at[i]).wait()
    for copy in stores:
        copy.wait()


def body(sizes, u_electric, u_magnetic, eps_inv, metal_map, pole_omega, pole_gamma, pole_strength):
    depth = u_electric.shape[3]
    cell_count = 6.0 * OWN * OWN * depth * sizes[0] * sizes[1] * sizes[2] * sizes[3]
    f32 = jnp.float32
    any_spec = pl.BlockSpec(memory_space=pl.ANY)
    hbm = pl.BlockSpec(memory_space=pltpu.HBM)
    vmem = pl.BlockSpec(memory_space=pltpu.VMEM)
    a_size = sizes[1] * sizes[3]
    b_size = sizes[0] * sizes[2]

    def stay(value):
        return pltpu.with_memory_space_constraint(value, pltpu.HBM)

    start = [u_electric.reshape(3, OWN * OWN, depth), u_magnetic.reshape(3, OWN * OWN, depth)]
    model = [stay(part) for part in (metal_map, pole_omega, pole_gamma, pole_strength)]
    dma = pltpu.SemaphoreType.DMA
    results = pl.pallas_call(
        functools.partial(exchange_kernel, sizes, metal_map.shape),
        out_shape=[
            jax.ShapeDtypeStruct((STEPS, 6, OWN, OWN, depth), f32),
            jax.ShapeDtypeStruct((16, depth), f32),
            jax.ShapeDtypeStruct((MS, STEPS, 3, 8, 8, depth), f32),
            jax.ShapeDtypeStruct((POLES * STEPS, depth), f32),
            jax.ShapeDtypeStruct((FIELDS, OWN * OWN, depth), f32),
        ],
        in_specs=[hbm] * 7,
        out_specs=[vmem] * 5,
        scratch_shapes=[
            pltpu.VMEM((2, FIELDS, EDGE * OWN, depth), f32),
            *[pltpu.VMEM((6, PADX, PADY, depth), f32)] * STEPS,
            pltpu.VMEM((FIELDS, ROW, depth), f32),
            pltpu.VMEM((len(TO_PREVIOUS), OWN, depth), f32),
            pltpu.VMEM((len(TO_PREVIOUS), OWN, depth), f32),
            pltpu.VMEM((len(TO_NEXT), OWN, depth), f32),
            pltpu.VMEM((len(TO_NEXT), OWN, depth), f32),
            pltpu.VMEM((4, CORNER_ROWS, depth), f32),
            pltpu.VMEM((4, CORNER_ROWS, depth), f32),
            pltpu.VMEM((4, PADY, depth), f32),
            pltpu.VMEM((128, depth), f32),
            pltpu.VMEM((a_size, 1, depth), f32),
            pltpu.VMEM((b_size, 1, depth), f32),
            pltpu.SMEM(metal_map.shape, jnp.int32),
            pltpu.SMEM((POLES,), f32),
            pltpu.SMEM((POLES,), f32),
            pltpu.SMEM((POLES,), f32),
            pltpu.SemaphoreType.REGULAR((3,)),
            dma((7,)),
            dma((8,)),
            dma((8,)),
            dma((2,)),
            dma((2,)),
        ],
        compiler_params=pltpu.CompilerParams(
            collective_id=0, has_side_effects=True, vmem_limit_bytes=VMEM_LIMIT
        ),
    )(*[stay(part) for part in start], stay(eps_inv.reshape(OWN * OWN, depth)), *model)

    own, gram, tiles, kicks, raw = results

    return pl.pallas_call(
        functools.partial(finish_kernel, cell_count),
        out_shape=[
            jax.ShapeDtypeStruct(u_electric.shape, f32),
            jax.ShapeDtypeStruct(u_magnetic.shape, f32),
            jax.ShapeDtypeStruct((MS, 2, POLES, 3, 8, 8, depth), f32),
            jax.ShapeDtypeStruct((STEPS, 3), f32),
        ],
        in_specs=[vmem] * 5,
        out_specs=[any_spec] * 4,
        scratch_shapes=[
            pltpu.VMEM((STEPS, 3), f32),
            pltpu.VMEM((56, depth), f32),
            pltpu.VMEM((6, OWN, OWN, depth), f32),
            pltpu.VMEM((MS, 2, POLES, 3, 8, 8, depth), f32),
            dma((3 * MS,)),
            dma((3,)),
        ],
        compiler_params=pltpu.CompilerParams(vmem_limit_bytes=VMEM_LIMIT),
    )(raw, own, gram, tiles, kicks)


def solution(mesh):
    sizes = layout(mesh.shape["gx"], mesh.shape["gy"])
    placed = (
        P(None, "gx", "gy", None),
        P(None, "gx", "gy", None),
        P("gx", "gy", None),
        P(),
        P(),
        P(),
        P(),
    )
    return jax.shard_map(
        functools.partial(body, sizes),
        mesh=mesh,
        in_specs=placed,
        out_specs=(
            P(None, "gx", "gy", None),
            P(None, "gx", "gy", None),
            P(("gx", "gy"), None, None, None, None, None, None),
            P(),
        ),
        check_vma=False,
    )
```

```python
import functools

import jax
import jax.numpy as jnp
from jax import lax
from jax.experimental import pallas as pl
from jax.experimental.pallas import tpu as pltpu
from jax.sharding import PartitionSpec as P

POLES = 6
STEPS = 4
MS = 2
EPSILON = 1e-06
MESH = pl.DeviceIdType.MESH

EDGE = 2
OWN = 16
PADX = OWN + 2 * EDGE
PADY = 24
HIGH = 18
LOW = 20
STRIP = 16
FIELDS = 7
TO_PREVIOUS = [(f, 0) for f in range(FIELDS)] + [(f, 1) for f in (0, 2, 3, 4, 5, 6)]
TO_NEXT = [(f, 1) for f in range(FIELDS)] + [(f, 0) for f in (0, 1, 2, 3, 5)]
ROW = PADX * PADY
CORNER_ROWS = 32
CHUNK = 5
PAIRS = [(i, j) for i in range(STEPS + 1) for j in range(i, STEPS + 1)]
VMEM_LIMIT = 40 * 1024 * 1024


def layout(gx_size, gy_size):
    cores = 2
    z_size = min(8, gy_size // 2)
    return gx_size // cores, cores, gy_size // z_size, z_size


def rings(sizes):
    result = []
    for axis, size in (("x", sizes[0]), ("y", sizes[2]), ("z", sizes[3])):
        near = sorted({1 % size, size - 1} - {0})
        far = sorted({2 % size, (size - 2) % size} - {0}) if size > 3 else []
        result.append((axis, size, near, far))
    return result


def farthest_first(first, second):
    def hops(step, size):
        return min(step, size - step)

    steps = [(a, b) for a in range(first) for b in range(second) if a or b]
    return sorted(steps, key=lambda step: -hops(step[0], first) - hops(step[1], second))


def next_y(value):
    return pltpu.roll(value, PADY - 1, 0)


def prev_y(value):
    return pltpu.roll(value, 1, 0)


def next_z(value):
    return pltpu.roll(value, value.shape[1] - 1, 1)


def prev_z(value):
    return pltpu.roll(value, 1, 1)


def settle(buffer, semaphore):
    pltpu.make_async_copy(buffer, buffer, semaphore).wait()


def exchange_kernel(
    sizes,
    tiles,
    u_e,
    u_h,
    eps_in,
    metal_in,
    omega_in,
    gamma_in,
    strength_in,
    own_out,
    gram_out,
    tiles_out,
    kicks_out,
    raw,
    face_in,
    k1,
    k2,
    k3,
    k4,
    u,
    previous_out,
    previous_in,
    next_out,
    next_in,
    corner_out,
    corner_in,
    mask,
    acc_rows,
    sum_a,
    sum_b,
    metal,
    omega,
    gamma,
    strength,
    heard,
    load_sem,
    face_send,
    face_recv,
    stage_send,
    stage_recv,
):
    x_size, cores, y_size, z_size = sizes
    gx_size, gy_size = x_size * cores, y_size * z_size
    gx = lax.axis_index("gx")
    gy = lax.axis_index("gy")

    loads = [
        pltpu.make_async_copy(u_e, raw.at[pl.ds(0, 3)], load_sem.at[0]),
        pltpu.make_async_copy(u_h, raw.at[pl.ds(3, 3)], load_sem.at[1]),
        pltpu.make_async_copy(eps_in, raw.at[6], load_sem.at[2]),
        pltpu.make_async_copy(metal_in, metal, load_sem.at[3]),
        pltpu.make_async_copy(omega_in, omega, load_sem.at[4]),
        pltpu.make_async_copy(gamma_in, gamma, load_sem.at[5]),
        pltpu.make_async_copy(strength_in, strength, load_sem.at[6]),
    ]
    for load in loads:
        load.start()

    def ring(position, size):
        return [position] + [lax.rem(position + step, size) for step in range(1, size)]

    def device(x, core, y, z):
        return (x * cores + core, y * z_size + z)

    around_x = {0: gx, -1: lax.rem(gx + gx_size - 1, gx_size), 1: lax.rem(gx + 1, gx_size)}
    around_y = {0: gy, -1: lax.rem(gy + gy_size - 1, gy_size), 1: lax.rem(gy + 1, gy_size)}

    def neighbour(dx, dy):
        return (around_x[dx], around_y[dy])

    my_x, my_core = lax.div(gx, cores), lax.rem(gx, cores)
    my_y, my_z = lax.div(gy, z_size), lax.rem(gy, z_size)
    ring_x, ring_core = ring(my_x, x_size), ring(my_core, cores)
    ring_y, ring_z = ring(my_y, y_size), ring(my_z, z_size)

    def along(axis, step, core=0):
        return device(
            ring_x[step if axis == "x" else 0],
            ring_core[core],
            ring_y[step if axis == "y" else 0],
            ring_z[step if axis == "z" else 0],
        )

    def signal(semaphore, target):
        pl.semaphore_signal(semaphore, inc=1, device_id=target, device_id_type=MESH)

    beside = [(0, -1), (0, 1), (-1, 0), (1, 0)]
    near = [(axis, step, 0) for axis, _, steps, _ in rings(sizes) for step in steps]
    near += [(axis, step, 1) for axis, step, _ in near if axis == "z"]
    far = [(axis, step) for axis, _, _, steps in rings(sizes) for step in steps]
    barrier = pltpu.get_barrier_semaphore()
    for dx, dy in beside:
        signal(barrier, neighbour(dx, dy))
    for place in near:
        signal(barrier, along(*place))

    for load in loads:
        load.wait()

    for number, (f, layer) in enumerate(TO_PREVIOUS):
        previous_out[number] = raw[f, pl.ds(layer, OWN, stride=OWN), :]
    for number, (f, layer) in enumerate(TO_NEXT):
        next_out[number] = raw[f, pl.ds(OWN - 2 + layer, OWN, stride=OWN), :]
    corners = [(0, 0), (0, 1), (1, 0), (1, 1)]
    for number, (side_x, side_y) in enumerate(corners):
        for f in range(FIELDS):
            for layer in range(2):
                if side_x != side_y:
                    x = (0 if side_x == 0 else OWN - 2) + layer
                    y = 0 if side_y == 0 else OWN - 2
                    cells = raw[f, pl.ds(x * OWN + y, 2), :]
                    corner_out[number, pl.ds(f * 4 + layer * 2, 2), :] = cells
                elif layer == 0:
                    cell = 0 if side_x == 0 else OWN * OWN - 1
                    corner_out[number, pl.ds(f, 1), :] = raw[f, pl.ds(cell, 1), :]

    pl.semaphore_wait(barrier, len(beside) + len(near))

    copies = []

    def send(src, dst, device):
        number = len(copies)
        copy = pltpu.make_async_remote_copy(
            src_ref=src,
            dst_ref=dst,
            send_sem=face_send.at[number],
            recv_sem=face_recv.at[number],
            device_id=device,
            device_id_type=MESH,
        )
        copy.start()
        copies.append(copy)

    send(previous_out, previous_in, neighbour(0, -1))
    send(next_out, next_in, neighbour(0, 1))
    everything = pl.ds(0, FIELDS)
    layers = EDGE * OWN
    send(raw.at[everything, pl.ds(0, layers)], face_in.at[0], neighbour(-1, 0))
    send(raw.at[everything, pl.ds(OWN * OWN - layers, layers)], face_in.at[1], neighbour(1, 0))
    for dx, dy in beside[2:]:
        signal(heard.at[2], neighbour(dx, dy))
    for place in near:
        signal(heard.at[0], along(*place))

    tile_rows = [lax.rem(2 * gx + s - 1 + tiles[0], tiles[0]) for s in range(4)]
    tile_cols = [lax.rem(2 * gy + t - 1 + tiles[1], tiles[1]) for t in range(4)]
    place = lax.broadcasted_iota(jnp.int32, (8, 128), 0)
    for s in range(4):
        flag = [
            jnp.full((8, 128), metal[tile_rows[s], tile_cols[t]].astype(jnp.float32)) for t in range(4)
        ]
        mask[s, 0:8] = jnp.where(place < 6, flag[1], flag[2])
        mask[s, 8:16] = jnp.where(place < 2, flag[1], flag[2])
        beyond = jnp.where(place < 4, flag[3], flag[0])
        mask[s, 16:24] = jnp.where(place < 2, flag[2], jnp.where(place < 6, beyond, flag[1]))

    response = [jnp.float32(0.0)] * 3
    for p in range(POLES):
        g0 = strength[p]
        g1 = -gamma[p] * g0
        g2 = -(omega[p] * omega[p]) * g0 - gamma[p] * g1
        response = [response[0] + g0, response[1] + g1, response[2] + g2]

    def put_row(f, x, low, high):
        first = pl.multiple_of(x * PADY, 8)
        low_by_6, low_by_2 = pltpu.roll(low, 6, 0), pltpu.roll(low, 2, 0)
        high_by_6, high_by_2 = pltpu.roll(high, 6, 0), pltpu.roll(high, 2, 0)
        u[f, pl.ds(first, 8), :] = jnp.where(place < 6, low_by_6, high_by_6)
        u[f, pl.ds(first + 8, 8), :] = jnp.where(place < 2, low_by_2, high_by_2)
        u[f, pl.ds(first + 16, 8), :] = jnp.where(place < 4, high_by_2, low_by_6)

    def copy_own(x, carry):
        first = pl.multiple_of(x * OWN, 8)
        for f in range(FIELDS):
            put_row(f, x + EDGE, raw[f, pl.ds(first, 8), :], raw[f, pl.ds(first + 8, 8), :])
        return carry

    lax.fori_loop(0, OWN, copy_own, 0)

    class Padded:
        def __getitem__(self, at):
            f, x = at
            return u[f, pl.ds(pl.multiple_of(x * PADY, 8), PADY), :]

    start = Padded()
    states = [start, k1, k2, k3, k4]

    def electric(step, x):
        old = states[step - 1]
        hx, hy, hz = old[3, x], old[4, x], old[5, x]
        hy_back, hz_back = old[4, x - 1], old[5, x - 1]
        curl = [
            (hz - prev_y(hz)) - (hy - prev_z(hy)),
            (hx - prev_z(hx)) - (hz - hz_back),
            (hy - hy_back) - (hx - prev_y(hx)),
        ]
        eps = start[6, x]
        if step > 1:
            metal_here = mask[(x + 6) // 8]
            for c in range(3):
                current = response[step - 2] * start[c, x]
                for j in range(1, step - 1):
                    current = current + response[step - 2 - j] * states[j][c, x]
                curl[c] = curl[c] - metal_here * current
        return [eps * part for part in curl]

    def magnetic(step, x):
        old = states[step - 1]
        ex, ey, ez = old[0, x], old[1, x], old[2, x]
        ey_next, ez_next = old[1, x + 1], old[2, x + 1]
        return [
            (next_z(ey) - ey) - (next_y(ez) - ez),
            (ez_next - ez) - (next_z(ex) - ex),
            (next_y(ex) - ex) - (ey_next - ey),
        ]

    def write_rows(step, starts, shift):
        new = states[step]
        parts = [(x, electric(step, x), magnetic(step, x - shift)) for x in starts]
        for x, of_e, of_h in parts:
            for c in range(3):
                new[c, x] = of_e[c]
                new[3 + c, x - shift] = of_h[c]

    def interior(step, low, high, shift):
        rest = high - low - CHUNK
        chunks = -(-rest // CHUNK) + 1

        def rows(i, carry):
            first = low + (i * rest) // (chunks - 1)
            write_rows(step, [first + k for k in range(CHUNK)], shift)
            return carry

        lax.fori_loop(0, chunks, rows, 0)

    def edges(step, low, high, shift):
        write_rows(step, [low, low + 1, high, high + 1], shift)

    def state_at(j, c, x, first, count):
        if j == 0:
            return u[c, pl.ds(x * PADY + first, count), :]
        return states[j][c, x, pl.ds(first, count), :]

    def strip(j, c, x):
        if j == 0:
            return u[c, pl.ds(pl.multiple_of(x * PADY + STRIP, 8), 8), :]
        return states[j][c, x, pl.ds(STRIP, 8), :]

    def strip_prev(j, c, x, value):
        return jnp.where(place == 0, state_at(j, c, x, STRIP - 1, 1), pltpu.roll(value, 1, 0))

    def strip_next(j, c, x, value):
        return jnp.where(place == 7, state_at(j, c, x, 0, 1), pltpu.roll(value, 7, 0))

    def strip_electric(step, x):
        old = step - 1
        hx, hy, hz = (strip(old, c, x) for c in (3, 4, 5))
        hy_back, hz_back = strip(old, 4, x - 1), strip(old, 5, x - 1)
        curl = [
            (hz - strip_prev(old, 5, x, hz)) - (hy - prev_z(hy)),
            (hx - prev_z(hx)) - (hz - hz_back),
            (hy - hy_back) - (hx - strip_prev(old, 3, x, hx)),
        ]
        if step > 1:
            metal_here = mask[(x + 6) // 8, pl.ds(STRIP, 8), :]
            for c in range(3):
                current = response[step - 2] * strip(0, c, x)
                for j in range(1, step - 1):
                    current = current + response[step - 2 - j] * strip(j, c, x)
                curl[c] = curl[c] - metal_here * current
        eps = strip(0, 6, x)
        return [eps * part for part in curl]

    def strip_magnetic(step, x):
        old = step - 1
        ex, ey, ez = (strip(old, c, x) for c in (0, 1, 2))
        ey_next, ez_next = strip(old, 1, x + 1), strip(old, 2, x + 1)
        return [
            (next_z(ey) - ey) - (strip_next(old, 2, x, ez) - ez),
            (ez_next - ez) - (next_z(ex) - ex),
            (strip_next(old, 0, x, ex) - ex) - (ey_next - ey),
        ]

    def write_strips(step, starts, shift):
        new = states[step]
        parts = [(x, strip_electric(step, x), strip_magnetic(step, x - shift)) for x in starts]
        for x, of_e, of_h in parts:
            for c in range(3):
                new[c, x, pl.ds(STRIP, 8), :] = of_e[c]
                new[3 + c, x - shift, pl.ds(STRIP, 8), :] = of_h[c]

    def interior_strips(step, low, high, shift):
        write_strips(step, list(range(low, high)), shift)

    def edge_strips(step, low, high, shift):
        write_strips(step, [low, low + 1, high, high + 1], shift)

    zero = jnp.zeros((8, 128), jnp.float32)

    def products(first, x, sums):
        sums = list(sums)
        cells = pl.ds(first, 8)
        for c in range(6):
            values = [u[c, pl.ds(pl.multiple_of(x * PADY + first, 8), 8), :]]
            values += [state[c, x, cells, :] for state in states[1:]]
            for number, (i, j) in enumerate(PAIRS):
                sums[number] = sums[number] + values[i] * values[j]
        return tuple(sums)

    ends = jnp.logical_or(place < 2, place >= 6)

    def strip_products(pairs, sums):
        sums = list(sums)
        for x, other in pairs:
            for c in range(6):
                values = [
                    jnp.where(ends, strip(j, c, x), pltpu.roll(strip(j, c, other), 4, 0))
                    for j in range(STEPS + 1)
                ]
                for number, (i, j) in enumerate(PAIRS):
                    sums[number] = sums[number] + values[i] * values[j]
        return tuple(sums)

    def interior_products(first, sums):
        return lax.fori_loop(
            EDGE + 2, EDGE + OWN - 2, lambda x, sums: products(first, x, sums), sums
        )

    def edge_products(first, sums):
        return lax.fori_loop(
            0,
            2 * EDGE,
            lambda i, sums: products(first, EDGE + i + i // 2 * (OWN - 4), sums),
            sums,
        )

    def keep(sums, wanted, into):
        for number, part in enumerate(sums):
            at = pl.ds(8 * number, 8)
            part = jnp.where(wanted, part, 0.0)
            acc_rows[at, :] = part + acc_rows[at, :] if into else part

    none = (zero,) * len(PAIRS)
    interior(1, EDGE + 1, EDGE + OWN, 1)
    interior(2, EDGE + 1, EDGE + OWN - 1, 0)
    interior(3, EDGE + 2, EDGE + OWN - 1, 1)
    interior(4, EDGE + 2, EDGE + OWN - 2, 0)
    pl.semaphore_wait(heard.at[2], len(beside[2:]))
    for number, (side_x, side_y) in enumerate(corners):
        rows = pl.ds(0, 8 if side_x == side_y else CORNER_ROWS)
        send(
            corner_out.at[number, rows],
            corner_in.at[number, rows],
            neighbour(2 * side_x - 1, 2 * side_y - 1),
        )
    pl.semaphore_wait(heard.at[0], len(near))
    for axis, step in far:
        signal(heard.at[1], along(axis, step))
    keep(interior_products(0, none), place < 6, False)
    keep(interior_products(8, none), place >= 2, True)
    acc_rows[pl.ds(8 * len(PAIRS), 8), :] = zero

    for copy in copies[2:4]:
        copy.wait_recv()
    for f in range(FIELDS):
        for side, first in ((0, EDGE + OWN), (1, 0)):
            for layer in range(2):
                low = face_in[side, f, pl.ds(layer * OWN, 8), :]
                high = face_in[side, f, pl.ds(layer * OWN + 8, 8), :]
                put_row(f, first + layer, low, high)
    edges(1, 1, EDGE + OWN, 1)
    edges(2, 1, EDGE + OWN - 1, 0)
    edges(3, EDGE, EDGE + OWN - 1, 1)
    edges(4, EDGE, EDGE + OWN - 2, 0)
    keep(edge_products(0, none), place < 6, True)
    keep(edge_products(8, none), place >= 2, True)

    for copy in copies[:2]:
        copy.wait_recv()
    for number, (f, layer) in enumerate(TO_PREVIOUS):
        u[f, pl.ds(EDGE * PADY + HIGH + layer, OWN, stride=PADY), :] = previous_in[number]
    for number, (f, layer) in enumerate(TO_NEXT):
        u[f, pl.ds(EDGE * PADY + LOW + layer, OWN, stride=PADY), :] = next_in[number]
    interior_strips(1, EDGE + 1, EDGE + OWN, 1)
    interior_strips(2, EDGE + 1, EDGE + OWN - 1, 0)
    interior_strips(3, EDGE + 2, EDGE + OWN - 1, 1)
    interior_strips(4, EDGE + 2, EDGE + OWN - 2, 0)
    sums = lax.fori_loop(
        0,
        3,
        lambda i, sums: strip_products([(4 + 4 * i, 5 + 4 * i), (6 + 4 * i, 7 + 4 * i)], sums),
        none,
    )

    for copy in copies[4:]:
        copy.wait_recv()
    for number, (side_x, side_y) in enumerate(corners):
        for f in range(FIELDS):
            for layer in range(2):
                x = (EDGE + OWN if side_x == 0 else 0) + layer
                y = HIGH if side_y == 0 else LOW
                if side_x != side_y:
                    source = corner_in[number, pl.ds(f * 4 + layer * 2, 2), :]
                    u[f, pl.ds(x * PADY + y, 2), :] = source
                elif layer == side_x:
                    u[f, pl.ds(x * PADY + y + layer, 1), :] = corner_in[number, pl.ds(f, 1), :]
    edge_strips(1, 1, EDGE + OWN, 1)
    edge_strips(2, 1, EDGE + OWN - 1, 0)
    edge_strips(3, EDGE, EDGE + OWN - 1, 1)
    edge_strips(4, EDGE, EDGE + OWN - 2, 0)
    keep(strip_products([(2, 3), (16, 17)], sums), place < 8, True)

    total = acc_rows[pl.ds(0, 16, stride=8), :]
    for s in range(1, 8):
        total = total + acc_rows[pl.ds(s, 16, stride=8), :]
    diagonal = lax.broadcasted_iota(jnp.int32, (16, 128), 0) == lax.broadcasted_iota(jnp.int32, (16, 128), 1)

    def to_row(column):
        return jnp.sum(jnp.where(diagonal, column, 0.0), axis=0, keepdims=True)

    def gather_metal():
        flags = [metal[tile_rows[1 + t // 2], tile_cols[1 + t % 2]] for t in range(4)]
        present = [flag.astype(jnp.float32) for flag in flags]
        before = jnp.float32(0.0)
        chosen = [[None] * 4 for _ in range(MS)]
        for t in range(4):
            taken = [present[t] * (1.0 - before), present[t] * before]
            before = before + present[t]
            for slot in range(MS):
                chosen[slot][t] = taken[slot]

        def rows(x, carry):
            for c in range(3):
                for j in range(STEPS):
                    parts = []
                    for t in range(4):
                        at = 8 * (t // 2) + x
                        y = 8 * (t % 2)
                        if j == 0:
                            parts.append(raw[c, pl.ds(pl.multiple_of(at * OWN + y, 8), 8), :])
                        else:
                            parts.append(own_out[j - 1, c, at, pl.ds(y, 8), :])
                    for slot in range(MS):
                        value = chosen[slot][0] * parts[0]
                        for t in range(1, 4):
                            value = value + chosen[slot][t] * parts[t]
                        tiles_out[slot, j, c, x] = value
            return carry

        lax.fori_loop(0, 8, rows, 0)
        for p in range(POLES):
            kicks = [strength[p]]
            kicks.append(-gamma[p] * kicks[0])
            for k in range(2, STEPS):
                kicks.append(-(omega[p] * omega[p]) * kicks[k - 2] - gamma[p] * kicks[k - 1])
            for k in range(STEPS):
                kicks_out[pl.ds(p * STEPS + k, 1), :] = jnp.full((1, 128), kicks[k])

    def order_own():
        def rows(x, carry):
            for j, state in enumerate(states[1:]):
                for c in range(6):
                    tile = [state[c, x + EDGE, pl.ds(8 * t, 8), :] for t in range(3)]
                    own_out[j, c, x, pl.ds(0, 8), :] = jnp.where(
                        place < 2, pltpu.roll(tile[2], 2, 0), pltpu.roll(tile[0], 2, 0)
                    )
                    own_out[j, c, x, pl.ds(8, 8), :] = jnp.where(
                        place < 6, pltpu.roll(tile[1], 6, 0), pltpu.roll(tile[2], 6, 0)
                    )
            return carry

        lax.fori_loop(0, OWN, rows, 0)

    row = to_row(jnp.sum(total, axis=1, keepdims=True))
    if far:
        pl.semaphore_wait(heard.at[1], len(far))
    me_a = my_core * z_size + my_z
    me_b = my_x * y_size + my_y
    targets_a = [
        device(my_x, ring_core[c], my_y, ring_z[z]) for c, z in farthest_first(cores, z_size)
    ]
    targets_b = [
        device(ring_x[x], my_core, ring_y[y], my_z) for x, y in farthest_first(x_size, y_size)
    ]
    for stage, (slots, me, targets) in enumerate(((sum_a, me_a, targets_a), (sum_b, me_b, targets_b))):
        slots[me] = row
        for target in targets:
            pltpu.make_async_remote_copy(
                src_ref=slots.at[me],
                dst_ref=slots.at[me],
                send_sem=stage_send.at[stage],
                recv_sem=stage_recv.at[stage],
                device_id=target,
                device_id_type=MESH,
            ).start()
        if stage == 0:
            order_own()
        else:
            gather_metal()
        settle(slots.at[pl.ds(0, len(targets))], stage_recv.at[stage])
        row = slots[0]
        for member in range(1, len(targets) + 1):
            row = row + slots[member]
    gram_out[...] = jnp.broadcast_to(
        jnp.sum(jnp.where(diagonal, row, 0.0), axis=1, keepdims=True), (16, 128)
    )

    for copy in copies:
        copy.wait_send()
    for stage, (slots, targets) in enumerate(((sum_a, targets_a), (sum_b, targets_b))):
        settle(slots.at[pl.ds(0, len(targets))], stage_send.at[stage])


def finish_kernel(
    cell_count,
    k0,
    own,
    gram,
    tiles,
    kicks,
    out_e,
    out_h,
    out_poles,
    out_coefficients,
    coefficients,
    table,
    fields,
    poles,
    pole_sem,
    store_sem,
):
    stores = []

    def store(src, dst):
        copy = pltpu.make_async_copy(src, dst, store_sem.at[len(stores)])
        copy.start()
        stores.append(copy)

    inner = {}
    for number, (i, j) in enumerate(PAIRS):
        inner[i, j] = inner[j, i] = gram[pl.ds(number, 1), :] * (1.0 / cell_count)
    unit = 1.0 / jnp.sqrt(inner[0, 0] + EPSILON)
    weights = [unit]
    lane = lax.broadcasted_iota(jnp.int32, (1, 128), 1)
    for step in range(1, STEPS + 1):
        image = [None] + weights

        def total(terms):
            return functools.reduce(jnp.add, terms)

        along_q = unit * total([image[j] * inner[0, j] for j in range(1, step + 1)])
        rest = [-along_q * unit] + image[1:]
        along_v = jnp.zeros_like(unit)
        if step > 1:
            along_v = total(
                [
                    image[j] * total([weights[i] * inner[i, j] for i in range(step)])
                    for j in range(1, step + 1)
                ]
            )
            for i in range(step):
                rest[i] = rest[i] - along_v * weights[i]
        squared = total(
            [rest[i] * total([rest[j] * inner[i, j] for j in range(step + 1)]) for i in range(step + 1)]
        )
        norm = jnp.sqrt(jnp.maximum(squared, 0.0) + EPSILON)
        scale = 1.0 / norm
        weights = [part * scale for part in rest]
        line = jnp.where(lane == 0, along_q, jnp.where(lane == 1, along_v, norm))
        coefficients[pl.ds(step - 1, 1), :] = line[:, :3]

    store(coefficients, out_coefficients)

    for p in range(POLES):
        kick = [kicks[pl.ds(p * STEPS + k, 1), :] for k in range(STEPS)]
        for j in range(STEPS):
            parts = [weights[k] * kick[k - 1 - j] for k in range(j + 1, STEPS + 1)]
            table[pl.ds(p * 8 + j, 1), :] = functools.reduce(jnp.add, parts)
        for j in range(STEPS - 1):
            parts = [weights[k] * kick[k - 2 - j] for k in range(j + 2, STEPS + 1)]
            table[pl.ds(p * 8 + 4 + j, 1), :] = functools.reduce(jnp.add, parts)
    for j in range(STEPS + 1):
        table[pl.ds(48 + j, 1), :] = weights[j]

    def entry(number):
        return jnp.broadcast_to(table[pl.ds(number, 1), :], (8, 128))

    def pole_part(i):
        return (i // 6, pl.ds(0, 2), pl.ds(0, POLES), i // 2 % 3, pl.ds(i % 2 * 4, 4))

    def pole_cells(i, carry):
        slot, c = i // 6, i // 2 % 3
        for x in [i % 2 * 4 + k for k in range(4)]:
            field = [tiles[slot, j, c, x] for j in range(STEPS)]
            for p in range(POLES):
                poles[slot, 1, p, c, x] = functools.reduce(
                    jnp.add, [entry(p * 8 + j) * field[j] for j in range(STEPS)]
                )
                poles[slot, 0, p, c, x] = functools.reduce(
                    jnp.add, [entry(p * 8 + 4 + j) * field[j] for j in range(STEPS - 1)]
                )
        pltpu.make_async_copy(
            poles.at[pole_part(i)], out_poles.at[pole_part(i)], pole_sem.at[i]
        ).start()
        return carry

    lax.fori_loop(0, 6 * MS, pole_cells, 0)

    for half, out in enumerate((out_e, out_h)):

        def field_cells(i, carry):
            for x in [4 * i + k for k in range(4)]:
                for c in range(3 * half, 3 * half + 3):
                    cells = pl.ds(pl.multiple_of(x * OWN, 8), OWN)
                    value = table[pl.ds(48, 1), :] * k0[c, cells, :]
                    for j in range(STEPS):
                        value = value + table[pl.ds(49 + j, 1), :] * own[j, c, x]
                    fields[c, x] = value
            return carry

        lax.fori_loop(0, OWN // 4, field_cells, 0)
        store(fields.at[pl.ds(3 * half, 3)], out)
    for i in range(6 * MS):
        pltpu.make_async_copy(poles.at[pole_part(i)], out_poles.at[pole_part(i)], pole_sem.at[i]).wait()
    for copy in stores:
        copy.wait()


def body(sizes, u_electric, u_magnetic, eps_inv, metal_map, pole_omega, pole_gamma, pole_strength):
    depth = u_electric.shape[3]
    cell_count = 6.0 * OWN * OWN * depth * sizes[0] * sizes[1] * sizes[2] * sizes[3]
    f32 = jnp.float32
    any_spec = pl.BlockSpec(memory_space=pl.ANY)
    hbm = pl.BlockSpec(memory_space=pltpu.HBM)
    vmem = pl.BlockSpec(memory_space=pltpu.VMEM)
    a_size = sizes[1] * sizes[3]
    b_size = sizes[0] * sizes[2]

    def stay(value):
        return pltpu.with_memory_space_constraint(value, pltpu.HBM)

    start = [u_electric.reshape(3, OWN * OWN, depth), u_magnetic.reshape(3, OWN * OWN, depth)]
    model = [stay(part) for part in (metal_map, pole_omega, pole_gamma, pole_strength)]
    dma = pltpu.SemaphoreType.DMA
    results = pl.pallas_call(
        functools.partial(exchange_kernel, sizes, metal_map.shape),
        out_shape=[
            jax.ShapeDtypeStruct((STEPS, 6, OWN, OWN, depth), f32),
            jax.ShapeDtypeStruct((16, depth), f32),
            jax.ShapeDtypeStruct((MS, STEPS, 3, 8, 8, depth), f32),
            jax.ShapeDtypeStruct((POLES * STEPS, depth), f32),
            jax.ShapeDtypeStruct((FIELDS, OWN * OWN, depth), f32),
        ],
        in_specs=[hbm] * 7,
        out_specs=[vmem] * 5,
        scratch_shapes=[
            pltpu.VMEM((2, FIELDS, EDGE * OWN, depth), f32),
            *[pltpu.VMEM((6, PADX, PADY, depth), f32)] * STEPS,
            pltpu.VMEM((FIELDS, ROW, depth), f32),
            pltpu.VMEM((len(TO_PREVIOUS), OWN, depth), f32),
            pltpu.VMEM((len(TO_PREVIOUS), OWN, depth), f32),
            pltpu.VMEM((len(TO_NEXT), OWN, depth), f32),
            pltpu.VMEM((len(TO_NEXT), OWN, depth), f32),
            pltpu.VMEM((4, CORNER_ROWS, depth), f32),
            pltpu.VMEM((4, CORNER_ROWS, depth), f32),
            pltpu.VMEM((4, PADY, depth), f32),
            pltpu.VMEM((128, depth), f32),
            pltpu.VMEM((a_size, 1, depth), f32),
            pltpu.VMEM((b_size, 1, depth), f32),
            pltpu.SMEM(metal_map.shape, jnp.int32),
            pltpu.SMEM((POLES,), f32),
            pltpu.SMEM((POLES,), f32),
            pltpu.SMEM((POLES,), f32),
            pltpu.SemaphoreType.REGULAR((3,)),
            dma((7,)),
            dma((8,)),
            dma((8,)),
            dma((2,)),
            dma((2,)),
        ],
        compiler_params=pltpu.CompilerParams(
            collective_id=0, has_side_effects=True, vmem_limit_bytes=VMEM_LIMIT
        ),
    )(*[stay(part) for part in start], stay(eps_inv.reshape(OWN * OWN, depth)), *model)

    own, gram, tiles, kicks, raw = results

    return pl.pallas_call(
        functools.partial(finish_kernel, cell_count),
        out_shape=[
            jax.ShapeDtypeStruct(u_electric.shape, f32),
            jax.ShapeDtypeStruct(u_magnetic.shape, f32),
            jax.ShapeDtypeStruct((MS, 2, POLES, 3, 8, 8, depth), f32),
            jax.ShapeDtypeStruct((STEPS, 3), f32),
        ],
        in_specs=[vmem] * 5,
        out_specs=[any_spec] * 4,
        scratch_shapes=[
            pltpu.VMEM((STEPS, 3), f32),
            pltpu.VMEM((56, depth), f32),
            pltpu.VMEM((6, OWN, OWN, depth), f32),
            pltpu.VMEM((MS, 2, POLES, 3, 8, 8, depth), f32),
            dma((6 * MS,)),
            dma((3,)),
        ],
        compiler_params=pltpu.CompilerParams(vmem_limit_bytes=VMEM_LIMIT),
    )(raw, own, gram, tiles, kicks)


def solution(mesh):
    sizes = layout(mesh.shape["gx"], mesh.shape["gy"])
    placed = (
        P(None, "gx", "gy", None),
        P(None, "gx", "gy", None),
        P("gx", "gy", None),
        P(),
        P(),
        P(),
        P(),
    )
    return jax.shard_map(
        functools.partial(body, sizes),
        mesh=mesh,
        in_specs=placed,
        out_specs=(
            P(None, "gx", "gy", None),
            P(None, "gx", "gy", None),
            P(("gx", "gy"), None, None, None, None, None, None),
            P(),
        ),
        check_vma=False,
    )
```
